32 devices in a mesh: groups: 2 (over y), blk: 16 (over z, x, core).
Axes of the slice: x: 2, y: 2, z: 4, core: 2. Of those that a mesh axis runs over, the one named last changes fastest.
Arguments:
- embeddings: bfloat16 [1536, 768], P(('groups', 'blk')), parts along dimension 0, may hold values from -6 to 6
- cluster_id: int32 [1536], P(('groups', 'blk')), parts along dimension 0, may hold values from 0 to 3, as said below
Outputs:
- neighbour: bfloat16 [1536, 768], P(('groups', 'blk')), parts along dimension 0
- dup_score: bfloat16 [1536], P(('groups', 'blk')), parts along dimension 0
The draws below stay inside these ranges and needn't reach their ends.
There are 2 independent parts, one for each index of `groups`. The reference program is written for one: setup_inputs(seed, part) draws one part's arguments, and reference() takes and returns one part's arrays. A program takes and returns all parts, laid end to end along the dimension named above; each array names one. Nothing has to cross between parts.
Inputs may be any that keep to these rules, and one draw needn't show every extreme that they name: `cluster_id`: on every device of a part, each of the 4 clusters has the same number of rows among that device's 48 rows; each such number is a positive multiple of 3, and the largest is exactly 24.
All inputs are finite; a program needn't handle non-finite values.
Results may differ from the reference program's by a relative error of at most 0.0059.
Values may be sent and summed in bfloat16 or wider, within the bound.
No kernel may reach another device: no remote copies, remote signals or barrier semaphores. Data moves between devices by JAX's collectives and lax.ppermute only.
A program may use at most 64 MiB of HBM per device.

```python
import jax
import jax.numpy as jnp
from jax import lax

D = 768
PEER_ROWS = 3
U_MAX = 8
ROWS_DEV = 48
ROWS = 768
N_BLK = 16


def draw_cluster_id(key, part):
    key = jax.random.fold_in(key, 7)
    first_key, second_key, third_key = jax.random.split(key, 3)
    clusters = N_BLK // 4
    others = clusters - 1
    remaining = N_BLK - U_MAX
    base_size = remaining // others
    leftover = remaining - base_size * others
    halves = others // 2
    shifts = jax.random.randint(first_key, (halves,), -(base_size - 1), base_size).astype(jnp.int32)
    deltas = jnp.concatenate([shifts, -shifts, jnp.zeros((others - 2 * halves,), jnp.int32)])
    extra = (jnp.arange(others, dtype=jnp.int32) < leftover).astype(jnp.int32)
    sizes = jnp.concatenate([jnp.full((1,), U_MAX, jnp.int32), base_size + deltas + extra])
    sizes = jax.random.permutation(second_key, sizes)
    bounds = jnp.cumsum(sizes * PEER_ROWS)
    position = jnp.arange(ROWS_DEV, dtype=jnp.int32)
    labels = jnp.sum((position[:, None] >= bounds[None, :]).astype(jnp.int32), axis=1)
    device_keys = jax.random.split(third_key, N_BLK)
    shuffles = jax.vmap(lambda single: jax.random.permutation(single, ROWS_DEV))(device_keys)
    return labels[shuffles].reshape(ROWS_DEV * N_BLK).astype(jnp.int32)


def levels(own_key, shape, shards, low, largest):
    def one(dim, shards_of):
        draws = jax.random.uniform(jax.random.fold_in(jax.random.fold_in(own_key, 6), dim), (shards_of,), jnp.float32, low / len(shards), largest / len(shards))
        return jnp.repeat(jnp.exp(draws), shape[dim] // shards_of).reshape((-1,) + (1,) * (len(shape) - dim - 1))

    factor_of = one(*shards[0])
    for cut in shards[1:]:
        factor_of = factor_of * one(*cut)
    return factor_of


def gaussian(rng, extent, deviation, most, cuts=(), kind=jnp.bfloat16):
    entries = jax.random.normal(rng, extent, jnp.float32) * deviation
    if len(cuts) > 0:
        entries = levels(rng, extent, cuts, -0.22, 0.18) * entries
    return jnp.clip(entries, min=-most, max=most).astype(kind)


def setup_inputs(seed: int = 0, part: int = 0) -> dict:
    splits = jax.random.split(jax.random.key(seed), 3)
    own_keys = jax.random.split(jax.random.fold_in(splits[2], part), 3)
    return {
        "embeddings": gaussian(own_keys[0], (ROWS, D), 1.0, 6.0, ((0, 16),)),
        "cluster_id": draw_cluster_id(jax.random.fold_in(jax.random.fold_in(splits[2], part), 71), part),
    }


sharpness = 10.0
epsilon = 1e-06

def reference(embeddings, cluster_id):
    total_rows = ROWS_DEV * N_BLK
    widened = embeddings.astype(jnp.float32)
    unit_rows = (widened * lax.rsqrt(lax.optimization_barrier(jnp.mean(widened * widened, axis=-1, keepdims=True)) + epsilon) * D ** (-0.5)).astype(jnp.bfloat16)
    position = jnp.arange(total_rows, dtype=jnp.int32)
    arrange_order = jnp.argsort(cluster_id.astype(jnp.int32) * total_rows + position).astype(jnp.int32)
    sorted_rows = unit_rows[arrange_order]
    sorted_labels = cluster_id.astype(jnp.int32)[arrange_order]
    margin = (U_MAX - 1) * ROWS_DEV
    padded_rows = jnp.concatenate([jnp.zeros((margin, D), sorted_rows.dtype), sorted_rows, jnp.zeros((margin, D), sorted_rows.dtype)], axis=0)
    padded_labels = jnp.concatenate([jnp.full((margin,), -1, jnp.int32), sorted_labels, jnp.full((margin,), -1, jnp.int32)])
    window = (2 * U_MAX - 1) * ROWS_DEV

    def per_block(block_index):
        first_row = (block_index * ROWS_DEV).astype(jnp.int32)
        queries = lax.dynamic_slice_in_dim(sorted_rows, first_row, ROWS_DEV, 0)
        query_labels = lax.dynamic_slice_in_dim(sorted_labels, first_row, ROWS_DEV, 0)
        key_rows = lax.dynamic_slice_in_dim(padded_rows, first_row, window, 0)
        key_labels = lax.dynamic_slice_in_dim(padded_labels, first_row, window, 0)
        similar = jnp.dot(queries, key_rows.T, preferred_element_type=jnp.float32)
        query_pos = first_row + jnp.arange(ROWS_DEV, dtype=jnp.int32)
        key_pos = first_row - margin + jnp.arange(window, dtype=jnp.int32)
        allowed = (query_labels[:, None] == key_labels[None, :]) & (query_pos[:, None] != key_pos[None, :])
        weights = jnp.where(allowed, jnp.exp(sharpness * (similar - 1.0)), jnp.zeros_like(similar))
        totals = lax.optimization_barrier(jnp.sum(weights, axis=1))
        weighted = jnp.dot(weights.astype(jnp.bfloat16), key_rows, preferred_element_type=jnp.float32)
        normed = (weighted * lax.rsqrt(lax.optimization_barrier(jnp.mean(weighted * weighted, axis=-1, keepdims=True)) + epsilon)).astype(jnp.bfloat16)
        return (normed, jnp.log(totals).astype(jnp.bfloat16))
    neighbour_blocks, score_blocks = lax.map(per_block, jnp.arange(N_BLK, dtype=jnp.int32))
    inverse = jnp.argsort(arrange_order).astype(jnp.int32)
    neighbour = neighbour_blocks.reshape(total_rows, D)[inverse]
    dup_score = score_blocks.reshape(total_rows)[inverse]
    return (neighbour, dup_score)
```

```python
import functools

import jax
import jax.numpy as jnp
from jax import lax
from jax.experimental import pallas as pl
from jax.experimental.pallas import tpu as pltpu
from jax.sharding import PartitionSpec as P

U_MAX = 8
GATHER_LIMIT = 4 * 1024 * 1024


sharpness = 10.0
epsilon = 1e-06


def normalize_rows(values):
    widened = values.astype(jnp.float32)
    return (
        widened
        * lax.rsqrt(jnp.mean(widened * widened, axis=-1, keepdims=True) + epsilon)
        * widened.shape[-1] ** (-0.5)
    ).astype(jnp.bfloat16)


def as_column(row):
    count = row.shape[1]
    across = lax.broadcasted_iota(jnp.int32, (count, count), 1)
    down = lax.broadcasted_iota(jnp.int32, (count, count), 0)
    return jnp.sum(jnp.where(across == down, row, jnp.zeros_like(row)), axis=1, keepdims=True)


def as_row(column):
    count = column.shape[0]
    across = lax.broadcasted_iota(jnp.int32, (count, count), 1)
    down = lax.broadcasted_iota(jnp.int32, (count, count), 0)
    return jnp.sum(jnp.where(across == down, column, jnp.zeros_like(column)), axis=0, keepdims=True)


def arrange_kernel(ids_ref, rows_ref, out_ref):
    count = rows_ref.shape[0]
    ids_row = ids_ref[...].reshape(1, count)
    ids_column = as_column(ids_row)
    across = lax.broadcasted_iota(jnp.int32, (count, count), 1)
    down = lax.broadcasted_iota(jnp.int32, (count, count), 0)
    before = (ids_column < ids_row) | ((ids_column == ids_row) & (down < across))
    rank_row = jnp.sum(before.astype(jnp.int32), axis=0, keepdims=True)
    moves = (down == rank_row).astype(jnp.bfloat16)
    unit = normalize_rows(rows_ref[...])
    out_ref[...] = jnp.dot(moves, unit, preferred_element_type=jnp.float32).astype(jnp.bfloat16)


def score_kernel(me_ref, ids_ref, rows_ref, keys_ref, neighbour_ref, score_ref):
    count = rows_ref.shape[0]
    total = keys_ref.shape[0]
    me = me_ref[0]
    ids_row = ids_ref[...].reshape(1, count)
    ids_column = as_column(ids_row)
    across = lax.broadcasted_iota(jnp.int32, (count, count), 1)
    down = lax.broadcasted_iota(jnp.int32, (count, count), 0)
    lower = (ids_row < ids_column).astype(jnp.int32)
    same = (ids_row == ids_column).astype(jnp.int32)
    earlier = jnp.where(across < down, same, 0)
    first = jnp.sum(lower, axis=1, keepdims=True)
    after = first + jnp.sum(same, axis=1, keepdims=True)
    own = me * count + first + jnp.sum(earlier, axis=1, keepdims=True)

    keys = keys_ref[...]
    unit = normalize_rows(rows_ref[...])
    similar = lax.dot_general(
        unit, keys, (((1,), (1,)), ((), ())), preferred_element_type=jnp.float32
    )
    key = lax.broadcasted_iota(jnp.int32, (count, total), 1)
    place = lax.rem(key, count)
    allowed = (place >= first) & (place < after) & (key != own)
    weights = jnp.where(allowed, jnp.exp(sharpness * (similar - 1.0)), 0.0)
    totals = jnp.sum(weights, axis=1, keepdims=True)
    weighted = jnp.dot(weights.astype(jnp.bfloat16), keys, preferred_element_type=jnp.float32)
    neighbour_ref[...] = (
        weighted * lax.rsqrt(jnp.mean(weighted * weighted, axis=-1, keepdims=True) + epsilon)
    ).astype(jnp.bfloat16)
    score_ref[...] = jnp.log(as_row(totals)).astype(jnp.bfloat16).reshape(count)


def gathered_body(embeddings, cluster_id):
    rows_dev, features = embeddings.shape
    vmem = pl.BlockSpec(memory_space=pltpu.VMEM)
    arranged = pl.pallas_call(
        arrange_kernel,
        out_shape=jax.ShapeDtypeStruct((rows_dev, features), jnp.bfloat16),
        in_specs=[vmem, vmem],
        out_specs=vmem,
        name="arrange",
    )(cluster_id, embeddings)
    keys = lax.all_gather(arranged, "blk", axis=0, tiled=True)
    me = lax.axis_index("blk").astype(jnp.int32).reshape(1)
    return tuple(
        pl.pallas_call(
            score_kernel,
            out_shape=(
                jax.ShapeDtypeStruct((rows_dev, features), jnp.bfloat16),
                jax.ShapeDtypeStruct((rows_dev,), jnp.bfloat16),
            ),
            in_specs=[pl.BlockSpec(memory_space=pltpu.SMEM), vmem, vmem, vmem],
            out_specs=(vmem, vmem),
            compiler_params=pltpu.CompilerParams(vmem_limit_bytes=32 * 1024 * 1024),
            name="score",
        )(me, cluster_id, embeddings, keys)
    )


def from_behind(value, axis, steps):
    count = lax.axis_size(axis)
    initial, last = (max(0, -steps), min(count, count - steps))
    return lax.ppermute(value, axis, [(source, source + steps) for source in range(initial, last)])


def pair_terms(queries, visiting, allowed):
    similar = jnp.dot(queries, visiting.T, preferred_element_type=jnp.float32)
    return jnp.where(allowed, jnp.exp(sharpness * (similar - 1.0)), jnp.zeros_like(similar))


def finish(weighted, totals):
    normed = (
        weighted * lax.rsqrt(jnp.mean(weighted * weighted, axis=-1, keepdims=True) + epsilon)
    ).astype(jnp.bfloat16)
    return (normed, jnp.log(totals).astype(jnp.bfloat16))


def collected_body(embeddings, cluster_id):
    rows_dev, features = embeddings.shape
    devices = lax.axis_size("blk")
    per_peer = rows_dev // devices
    clusters = devices // 4
    unit_rows = normalize_rows(embeddings)
    labels = jnp.arange(clusters, dtype=jnp.int32)
    counts = jnp.sum((cluster_id[:, None] == labels[None, :]).astype(jnp.int32), axis=0)
    group_ends = jnp.cumsum(counts // per_peer)

    def owner_cluster(device):
        in_range = (device >= 0) & (device < devices)
        return jnp.where(in_range, jnp.sum((device >= group_ends).astype(jnp.int32)), -1)

    position = jnp.arange(rows_dev, dtype=jnp.int32)
    arrange_order = jnp.argsort(cluster_id * rows_dev + position)
    inverse = jnp.argsort(arrange_order)
    arranged = unit_rows[arrange_order].reshape(devices, per_peer, features)
    held_rows = lax.all_to_all(arranged, "blk", split_axis=0, concat_axis=0, tiled=True).reshape(
        rows_dev, features
    )
    self_index = lax.axis_index("blk")
    mine = owner_cluster(self_index)
    weights = pair_terms(held_rows, held_rows, position[:, None] != position[None, :])
    totals = jnp.sum(weights, axis=1)
    weighted = jnp.dot(weights.astype(jnp.bfloat16), held_rows, preferred_element_type=jnp.float32)
    from_lower = held_rows
    from_upper = held_rows
    for distance in range(1, U_MAX):
        from_lower = from_behind(from_lower, "blk", 1)
        from_upper = from_behind(from_upper, "blk", -1)
        for visiting, source in (
            (from_lower, self_index - distance),
            (from_upper, self_index + distance),
        ):
            weights = pair_terms(held_rows, visiting, owner_cluster(source) == mine)
            totals = totals + jnp.sum(weights, axis=1)
            weighted = weighted + jnp.dot(
                weights.astype(jnp.bfloat16), visiting, preferred_element_type=jnp.float32
            )
    normed, scores = finish(weighted, totals)
    returned_rows, returned_scores = (
        lax.all_to_all(
            normed.reshape(devices, per_peer, features),
            "blk",
            split_axis=0,
            concat_axis=0,
            tiled=True,
        ),
        lax.all_to_all(
            scores.reshape(devices, per_peer), "blk", split_axis=0, concat_axis=0, tiled=True
        ),
    )
    neighbour = returned_rows.reshape(rows_dev, features)[inverse]
    dup_score = returned_scores.reshape(rows_dev)[inverse]
    return (neighbour, dup_score)


def solution(mesh):
    placed = (P(("groups", "blk"), None), P(("groups", "blk")))
    devices = mesh.shape["blk"]

    def body(embeddings, cluster_id):
        gathered = embeddings.size * embeddings.dtype.itemsize * devices
        plan = gathered_body if gathered <= GATHER_LIMIT else collected_body
        return plan(embeddings, cluster_id)

    return jax.shard_map(
        body,
        mesh=mesh,
        in_specs=placed,
        out_specs=(P(("groups", "blk"), None), P(("groups", "blk"))),
        check_vma=False,
    )
```

```python
import jax
import jax.numpy as jnp
from jax import lax
from jax.experimental import pallas as pl
from jax.experimental.pallas import tpu as pltpu
from jax.sharding import PartitionSpec as P

U_MAX = 8
GATHER_LIMIT = 4 * 1024 * 1024


sharpness = 10.0
epsilon = 1e-06


def normalize_rows(values):
    widened = values.astype(jnp.float32)
    return (
        widened
        * lax.rsqrt(jnp.mean(widened * widened, axis=-1, keepdims=True) + epsilon)
        * widened.shape[-1] ** (-0.5)
    ).astype(jnp.bfloat16)


def as_column(row):
    count = row.shape[1]
    across = lax.broadcasted_iota(jnp.int32, (count, count), 1)
    down = lax.broadcasted_iota(jnp.int32, (count, count), 0)
    return jnp.sum(jnp.where(across == down, row, jnp.zeros_like(row)), axis=1, keepdims=True)


def as_row(column):
    count = column.shape[0]
    across = lax.broadcasted_iota(jnp.int32, (count, count), 1)
    down = lax.broadcasted_iota(jnp.int32, (count, count), 0)
    return jnp.sum(jnp.where(across == down, column, jnp.zeros_like(column)), axis=0, keepdims=True)


def arrange_kernel(ids_ref, rows_ref, out_ref, moves_ref, bounds_ref):
    count = rows_ref.shape[0]
    ids_row = ids_ref[...].reshape(1, count)
    ids_column = as_column(ids_row)
    across = lax.broadcasted_iota(jnp.int32, (count, count), 1)
    down = lax.broadcasted_iota(jnp.int32, (count, count), 0)
    before = (ids_column < ids_row) | ((ids_column == ids_row) & (down < across))
    rank_row = jnp.sum(before.astype(jnp.int32), axis=0, keepdims=True)
    moved = down == rank_row
    moves = moved.astype(jnp.bfloat16)
    unit = normalize_rows(rows_ref[...])
    arranged = jnp.dot(moves, unit, preferred_element_type=jnp.float32).astype(jnp.bfloat16)
    for copy in range(out_ref.shape[0]):
        out_ref[copy] = arranged
    moves_ref[...] = moves
    label = jnp.sum(jnp.where(moved, ids_row, 0), axis=1, keepdims=True)
    first = jnp.sum((ids_row < label).astype(jnp.int32), axis=1, keepdims=True)
    after = jnp.sum((ids_row <= label).astype(jnp.int32), axis=1, keepdims=True)
    lane = lax.broadcasted_iota(jnp.int32, bounds_ref.shape, 1)
    bounds_ref[...] = jnp.where(lane == 0, first, after)


def partial_kernel(bounds_ref, queries_ref, keys_ref, out_ref):
    planes, count, features = keys_ref.shape
    across = queries_ref.shape[0]
    me = lax.axis_index("blk")
    plane, column = me // across, lax.rem(me, across)
    queries = queries_ref[...].reshape(across * count, features)
    keys = keys_ref[...].reshape(planes * count, features)
    similar = lax.dot_general(
        queries, keys, (((1,), (1,)), ((), ())), preferred_element_type=jnp.float32
    )
    bounds = jnp.concatenate([bounds_ref[...]] * across, axis=0)
    first, after = bounds[:, 0:1], bounds[:, 1:2]
    key = lax.broadcasted_iota(jnp.int32, similar.shape, 1)
    query = lax.broadcasted_iota(jnp.int32, similar.shape, 0)
    place = lax.rem(key, count)
    own = key - plane * count == query - column * count
    own_block = (query >= column * count) & (query < (column + 1) * count)
    allowed = (place >= first) & (place < after) & ~(own & own_block)
    weights = jnp.where(allowed, jnp.exp(sharpness * (similar - 1.0)), 0.0)
    totals = jnp.sum(weights, axis=1, keepdims=True)
    weighted = jnp.dot(weights.astype(jnp.bfloat16), keys, preferred_element_type=jnp.float32)
    out_ref[:, :, :features] = weighted.astype(jnp.bfloat16).reshape(across, count, features)
    high = totals.astype(jnp.bfloat16)
    low = (totals - high.astype(jnp.float32)).astype(jnp.bfloat16)
    lane = lax.broadcasted_iota(jnp.int32, (across * count, out_ref.shape[2] - features), 1)
    pair = jnp.where(lane == 0, high.astype(jnp.float32), low.astype(jnp.float32))
    out_ref[:, :, features:] = pair.astype(jnp.bfloat16).reshape(across, count, -1)


def finish_kernel(moves_ref, partial_ref, neighbour_ref, score_ref):
    count, features = neighbour_ref.shape
    summed = partial_ref[0].astype(jnp.float32)
    for block in range(1, partial_ref.shape[0]):
        summed = summed + partial_ref[block].astype(jnp.float32)
    weighted = summed[:, :features]
    totals = summed[:, features : features + 1] + summed[:, features + 1 : features + 2]
    normed = (
        weighted * lax.rsqrt(jnp.mean(weighted * weighted, axis=-1, keepdims=True) + epsilon)
    ).astype(jnp.bfloat16)
    moves = moves_ref[...]
    neighbour_ref[...] = lax.dot_general(
        moves, normed, (((0,), (0,)), ((), ())), preferred_element_type=jnp.float32
    ).astype(jnp.bfloat16)
    scores = jnp.sum(
        moves.astype(jnp.float32) * jnp.log(totals), axis=0, keepdims=True
    )
    score_ref[...] = scores.astype(jnp.bfloat16).reshape(count)


ACROSS = 4
EXTRA = 128


def gathered_body(embeddings, cluster_id):
    rows_dev, features = embeddings.shape
    devices = lax.axis_size("blk")
    planes = devices // ACROSS
    along = [[plane * ACROSS + column for plane in range(planes)] for column in range(ACROSS)]
    within = [[plane * ACROSS + column for column in range(ACROSS)] for plane in range(planes)]
    vmem = pl.BlockSpec(memory_space=pltpu.VMEM)
    params = pltpu.CompilerParams(vmem_limit_bytes=32 * 1024 * 1024)

    def exchange(blocks, groups):
        return lax.all_to_all(
            blocks, "blk", split_axis=0, concat_axis=0, axis_index_groups=groups, tiled=True
        )

    arranged, moves, bounds = pl.pallas_call(
        arrange_kernel,
        out_shape=(
            jax.ShapeDtypeStruct((max(planes, ACROSS), rows_dev, features), jnp.bfloat16),
            jax.ShapeDtypeStruct((rows_dev, rows_dev), jnp.bfloat16),
            jax.ShapeDtypeStruct((rows_dev, 128), jnp.int32),
        ),
        in_specs=[vmem, vmem],
        out_specs=(vmem, vmem, vmem),
        compiler_params=params,
        name="arrange",
    )(cluster_id, embeddings)
    keys = exchange(arranged[:planes], along)
    queries = exchange(arranged[:ACROSS], within)
    partial = pl.pallas_call(
        partial_kernel,
        out_shape=jax.ShapeDtypeStruct((ACROSS, rows_dev, features + EXTRA), jnp.bfloat16),
        in_specs=[vmem, vmem, vmem],
        out_specs=vmem,
        compiler_params=params,
        name="partial",
    )(bounds, queries, keys)
    partial = exchange(partial, within)
    return tuple(
        pl.pallas_call(
            finish_kernel,
            out_shape=(
                jax.ShapeDtypeStruct((rows_dev, features), jnp.bfloat16),
                jax.ShapeDtypeStruct((rows_dev,), jnp.bfloat16),
            ),
            in_specs=[vmem, vmem],
            out_specs=(vmem, vmem),
            compiler_params=params,
            name="finish",
        )(moves, partial)
    )


def from_behind(value, axis, steps):
    count = lax.axis_size(axis)
    initial, last = (max(0, -steps), min(count, count - steps))
    return lax.ppermute(value, axis, [(source, source + steps) for source in range(initial, last)])


def pair_terms(queries, visiting, allowed):
    similar = jnp.dot(queries, visiting.T, preferred_element_type=jnp.float32)
    return jnp.where(allowed, jnp.exp(sharpness * (similar - 1.0)), jnp.zeros_like(similar))


def finish(weighted, totals):
    normed = (
        weighted * lax.rsqrt(jnp.mean(weighted * weighted, axis=-1, keepdims=True) + epsilon)
    ).astype(jnp.bfloat16)
    return (normed, jnp.log(totals).astype(jnp.bfloat16))


def collected_body(embeddings, cluster_id):
    rows_dev, features = embeddings.shape
    devices = lax.axis_size("blk")
    per_peer = rows_dev // devices
    clusters = devices // 4
    unit_rows = normalize_rows(embeddings)
    labels = jnp.arange(clusters, dtype=jnp.int32)
    counts = jnp.sum((cluster_id[:, None] == labels[None, :]).astype(jnp.int32), axis=0)
    group_ends = jnp.cumsum(counts // per_peer)

    def owner_cluster(device):
        in_range = (device >= 0) & (device < devices)
        return jnp.where(in_range, jnp.sum((device >= group_ends).astype(jnp.int32)), -1)

    position = jnp.arange(rows_dev, dtype=jnp.int32)
    arrange_order = jnp.argsort(cluster_id * rows_dev + position)
    inverse = jnp.argsort(arrange_order)
    arranged = unit_rows[arrange_order].reshape(devices, per_peer, features)
    held_rows = lax.all_to_all(arranged, "blk", split_axis=0, concat_axis=0, tiled=True).reshape(
        rows_dev, features
    )
    self_index = lax.axis_index("blk")
    mine = owner_cluster(self_index)
    weights = pair_terms(held_rows, held_rows, position[:, None] != position[None, :])
    totals = jnp.sum(weights, axis=1)
    weighted = jnp.dot(weights.astype(jnp.bfloat16), held_rows, preferred_element_type=jnp.float32)
    from_lower = held_rows
    from_upper = held_rows
    for distance in range(1, U_MAX):
        from_lower = from_behind(from_lower, "blk", 1)
        from_upper = from_behind(from_upper, "blk", -1)
        for visiting, source in (
            (from_lower, self_index - distance),
            (from_upper, self_index + distance),
        ):
            weights = pair_terms(held_rows, visiting, owner_cluster(source) == mine)
            totals = totals + jnp.sum(weights, axis=1)
            weighted = weighted + jnp.dot(
                weights.astype(jnp.bfloat16), visiting, preferred_element_type=jnp.float32
            )
    normed, scores = finish(weighted, totals)
    returned_rows, returned_scores = (
        lax.all_to_all(
            normed.reshape(devices, per_peer, features),
            "blk",
            split_axis=0,
            concat_axis=0,
            tiled=True,
        ),
        lax.all_to_all(
            scores.reshape(devices, per_peer), "blk", split_axis=0, concat_axis=0, tiled=True
        ),
    )
    neighbour = returned_rows.reshape(rows_dev, features)[inverse]
    dup_score = returned_scores.reshape(rows_dev)[inverse]
    return (neighbour, dup_score)


def solution(mesh):
    placed = (P(("groups", "blk"), None), P(("groups", "blk")))
    devices = mesh.shape["blk"]

    def body(embeddings, cluster_id):
        gathered = embeddings.size * embeddings.dtype.itemsize * devices
        fits = gathered <= GATHER_LIMIT and devices % ACROSS == 0
        plan = gathered_body if fits else collected_body
        return plan(embeddings, cluster_id)

    return jax.shard_map(
        body,
        mesh=mesh,
        in_specs=placed,
        out_specs=(P(("groups", "blk"), None), P(("groups", "blk"))),
        check_vma=False,
    )
```

```python
import jax
import jax.numpy as jnp
from jax import lax
from jax.experimental import pallas as pl
from jax.experimental.pallas import tpu as pltpu
from jax.sharding import PartitionSpec as P

U_MAX = 8
GATHER_LIMIT = 4 * 1024 * 1024


sharpness = 10.0
epsilon = 1e-06


def normalize_rows(values):
    widened = values.astype(jnp.float32)
    return (
        widened
        * lax.rsqrt(jnp.mean(widened * widened, axis=-1, keepdims=True) + epsilon)
        * widened.shape[-1] ** (-0.5)
    ).astype(jnp.bfloat16)


def as_column(row):
    count = row.shape[1]
    across = lax.broadcasted_iota(jnp.int32, (count, count), 1)
    down = lax.broadcasted_iota(jnp.int32, (count, count), 0)
    return jnp.sum(jnp.where(across == down, row, jnp.zeros_like(row)), axis=1, keepdims=True)


def as_row(column):
    count = column.shape[0]
    across = lax.broadcasted_iota(jnp.int32, (count, count), 1)
    down = lax.broadcasted_iota(jnp.int32, (count, count), 0)
    return jnp.sum(jnp.where(across == down, column, jnp.zeros_like(column)), axis=0, keepdims=True)


def arrange_kernel(ids_hbm, rows_hbm, out_ref, moves_ref, bounds_ref, ids_ref, rows_ref, sems):
    rows_copy = pltpu.make_async_copy(rows_hbm, rows_ref, sems.at[0])
    ids_copy = pltpu.make_async_copy(ids_hbm, ids_ref, sems.at[1])
    rows_copy.start()
    ids_copy.start()
    count = rows_ref.shape[0]
    ids_copy.wait()
    ids_row = ids_ref[...].reshape(1, count)
    ids_column = as_column(ids_row)
    across = lax.broadcasted_iota(jnp.int32, (count, count), 1)
    down = lax.broadcasted_iota(jnp.int32, (count, count), 0)
    before = (ids_column < ids_row) | ((ids_column == ids_row) & (down < across))
    rank_row = jnp.sum(before.astype(jnp.int32), axis=0, keepdims=True)
    moved = down == rank_row
    moves = moved.astype(jnp.bfloat16)
    moves_ref[...] = moves
    label = jnp.sum(jnp.where(moved, ids_row, 0), axis=1, keepdims=True)
    first = jnp.sum((ids_row < label).astype(jnp.int32), axis=1, keepdims=True)
    after = jnp.sum((ids_row <= label).astype(jnp.int32), axis=1, keepdims=True)
    lane = lax.broadcasted_iota(jnp.int32, bounds_ref.shape, 1)
    bounds_ref[...] = jnp.where(lane == 0, first, after)
    rows_copy.wait()
    unit = normalize_rows(rows_ref[...])
    out_ref[...] = jnp.dot(moves, unit, preferred_element_type=jnp.float32).astype(jnp.bfloat16)


def partial_sums(queries, key_blocks, bounds, own):
    count = queries.shape[0]
    first, after = bounds[:, 0:1], bounds[:, 1:2]
    totals, weighted = 0.0, 0.0
    for index, keys in enumerate(key_blocks):
        similar = lax.dot_general(
            queries, keys, (((1,), (1,)), ((), ())), preferred_element_type=jnp.float32
        )
        key = lax.broadcasted_iota(jnp.int32, similar.shape, 1)
        place = lax.rem(key, count)
        allowed = (place >= first) & (place < after)
        if own and index == 0:
            allowed = allowed & (key != lax.broadcasted_iota(jnp.int32, similar.shape, 0))
        weights = jnp.where(allowed, jnp.exp(sharpness * (similar - 1.0)), 0.0)
        totals = totals + jnp.sum(weights, axis=1, keepdims=True)
        weighted = weighted + jnp.dot(
            weights.astype(jnp.bfloat16), keys, preferred_element_type=jnp.float32
        )
    return totals, weighted


def as_keys(block):
    return block.reshape(-1, block.shape[-1])


def neighbour_kernel(bounds_ref, queries_ref, column_ref, other_ref, out_ref):
    count, features = queries_ref.shape
    blocks = [as_keys(column_ref[...]), as_keys(other_ref[...])]
    totals, weighted = partial_sums(queries_ref[...], blocks, bounds_ref[...], False)
    out_ref[:, :features] = weighted.astype(jnp.bfloat16)
    high = totals.astype(jnp.bfloat16).astype(jnp.float32)
    lane = lax.broadcasted_iota(jnp.int32, (count, out_ref.shape[1] - features), 1)
    out_ref[:, features:] = jnp.where(lane == 0, high, totals - high).astype(jnp.bfloat16)


def own_kernel(bounds_ref, queries_ref, column_ref, other_ref, weighted_ref, totals_ref):
    blocks = [as_keys(column_ref[...]), as_keys(other_ref[...])]
    totals, weighted = partial_sums(queries_ref[...], blocks, bounds_ref[...], True)
    weighted_ref[...] = weighted
    totals_ref[...] = jnp.broadcast_to(totals, totals_ref.shape)


def finish_kernel(moves_ref, weighted_ref, totals_ref, back_ref, neighbour_ref, score_ref):
    count, features = neighbour_ref.shape
    back = back_ref[...].astype(jnp.float32)
    weighted = weighted_ref[...] + back[:, :features]
    totals = totals_ref[:, 0:1] + (
        back[:, features : features + 1] + back[:, features + 1 : features + 2]
    )
    normed = (
        weighted * lax.rsqrt(jnp.mean(weighted * weighted, axis=-1, keepdims=True) + epsilon)
    ).astype(jnp.bfloat16)
    moves = moves_ref[...]
    neighbour_ref[...] = lax.dot_general(
        moves, normed, (((0,), (0,)), ((), ())), preferred_element_type=jnp.float32
    ).astype(jnp.bfloat16)
    scores = jnp.sum(moves.astype(jnp.float32) * jnp.log(totals), axis=0, keepdims=True)
    score_ref[...] = scores.astype(jnp.bfloat16).reshape(count)


ACROSS = 4
EXTRA = 128


def gathered_body(embeddings, cluster_id):
    rows_dev, features = embeddings.shape
    devices = lax.axis_size("blk")
    planes = devices // ACROSS
    vmem = pl.BlockSpec(memory_space=pltpu.VMEM)
    stored = pl.BlockSpec(memory_space=pltpu.HBM)
    params = pltpu.CompilerParams(vmem_limit_bytes=32 * 1024 * 1024)

    def send(value, target):
        return lax.ppermute(value, "blk", [(device, target(device)) for device in range(devices)])

    def along(value, steps):
        return send(value, lambda device: (device + ACROSS * steps) % devices)

    def kernel(body, name, out_shape, *inputs, specs=None, scratch=()):
        return pl.pallas_call(
            body,
            out_shape=out_shape,
            in_specs=specs or [vmem] * len(inputs),
            out_specs=jax.tree.map(lambda _: vmem, out_shape),
            scratch_shapes=scratch,
            compiler_params=params,
            name=name,
        )(*inputs)

    def block(shape, kind):
        return jax.ShapeDtypeStruct(shape, kind)

    arranged, moves, bounds = kernel(
        arrange_kernel,
        "arrange",
        (
            block((rows_dev, features), jnp.bfloat16),
            block((rows_dev, rows_dev), jnp.bfloat16),
            block((rows_dev, 128), jnp.int32),
        ),
        cluster_id,
        embeddings,
        specs=[stored, stored],
        scratch=(
            pltpu.VMEM((rows_dev,), jnp.int32),
            pltpu.VMEM((rows_dev, features), jnp.bfloat16),
            pltpu.SemaphoreType.DMA((2,)),
        ),
    )
    visiting = [along(arranged, steps) for steps in range(1, planes)]
    queries = send(arranged, lambda device: device ^ 2)
    queries, *visiting = lax.optimization_barrier((queries, *visiting))
    column = jnp.concatenate([arranged, *visiting], axis=0)
    other = send(column, lambda device: device ^ 1)
    partial = kernel(
        neighbour_kernel,
        "neighbour",
        block((rows_dev, features + EXTRA), jnp.bfloat16),
        bounds,
        queries,
        column,
        other,
    )
    back = send(partial, lambda device: device ^ 2)
    weighted, totals = kernel(
        own_kernel,
        "own",
        (block((rows_dev, features), jnp.float32), block((rows_dev, 128), jnp.float32)),
        bounds,
        arranged,
        column,
        other,
    )
    return tuple(
        kernel(
            finish_kernel,
            "finish",
            (block((rows_dev, features), jnp.bfloat16), block((rows_dev,), jnp.bfloat16)),
            moves,
            weighted,
            totals,
            back,
        )
    )


def from_behind(value, axis, steps):
    count = lax.axis_size(axis)
    initial, last = (max(0, -steps), min(count, count - steps))
    return lax.ppermute(value, axis, [(source, source + steps) for source in range(initial, last)])


def pair_terms(queries, visiting, allowed):
    similar = jnp.dot(queries, visiting.T, preferred_element_type=jnp.float32)
    return jnp.where(allowed, jnp.exp(sharpness * (similar - 1.0)), jnp.zeros_like(similar))


def finish(weighted, totals):
    normed = (
        weighted * lax.rsqrt(jnp.mean(weighted * weighted, axis=-1, keepdims=True) + epsilon)
    ).astype(jnp.bfloat16)
    return (normed, jnp.log(totals).astype(jnp.bfloat16))


def collected_body(embeddings, cluster_id):
    rows_dev, features = embeddings.shape
    devices = lax.axis_size("blk")
    per_peer = rows_dev // devices
    clusters = devices // 4
    unit_rows = normalize_rows(embeddings)
    labels = jnp.arange(clusters, dtype=jnp.int32)
    counts = jnp.sum((cluster_id[:, None] == labels[None, :]).astype(jnp.int32), axis=0)
    group_ends = jnp.cumsum(counts // per_peer)

    def owner_cluster(device):
        in_range = (device >= 0) & (device < devices)
        return jnp.where(in_range, jnp.sum((device >= group_ends).astype(jnp.int32)), -1)

    position = jnp.arange(rows_dev, dtype=jnp.int32)
    arrange_order = jnp.argsort(cluster_id * rows_dev + position)
    inverse = jnp.argsort(arrange_order)
    arranged = unit_rows[arrange_order].reshape(devices, per_peer, features)
    held_rows = lax.all_to_all(arranged, "blk", split_axis=0, concat_axis=0, tiled=True).reshape(
        rows_dev, features
    )
    self_index = lax.axis_index("blk")
    mine = owner_cluster(self_index)
    weights = pair_terms(held_rows, held_rows, position[:, None] != position[None, :])
    totals = jnp.sum(weights, axis=1)
    weighted = jnp.dot(weights.astype(jnp.bfloat16), held_rows, preferred_element_type=jnp.float32)
    from_lower = held_rows
    from_upper = held_rows
    for distance in range(1, U_MAX):
        from_lower = from_behind(from_lower, "blk", 1)
        from_upper = from_behind(from_upper, "blk", -1)
        for visiting, source in (
            (from_lower, self_index - distance),
            (from_upper, self_index + distance),
        ):
            weights = pair_terms(held_rows, visiting, owner_cluster(source) == mine)
            totals = totals + jnp.sum(weights, axis=1)
            weighted = weighted + jnp.dot(
                weights.astype(jnp.bfloat16), visiting, preferred_element_type=jnp.float32
            )
    normed, scores = finish(weighted, totals)
    returned_rows, returned_scores = (
        lax.all_to_all(
            normed.reshape(devices, per_peer, features),
            "blk",
            split_axis=0,
            concat_axis=0,
            tiled=True,
        ),
        lax.all_to_all(
            scores.reshape(devices, per_peer), "blk", split_axis=0, concat_axis=0, tiled=True
        ),
    )
    neighbour = returned_rows.reshape(rows_dev, features)[inverse]
    dup_score = returned_scores.reshape(rows_dev)[inverse]
    return (neighbour, dup_score)


def solution(mesh):
    placed = (P(("groups", "blk"), None), P(("groups", "blk")))
    devices = mesh.shape["blk"]

    def body(embeddings, cluster_id):
        gathered = embeddings.size * embeddings.dtype.itemsize * devices
        fits = gathered <= GATHER_LIMIT and devices % ACROSS == 0
        plan = gathered_body if fits else collected_body
        return plan(embeddings, cluster_id)

    return jax.shard_map(
        body,
        mesh=mesh,
        in_specs=placed,
        out_specs=(P(("groups", "blk"), None), P(("groups", "blk"))),
        check_vma=False,
    )
```

```python
import jax
import jax.numpy as jnp
from jax import lax
from jax.experimental import pallas as pl
from jax.experimental.pallas import tpu as pltpu
from jax.sharding import PartitionSpec as P

U_MAX = 8
GATHER_LIMIT = 4 * 1024 * 1024


sharpness = 10.0
epsilon = 1e-06


def normalize_rows(values):
    widened = values.astype(jnp.float32)
    return (
        widened
        * lax.rsqrt(jnp.mean(widened * widened, axis=-1, keepdims=True) + epsilon)
        * widened.shape[-1] ** (-0.5)
    ).astype(jnp.bfloat16)


def as_column(row):
    count = row.shape[1]
    across = lax.broadcasted_iota(jnp.int32, (count, count), 1)
    down = lax.broadcasted_iota(jnp.int32, (count, count), 0)
    return jnp.sum(jnp.where(across == down, row, jnp.zeros_like(row)), axis=1, keepdims=True)


def as_row(column):
    count = column.shape[0]
    across = lax.broadcasted_iota(jnp.int32, (count, count), 1)
    down = lax.broadcasted_iota(jnp.int32, (count, count), 0)
    return jnp.sum(jnp.where(across == down, column, jnp.zeros_like(column)), axis=0, keepdims=True)


def arrange_kernel(ids_hbm, rows_hbm, out_ref, moves_ref, bounds_ref, ids_ref, rows_ref, sems):
    rows_copy = pltpu.make_async_copy(rows_hbm, rows_ref, sems.at[0])
    ids_copy = pltpu.make_async_copy(ids_hbm, ids_ref, sems.at[1])
    rows_copy.start()
    ids_copy.start()
    count = rows_ref.shape[0]
    ids_copy.wait()
    ids_row = ids_ref[...].reshape(1, count)
    ids_column = as_column(ids_row)
    across = lax.broadcasted_iota(jnp.int32, (count, count), 1)
    down = lax.broadcasted_iota(jnp.int32, (count, count), 0)
    before = (ids_column < ids_row) | ((ids_column == ids_row) & (down < across))
    rank_row = jnp.sum(before.astype(jnp.int32), axis=0, keepdims=True)
    moved = down == rank_row
    moves = moved.astype(jnp.bfloat16)
    moves_ref[...] = moves
    label = jnp.sum(jnp.where(moved, ids_row, 0), axis=1, keepdims=True)
    first = jnp.sum((ids_row < label).astype(jnp.int32), axis=1, keepdims=True)
    after = jnp.sum((ids_row <= label).astype(jnp.int32), axis=1, keepdims=True)
    lane = lax.broadcasted_iota(jnp.int32, bounds_ref.shape, 1)
    bounds_ref[...] = jnp.where(lane == 0, first, after)
    rows_copy.wait()
    unit = normalize_rows(rows_ref[...])
    out_ref[...] = jnp.dot(moves, unit, preferred_element_type=jnp.float32).astype(jnp.bfloat16)


def partial_sums(queries, key_blocks, first, after, own):
    count = key_blocks[0].shape[0]
    totals, weighted = 0.0, 0.0
    for index, keys in enumerate(key_blocks):
        similar = lax.dot_general(
            queries, keys, (((1,), (1,)), ((), ())), preferred_element_type=jnp.float32
        )
        place = lax.broadcasted_iota(jnp.int32, similar.shape, 1)
        allowed = (place >= first) & (place < after)
        if own and index == 0:
            allowed = allowed & (place != lax.broadcasted_iota(jnp.int32, similar.shape, 0))
        weights = jnp.where(allowed, jnp.exp(sharpness * (similar - 1.0)), 0.0)
        totals = totals + jnp.sum(weights, axis=1, keepdims=True)
        weighted = weighted + jnp.dot(
            weights.astype(jnp.bfloat16), keys, preferred_element_type=jnp.float32
        )
    return totals, weighted


def both(own, mate, bounds):
    bounds = jnp.concatenate([bounds, bounds], axis=0)
    return jnp.concatenate([own, mate], axis=0), bounds[:, 0:1], bounds[:, 1:2]


def first_kernel(bounds_ref, own_ref, mate_ref, *refs):
    *key_refs, weighted_ref, totals_ref = refs
    queries, first, after = both(own_ref[...], mate_ref[...], bounds_ref[...])
    totals, weighted = partial_sums(queries, [ref[...] for ref in key_refs], first, after, True)
    weighted_ref[...] = weighted
    totals_ref[...] = jnp.broadcast_to(totals, totals_ref.shape)


def second_kernel(bounds_ref, own_ref, mate_ref, so_far_ref, totals_so_far_ref, *refs):
    *key_refs, weighted_ref, totals_ref, out_ref = refs
    count, features = own_ref.shape
    queries, first, after = both(own_ref[...], mate_ref[...], bounds_ref[...])
    totals, weighted = partial_sums(queries, [ref[...] for ref in key_refs], first, after, False)
    totals = totals + totals_so_far_ref[:, 0:1]
    weighted = weighted + so_far_ref[...]
    out_ref[:, :features] = weighted[count:].astype(jnp.bfloat16)
    high = totals[count:].astype(jnp.bfloat16).astype(jnp.float32)
    lane = lax.broadcasted_iota(jnp.int32, (count, out_ref.shape[1] - features), 1)
    out_ref[:, features:] = jnp.where(lane == 0, high, totals[count:] - high).astype(jnp.bfloat16)
    weighted_ref[...] = weighted[:count]
    totals_ref[...] = jnp.broadcast_to(totals[:count], totals_ref.shape)


def finish_kernel(moves_ref, weighted_ref, totals_ref, back_ref, neighbour_ref, score_ref):
    count, features = neighbour_ref.shape
    back = back_ref[...].astype(jnp.float32)
    weighted = weighted_ref[...] + back[:, :features]
    totals = totals_ref[:, 0:1] + (
        back[:, features : features + 1] + back[:, features + 1 : features + 2]
    )
    normed = (
        weighted * lax.rsqrt(jnp.mean(weighted * weighted, axis=-1, keepdims=True) + epsilon)
    ).astype(jnp.bfloat16)
    moves = moves_ref[...]
    neighbour_ref[...] = lax.dot_general(
        moves, normed, (((0,), (0,)), ((), ())), preferred_element_type=jnp.float32
    ).astype(jnp.bfloat16)
    scores = jnp.sum(moves.astype(jnp.float32) * jnp.log(totals), axis=0, keepdims=True)
    score_ref[...] = scores.astype(jnp.bfloat16).reshape(count)


EXTRA = 128
CORE, ACROSS, NEAR, FAR = 1, 2, 4, 8
GRID = 16


def gathered_body(embeddings, cluster_id):
    rows_dev, features = embeddings.shape
    vmem = pl.BlockSpec(memory_space=pltpu.VMEM)
    anywhere = pl.BlockSpec(memory_space=pl.ANY)

    def swap(value, bit):
        return lax.ppermute(value, "blk", [(device, device ^ bit) for device in range(GRID)])

    def block(kind, *shape):
        return jax.ShapeDtypeStruct(shape, kind)

    rows = block(jnp.bfloat16, rows_dev, features)
    arranged, moves, bounds = pl.pallas_call(
        arrange_kernel,
        out_shape=(
            rows,
            block(jnp.bfloat16, rows_dev, rows_dev),
            block(jnp.int32, rows_dev, 128),
        ),
        in_specs=[anywhere, anywhere],
        out_specs=(vmem, vmem, vmem),
        scratch_shapes=(
            pltpu.VMEM((rows_dev,), jnp.int32),
            pltpu.VMEM((rows_dev, features), jnp.bfloat16),
            pltpu.SemaphoreType.DMA((2,)),
        ),
        name="arrange",
    )(cluster_id, embeddings)

    def kernel(body, name, out_shape, *inputs):
        return pl.pallas_call(
            body,
            out_shape=out_shape,
            in_specs=[vmem] * len(inputs),
            out_specs=(vmem,) * len(out_shape),
            compiler_params=pltpu.CompilerParams(vmem_limit_bytes=32 * 1024 * 1024),
            name=name,
        )(*inputs)

    far = swap(arranged, FAR)
    near = swap(arranged, NEAR)
    beside = swap(arranged, ACROSS)
    mate = swap(arranged, CORE)
    near_beside = swap(near, ACROSS)
    both_ways = swap(far, NEAR)
    far_beside = swap(far, ACROSS)
    weighted, totals = kernel(
        first_kernel,
        "first",
        (block(jnp.float32, 2 * rows_dev, features), block(jnp.float32, 2 * rows_dev, 128)),
        bounds,
        arranged,
        mate,
        *(arranged, near, beside, far),
    )
    both_beside = swap(both_ways, ACROSS)
    weighted, totals, partial = kernel(
        second_kernel,
        "second",
        (
            block(jnp.float32, rows_dev, features),
            block(jnp.float32, rows_dev, 128),
            block(jnp.bfloat16, rows_dev, features + EXTRA),
        ),
        bounds,
        arranged,
        mate,
        weighted,
        totals,
        *(near_beside, both_ways, far_beside, both_beside),
    )
    back = swap(partial, CORE)
    return tuple(
        kernel(
            finish_kernel,
            "finish",
            (rows, block(jnp.bfloat16, rows_dev)),
            moves,
            weighted,
            totals,
            back,
        )
    )


def from_behind(value, axis, steps):
    count = lax.axis_size(axis)
    initial, last = (max(0, -steps), min(count, count - steps))
    return lax.ppermute(value, axis, [(source, source + steps) for source in range(initial, last)])


def pair_terms(queries, visiting, allowed):
    similar = jnp.dot(queries, visiting.T, preferred_element_type=jnp.float32)
    return jnp.where(allowed, jnp.exp(sharpness * (similar - 1.0)), jnp.zeros_like(similar))


def finish(weighted, totals):
    normed = (
        weighted * lax.rsqrt(jnp.mean(weighted * weighted, axis=-1, keepdims=True) + epsilon)
    ).astype(jnp.bfloat16)
    return (normed, jnp.log(totals).astype(jnp.bfloat16))


def collected_body(embeddings, cluster_id):
    rows_dev, features = embeddings.shape
    devices = lax.axis_size("blk")
    per_peer = rows_dev // devices
    clusters = devices // 4
    unit_rows = normalize_rows(embeddings)
    labels = jnp.arange(clusters, dtype=jnp.int32)
    counts = jnp.sum((cluster_id[:, None] == labels[None, :]).astype(jnp.int32), axis=0)
    group_ends = jnp.cumsum(counts // per_peer)

    def owner_cluster(device):
        in_range = (device >= 0) & (device < devices)
        return jnp.where(in_range, jnp.sum((device >= group_ends).astype(jnp.int32)), -1)

    position = jnp.arange(rows_dev, dtype=jnp.int32)
    arrange_order = jnp.argsort(cluster_id * rows_dev + position)
    inverse = jnp.argsort(arrange_order)
    arranged = unit_rows[arrange_order].reshape(devices, per_peer, features)
    held_rows = lax.all_to_all(arranged, "blk", split_axis=0, concat_axis=0, tiled=True).reshape(
        rows_dev, features
    )
    self_index = lax.axis_index("blk")
    mine = owner_cluster(self_index)
    weights = pair_terms(held_rows, held_rows, position[:, None] != position[None, :])
    totals = jnp.sum(weights, axis=1)
    weighted = jnp.dot(weights.astype(jnp.bfloat16), held_rows, preferred_element_type=jnp.float32)
    from_lower = held_rows
    from_upper = held_rows
    for distance in range(1, U_MAX):
        from_lower = from_behind(from_lower, "blk", 1)
        from_upper = from_behind(from_upper, "blk", -1)
        for visiting, source in (
            (from_lower, self_index - distance),
            (from_upper, self_index + distance),
        ):
            weights = pair_terms(held_rows, visiting, owner_cluster(source) == mine)
            totals = totals + jnp.sum(weights, axis=1)
            weighted = weighted + jnp.dot(
                weights.astype(jnp.bfloat16), visiting, preferred_element_type=jnp.float32
            )
    normed, scores = finish(weighted, totals)
    returned_rows, returned_scores = (
        lax.all_to_all(
            normed.reshape(devices, per_peer, features),
            "blk",
            split_axis=0,
            concat_axis=0,
            tiled=True,
        ),
        lax.all_to_all(
            scores.reshape(devices, per_peer), "blk", split_axis=0, concat_axis=0, tiled=True
        ),
    )
    neighbour = returned_rows.reshape(rows_dev, features)[inverse]
    dup_score = returned_scores.reshape(rows_dev)[inverse]
    return (neighbour, dup_score)


def solution(mesh):
    placed = (P(("groups", "blk"), None), P(("groups", "blk")))
    devices = mesh.shape["blk"]

    def body(embeddings, cluster_id):
        gathered = embeddings.size * embeddings.dtype.itemsize * devices
        fits = gathered <= GATHER_LIMIT and devices == GRID
        plan = gathered_body if fits else collected_body
        return plan(embeddings, cluster_id)

    return jax.shard_map(
        body,
        mesh=mesh,
        in_specs=placed,
        out_specs=(P(("groups", "blk"), None), P(("groups", "blk"))),
        check_vma=False,
    )
```

```python
import jax
import jax.numpy as jnp
from jax import lax
from jax.experimental import pallas as pl
from jax.experimental.pallas import tpu as pltpu
from jax.sharding import PartitionSpec as P

U_MAX = 8
GATHER_LIMIT = 4 * 1024 * 1024


sharpness = 10.0
epsilon = 1e-06


def normalize_rows(values):
    widened = values.astype(jnp.float32)
    return (
        widened
        * lax.rsqrt(jnp.mean(widened * widened, axis=-1, keepdims=True) + epsilon)
        * widened.shape[-1] ** (-0.5)
    ).astype(jnp.bfloat16)


def as_column(row):
    count = row.shape[1]
    across = lax.broadcasted_iota(jnp.int32, (count, count), 1)
    down = lax.broadcasted_iota(jnp.int32, (count, count), 0)
    return jnp.sum(jnp.where(across == down, row, jnp.zeros_like(row)), axis=1, keepdims=True)


def as_row(column):
    count = column.shape[0]
    across = lax.broadcasted_iota(jnp.int32, (count, count), 1)
    down = lax.broadcasted_iota(jnp.int32, (count, count), 0)
    return jnp.sum(jnp.where(across == down, column, jnp.zeros_like(column)), axis=0, keepdims=True)


def arrange_kernel(ids_hbm, rows_hbm, out_ref, moves_ref, bounds_ref, ids_ref, rows_ref, sems):
    rows_copy = pltpu.make_async_copy(rows_hbm, rows_ref, sems.at[0])
    ids_copy = pltpu.make_async_copy(ids_hbm, ids_ref, sems.at[1])
    rows_copy.start()
    ids_copy.start()
    count = rows_ref.shape[0]
    ids_copy.wait()
    ids_row = ids_ref[...].reshape(1, count)
    ids_column = as_column(ids_row)
    across = lax.broadcasted_iota(jnp.int32, (count, count), 1)
    down = lax.broadcasted_iota(jnp.int32, (count, count), 0)
    before = (ids_column < ids_row) | ((ids_column == ids_row) & (down < across))
    rank_row = jnp.sum(before.astype(jnp.int32), axis=0, keepdims=True)
    moved = down == rank_row
    moves = moved.astype(jnp.bfloat16)
    moves_ref[...] = moves
    label = jnp.sum(jnp.where(moved, ids_row, 0), axis=1, keepdims=True)
    first = jnp.sum((ids_row < label).astype(jnp.int32), axis=1, keepdims=True)
    after = jnp.sum((ids_row <= label).astype(jnp.int32), axis=1, keepdims=True)
    lane = lax.broadcasted_iota(jnp.int32, bounds_ref.shape, 1)
    bounds_ref[...] = jnp.where(lane == 0, first, after)
    rows_copy.wait()
    unit = normalize_rows(rows_ref[...])
    out_ref[...] = jnp.dot(moves, unit, preferred_element_type=jnp.float32).astype(jnp.bfloat16)


def partial_sums(queries, key_blocks, bounds, own):
    totals, weighted = 0.0, 0.0
    first, after = bounds[:, 0:1], bounds[:, 1:2]
    for index, keys in enumerate(key_blocks):
        similar = lax.dot_general(
            queries, keys, (((1,), (1,)), ((), ())), preferred_element_type=jnp.float32
        )
        place = lax.broadcasted_iota(jnp.int32, similar.shape, 1)
        allowed = (place >= first) & (place < after)
        if own and index == 0:
            allowed = allowed & (place != lax.broadcasted_iota(jnp.int32, similar.shape, 0))
        weights = jnp.where(allowed, jnp.exp(sharpness * (similar - 1.0)), 0.0)
        totals = totals + jnp.sum(weights, axis=1, keepdims=True)
        weighted = weighted + jnp.dot(
            weights.astype(jnp.bfloat16), keys, preferred_element_type=jnp.float32
        )
    return totals, weighted


QUERIES = 4


def first_kernel(bounds_ref, *refs):
    query_refs, key_refs, (weighted_ref, totals_ref) = refs[:QUERIES], refs[QUERIES:-2], refs[-2:]
    queries = jnp.concatenate([ref[...] for ref in query_refs], axis=0)
    bounds = jnp.concatenate([bounds_ref[...]] * QUERIES, axis=0)
    totals, weighted = partial_sums(queries, [ref[...] for ref in key_refs], bounds, True)
    weighted_ref[...] = weighted
    totals_ref[...] = jnp.broadcast_to(totals, totals_ref.shape)


def second_kernel(so_far_ref, totals_so_far_ref, bounds_ref, *refs):
    query_refs, (key_ref, weighted_ref, totals_ref), out_refs = (
        refs[:QUERIES],
        refs[QUERIES : QUERIES + 3],
        refs[QUERIES + 3 :],
    )
    queries = jnp.concatenate([ref[...] for ref in query_refs], axis=0)
    bounds = jnp.concatenate([bounds_ref[...]] * QUERIES, axis=0)
    totals, weighted = partial_sums(queries, [key_ref[...]], bounds, False)
    totals = totals + totals_so_far_ref[:, 0:1]
    weighted = weighted + so_far_ref[...]
    count, features = weighted_ref.shape
    weighted_ref[...] = weighted[:count]
    totals_ref[...] = jnp.broadcast_to(totals[:count], totals_ref.shape)
    for index, out_ref in enumerate(out_refs):
        rows = slice((index + 1) * count, (index + 2) * count)
        out_ref[:, :features] = weighted[rows].astype(jnp.bfloat16)
        high = totals[rows].astype(jnp.bfloat16).astype(jnp.float32)
        lane = lax.broadcasted_iota(jnp.int32, (count, out_ref.shape[1] - features), 1)
        out_ref[:, features:] = jnp.where(lane == 0, high, totals[rows] - high).astype(jnp.bfloat16)


def finish_kernel(moves_ref, weighted_ref, totals_ref, *refs):
    *back_refs, neighbour_ref, score_ref = refs
    count, features = neighbour_ref.shape
    weighted, totals = weighted_ref[...], totals_ref[:, 0:1]
    for back_ref in back_refs:
        back = back_ref[...].astype(jnp.float32)
        weighted = weighted + back[:, :features]
        totals = totals + (
            back[:, features : features + 1] + back[:, features + 1 : features + 2]
        )
    normed = (
        weighted * lax.rsqrt(jnp.mean(weighted * weighted, axis=-1, keepdims=True) + epsilon)
    ).astype(jnp.bfloat16)
    moves = moves_ref[...]
    neighbour_ref[...] = lax.dot_general(
        moves, normed, (((0,), (0,)), ((), ())), preferred_element_type=jnp.float32
    ).astype(jnp.bfloat16)
    scores = jnp.sum(moves.astype(jnp.float32) * jnp.log(totals), axis=0, keepdims=True)
    score_ref[...] = scores.astype(jnp.bfloat16).reshape(count)


EXTRA = 128
CORE, ACROSS, NEAR, FAR = 1, 2, 4, 8
GRID = 16


def gathered_body(embeddings, cluster_id):
    rows_dev, features = embeddings.shape
    vmem = pl.BlockSpec(memory_space=pltpu.VMEM)
    stored = pl.BlockSpec(memory_space=pltpu.HBM)

    def swap(value, bits):
        return lax.ppermute(value, "blk", [(device, device ^ bits) for device in range(GRID)])

    def block(kind, *shape):
        return jax.ShapeDtypeStruct(shape, kind)

    def kernel(body, name, out_shape, *inputs, specs=None, scratch=()):
        return pl.pallas_call(
            body,
            out_shape=out_shape,
            in_specs=specs or [vmem] * len(inputs),
            out_specs=(vmem,) * len(out_shape),
            scratch_shapes=scratch,
            compiler_params=pltpu.CompilerParams(vmem_limit_bytes=32 * 1024 * 1024),
            name=name,
        )(*inputs)

    rows = block(jnp.bfloat16, rows_dev, features)
    own, moves, bounds = kernel(
        arrange_kernel,
        "arrange",
        (rows, block(jnp.bfloat16, rows_dev, rows_dev), block(jnp.int32, rows_dev, 128)),
        pltpu.with_memory_space_constraint(cluster_id, pltpu.HBM),
        pltpu.with_memory_space_constraint(embeddings, pltpu.HBM),
        specs=[stored, stored],
        scratch=(
            pltpu.VMEM((rows_dev,), jnp.int32),
            pltpu.VMEM((rows_dev, features), jnp.bfloat16),
            pltpu.SemaphoreType.DMA((2,)),
        ),
    )

    others = (NEAR | ACROSS, ACROSS, NEAR)
    queries = (own, *(swap(own, bits) for bits in others))
    far = swap(own, FAR)
    mate = swap(own, CORE)
    *queries, far = lax.optimization_barrier((*queries, far))
    far_mate = swap(far, CORE)
    weighted, totals = kernel(
        first_kernel,
        "first",
        (
            block(jnp.float32, QUERIES * rows_dev, features),
            block(jnp.float32, QUERIES * rows_dev, 128),
        ),
        bounds,
        *queries,
        *(own, mate, far),
    )
    weighted, totals, *partials = kernel(
        second_kernel,
        "second",
        (
            block(jnp.float32, rows_dev, features),
            block(jnp.float32, rows_dev, 128),
            *(block(jnp.bfloat16, rows_dev, features + EXTRA) for _ in others),
        ),
        weighted,
        totals,
        bounds,
        *queries,
        far_mate,
    )
    backs = [swap(partial, bits) for partial, bits in zip(partials, others)]
    return tuple(
        kernel(
            finish_kernel,
            "finish",
            (rows, block(jnp.bfloat16, rows_dev)),
            moves,
            weighted,
            totals,
            *backs,
        )
    )


def from_behind(value, axis, steps):
    count = lax.axis_size(axis)
    initial, last = (max(0, -steps), min(count, count - steps))
    return lax.ppermute(value, axis, [(source, source + steps) for source in range(initial, last)])


def pair_terms(queries, visiting, allowed):
    similar = jnp.dot(queries, visiting.T, preferred_element_type=jnp.float32)
    return jnp.where(allowed, jnp.exp(sharpness * (similar - 1.0)), jnp.zeros_like(similar))


def finish(weighted, totals):
    normed = (
        weighted * lax.rsqrt(jnp.mean(weighted * weighted, axis=-1, keepdims=True) + epsilon)
    ).astype(jnp.bfloat16)
    return (normed, jnp.log(totals).astype(jnp.bfloat16))


def collected_body(embeddings, cluster_id):
    rows_dev, features = embeddings.shape
    devices = lax.axis_size("blk")
    per_peer = rows_dev // devices
    clusters = devices // 4
    unit_rows = normalize_rows(embeddings)
    labels = jnp.arange(clusters, dtype=jnp.int32)
    counts = jnp.sum((cluster_id[:, None] == labels[None, :]).astype(jnp.int32), axis=0)
    group_ends = jnp.cumsum(counts // per_peer)

    def owner_cluster(device):
        in_range = (device >= 0) & (device < devices)
        return jnp.where(in_range, jnp.sum((device >= group_ends).astype(jnp.int32)), -1)

    position = jnp.arange(rows_dev, dtype=jnp.int32)
    arrange_order = jnp.argsort(cluster_id * rows_dev + position)
    inverse = jnp.argsort(arrange_order)
    arranged = unit_rows[arrange_order].reshape(devices, per_peer, features)
    held_rows = lax.all_to_all(arranged, "blk", split_axis=0, concat_axis=0, tiled=True).reshape(
        rows_dev, features
    )
    self_index = lax.axis_index("blk")
    mine = owner_cluster(self_index)
    weights = pair_terms(held_rows, held_rows, position[:, None] != position[None, :])
    totals = jnp.sum(weights, axis=1)
    weighted = jnp.dot(weights.astype(jnp.bfloat16), held_rows, preferred_element_type=jnp.float32)
    from_lower = held_rows
    from_upper = held_rows
    for distance in range(1, U_MAX):
        from_lower = from_behind(from_lower, "blk", 1)
        from_upper = from_behind(from_upper, "blk", -1)
        for visiting, source in (
            (from_lower, self_index - distance),
            (from_upper, self_index + distance),
        ):
            weights = pair_terms(held_rows, visiting, owner_cluster(source) == mine)
            totals = totals + jnp.sum(weights, axis=1)
            weighted = weighted + jnp.dot(
                weights.astype(jnp.bfloat16), visiting, preferred_element_type=jnp.float32
            )
    normed, scores = finish(weighted, totals)
    returned_rows, returned_scores = (
        lax.all_to_all(
            normed.reshape(devices, per_peer, features),
            "blk",
            split_axis=0,
            concat_axis=0,
            tiled=True,
        ),
        lax.all_to_all(
            scores.reshape(devices, per_peer), "blk", split_axis=0, concat_axis=0, tiled=True
        ),
    )
    neighbour = returned_rows.reshape(rows_dev, features)[inverse]
    dup_score = returned_scores.reshape(rows_dev)[inverse]
    return (neighbour, dup_score)


def solution(mesh):
    placed = (P(("groups", "blk"), None), P(("groups", "blk")))
    devices = mesh.shape["blk"]

    def body(embeddings, cluster_id):
        gathered = embeddings.size * embeddings.dtype.itemsize * devices
        fits = gathered <= GATHER_LIMIT and devices == GRID
        plan = gathered_body if fits else collected_body
        return plan(embeddings, cluster_id)

    return jax.shard_map(
        body,
        mesh=mesh,
        in_specs=placed,
        out_specs=(P(("groups", "blk"), None), P(("groups", "blk"))),
        check_vma=False,
    )
```

```python
import jax
import jax.numpy as jnp
from jax import lax
from jax.experimental import pallas as pl
from jax.experimental.pallas import tpu as pltpu
from jax.sharding import PartitionSpec as P

U_MAX = 8
GATHER_LIMIT = 4 * 1024 * 1024


sharpness = 10.0
epsilon = 1e-06


def normalize_rows(values):
    widened = values.astype(jnp.float32)
    return (
        widened
        * lax.rsqrt(jnp.mean(widened * widened, axis=-1, keepdims=True) + epsilon)
        * widened.shape[-1] ** (-0.5)
    ).astype(jnp.bfloat16)


def as_column(row):
    count = row.shape[1]
    across = lax.broadcasted_iota(jnp.int32, (count, count), 1)
    down = lax.broadcasted_iota(jnp.int32, (count, count), 0)
    return jnp.sum(jnp.where(across == down, row, jnp.zeros_like(row)), axis=1, keepdims=True)


def as_row(column):
    count = column.shape[0]
    across = lax.broadcasted_iota(jnp.int32, (count, count), 1)
    down = lax.broadcasted_iota(jnp.int32, (count, count), 0)
    return jnp.sum(jnp.where(across == down, column, jnp.zeros_like(column)), axis=0, keepdims=True)


def arrange_kernel(ids_hbm, rows_hbm, out_ref, moves_ref, bounds_ref, ids_ref, rows_ref, sems):
    rows_copy = pltpu.make_async_copy(rows_hbm, rows_ref, sems.at[0])
    ids_copy = pltpu.make_async_copy(ids_hbm, ids_ref, sems.at[1])
    rows_copy.start()
    ids_copy.start()
    count = rows_ref.shape[0]
    ids_copy.wait()
    ids_row = ids_ref[...].reshape(1, count)
    ids_column = as_column(ids_row)
    across = lax.broadcasted_iota(jnp.int32, (count, count), 1)
    down = lax.broadcasted_iota(jnp.int32, (count, count), 0)
    before = (ids_column < ids_row) | ((ids_column == ids_row) & (down < across))
    rank_row = jnp.sum(before.astype(jnp.int32), axis=0, keepdims=True)
    moved = down == rank_row
    moves = moved.astype(jnp.bfloat16)
    moves_ref[...] = moves
    label = jnp.sum(jnp.where(moved, ids_row, 0), axis=1, keepdims=True)
    first = jnp.sum((ids_row < label).astype(jnp.int32), axis=1, keepdims=True)
    after = jnp.sum((ids_row <= label).astype(jnp.int32), axis=1, keepdims=True)
    lane = lax.broadcasted_iota(jnp.int32, bounds_ref.shape, 1)
    bounds_ref[...] = jnp.where(lane == 0, first, after)
    rows_copy.wait()
    unit = normalize_rows(rows_ref[...])
    out_ref[...] = jnp.dot(moves, unit, preferred_element_type=jnp.float32).astype(jnp.bfloat16)


def partial_sums(queries, key_blocks, bounds, own, block_rows):
    totals, weighted = 0.0, 0.0
    first, after = bounds[:, 0:1], bounds[:, 1:2]
    for index, keys in enumerate(key_blocks):
        similar = lax.dot_general(
            queries, keys, (((1,), (1,)), ((), ())), preferred_element_type=jnp.float32
        )
        place = lax.rem(lax.broadcasted_iota(jnp.int32, similar.shape, 1), block_rows)
        allowed = (place >= first) & (place < after)
        if own and index == 0:
            allowed = allowed & (place != lax.broadcasted_iota(jnp.int32, similar.shape, 0))
        weights = jnp.where(allowed, jnp.exp(sharpness * (similar - 1.0)), 0.0)
        totals = totals + jnp.sum(weights, axis=1, keepdims=True)
        weighted = weighted + jnp.dot(
            weights.astype(jnp.bfloat16), keys, preferred_element_type=jnp.float32
        )
    return totals, weighted


LANES = 128


def gather_refs(refs):
    return [ref[...] for ref in refs]


def first_kernel(bounds_ref, own_ref, beside_ref, *refs):
    *key_refs, weighted_ref, totals_ref = refs
    queries = jnp.concatenate([own_ref[...], beside_ref[...]], axis=0)
    bounds = jnp.concatenate([bounds_ref[...]] * 2, axis=0)
    totals, weighted = partial_sums(queries, gather_refs(key_refs), bounds, True, own_ref.shape[0])
    weighted_ref[...] = weighted
    totals_ref[...] = jnp.broadcast_to(totals, totals_ref.shape)


def beside_kernel(so_far_ref, totals_so_far_ref, bounds_ref, beside_ref, *refs):
    *key_refs, out_ref = refs
    count = beside_ref.shape[0]
    keys = gather_refs(key_refs)
    totals, weighted = partial_sums(beside_ref[...], keys, bounds_ref[...], False, count)
    totals = totals + totals_so_far_ref[count:, 0:1]
    weighted = (weighted + so_far_ref[count:, :]).astype(jnp.bfloat16)
    columns = weighted.shape[1] // LANES
    for index in range(columns):
        out_ref[index * count : (index + 1) * count, :] = weighted[
            :, index * LANES : (index + 1) * LANES
        ]
    extra = out_ref.shape[0] - columns * count
    totals = jnp.concatenate([as_row(totals), jnp.zeros((1, LANES - count), jnp.float32)], axis=1)
    high = totals.astype(jnp.bfloat16).astype(jnp.float32)
    row = lax.broadcasted_iota(jnp.int32, (extra, LANES), 0)
    out_ref[columns * count :, :] = jnp.where(row == 0, high, totals - high).astype(jnp.bfloat16)


def own_kernel(so_far_ref, totals_so_far_ref, bounds_ref, own_ref, *refs):
    *key_refs, weighted_ref, totals_ref = refs
    count = own_ref.shape[0]
    keys = gather_refs(key_refs)
    totals, weighted = partial_sums(own_ref[...], keys, bounds_ref[...], False, count)
    weighted_ref[...] = weighted + so_far_ref[:count, :]
    totals_ref[...] = as_row(totals + totals_so_far_ref[:count, 0:1])


def finish_kernel(moves_ref, weighted_ref, totals_ref, back_ref, neighbour_hbm, score_hbm, neighbour_ref, score_ref, sems):
    count, features = neighbour_ref.shape
    columns = features // LANES
    back = [
        back_ref[index * count : (index + 1) * count, :].astype(jnp.float32)
        for index in range(columns)
    ]
    weighted = weighted_ref[...] + jnp.concatenate(back, axis=1)
    normed = (
        weighted * lax.rsqrt(jnp.mean(weighted * weighted, axis=-1, keepdims=True) + epsilon)
    ).astype(jnp.bfloat16)
    moves = moves_ref[...]
    neighbour_ref[...] = lax.dot_general(
        moves, normed, (((0,), (0,)), ((), ())), preferred_element_type=jnp.float32
    ).astype(jnp.bfloat16)
    neighbour_copy = pltpu.make_async_copy(neighbour_ref, neighbour_hbm, sems.at[0])
    neighbour_copy.start()
    pair = back_ref[columns * count :, :].astype(jnp.float32)
    totals = totals_ref[...] + (pair[0:1, :count] + pair[1:2, :count])
    scores = jnp.sum(moves.astype(jnp.float32) * as_column(jnp.log(totals)), axis=0, keepdims=True)
    score_ref[...] = scores.astype(jnp.bfloat16).reshape(count)
    score_copy = pltpu.make_async_copy(score_ref, score_hbm, sems.at[1])
    score_copy.start()
    neighbour_copy.wait()
    score_copy.wait()


EXTRA = 16
CORE, ACROSS, NEAR, FAR = 1, 2, 4, 8
GRID = 16


def gathered_body(embeddings, cluster_id):
    rows_dev, features = embeddings.shape
    vmem = pl.BlockSpec(memory_space=pltpu.VMEM)
    stored = pl.BlockSpec(memory_space=pltpu.HBM)

    def swap(value, bits):
        return lax.ppermute(value, "blk", [(device, device ^ bits) for device in range(GRID)])

    def block(kind, *shape):
        return jax.ShapeDtypeStruct(shape, kind)

    def kernel(body, name, out_shape, *inputs, specs=vmem, out_specs=vmem, scratch=()):
        return pl.pallas_call(
            body,
            out_shape=out_shape,
            in_specs=[specs] * len(inputs),
            out_specs=(out_specs,) * len(out_shape),
            scratch_shapes=scratch,
            compiler_params=pltpu.CompilerParams(vmem_limit_bytes=32 * 1024 * 1024),
            name=name,
        )(*inputs)

    rows = block(jnp.bfloat16, rows_dev, features)
    own, moves, bounds = kernel(
        arrange_kernel,
        "arrange",
        (rows, block(jnp.bfloat16, rows_dev, rows_dev), block(jnp.int32, rows_dev, LANES)),
        pltpu.with_memory_space_constraint(cluster_id, pltpu.HBM),
        pltpu.with_memory_space_constraint(embeddings, pltpu.HBM),
        specs=stored,
        scratch=(
            pltpu.VMEM((rows_dev,), jnp.int32),
            pltpu.VMEM((rows_dev, features), jnp.bfloat16),
            pltpu.SemaphoreType.DMA((2,)),
        ),
    )

    farther, far, near, beside, mate = lax.optimization_barrier(
        tuple(swap(own, bits) for bits in (FAR | NEAR, FAR, NEAR, ACROSS, CORE))
    )
    mates = swap(jnp.concatenate([near, far, farther], axis=0), CORE)
    weighted, totals = kernel(
        first_kernel,
        "first",
        (block(jnp.float32, 2 * rows_dev, features), block(jnp.float32, 2 * rows_dev, LANES)),
        *(bounds, own, beside),
        *(own, mate, near, far, farther),
    )
    (partial,) = kernel(
        beside_kernel,
        "beside",
        (block(jnp.bfloat16, rows_dev * features // LANES + EXTRA, LANES),),
        *(weighted, totals, bounds, beside, mates),
    )
    back = swap(partial, ACROSS)
    weighted, totals = kernel(
        own_kernel,
        "own",
        (block(jnp.float32, rows_dev, features), block(jnp.float32, 1, rows_dev)),
        *(weighted, totals, bounds, own, mates),
    )
    return tuple(
        kernel(
            finish_kernel,
            "finish",
            (rows, block(jnp.bfloat16, rows_dev)),
            *(moves, weighted, totals, back),
            out_specs=stored,
            scratch=(
                pltpu.VMEM((rows_dev, features), jnp.bfloat16),
                pltpu.VMEM((rows_dev,), jnp.bfloat16),
                pltpu.SemaphoreType.DMA((2,)),
            ),
        )
    )


def from_behind(value, axis, steps):
    count = lax.axis_size(axis)
    initial, last = (max(0, -steps), min(count, count - steps))
    return lax.ppermute(value, axis, [(source, source + steps) for source in range(initial, last)])


def pair_terms(queries, visiting, allowed):
    similar = jnp.dot(queries, visiting.T, preferred_element_type=jnp.float32)
    return jnp.where(allowed, jnp.exp(sharpness * (similar - 1.0)), jnp.zeros_like(similar))


def finish(weighted, totals):
    normed = (
        weighted * lax.rsqrt(jnp.mean(weighted * weighted, axis=-1, keepdims=True) + epsilon)
    ).astype(jnp.bfloat16)
    return (normed, jnp.log(totals).astype(jnp.bfloat16))


def collected_body(embeddings, cluster_id):
    rows_dev, features = embeddings.shape
    devices = lax.axis_size("blk")
    per_peer = rows_dev // devices
    clusters = devices // 4
    unit_rows = normalize_rows(embeddings)
    labels = jnp.arange(clusters, dtype=jnp.int32)
    counts = jnp.sum((cluster_id[:, None] == labels[None, :]).astype(jnp.int32), axis=0)
    group_ends = jnp.cumsum(counts // per_peer)

    def owner_cluster(device):
        in_range = (device >= 0) & (device < devices)
        return jnp.where(in_range, jnp.sum((device >= group_ends).astype(jnp.int32)), -1)

    position = jnp.arange(rows_dev, dtype=jnp.int32)
    arrange_order = jnp.argsort(cluster_id * rows_dev + position)
    inverse = jnp.argsort(arrange_order)
    arranged = unit_rows[arrange_order].reshape(devices, per_peer, features)
    held_rows = lax.all_to_all(arranged, "blk", split_axis=0, concat_axis=0, tiled=True).reshape(
        rows_dev, features
    )
    self_index = lax.axis_index("blk")
    mine = owner_cluster(self_index)
    weights = pair_terms(held_rows, held_rows, position[:, None] != position[None, :])
    totals = jnp.sum(weights, axis=1)
    weighted = jnp.dot(weights.astype(jnp.bfloat16), held_rows, preferred_element_type=jnp.float32)
    from_lower = held_rows
    from_upper = held_rows
    for distance in range(1, U_MAX):
        from_lower = from_behind(from_lower, "blk", 1)
        from_upper = from_behind(from_upper, "blk", -1)
        for visiting, source in (
            (from_lower, self_index - distance),
            (from_upper, self_index + distance),
        ):
            weights = pair_terms(held_rows, visiting, owner_cluster(source) == mine)
            totals = totals + jnp.sum(weights, axis=1)
            weighted = weighted + jnp.dot(
                weights.astype(jnp.bfloat16), visiting, preferred_element_type=jnp.float32
            )
    normed, scores = finish(weighted, totals)
    returned_rows, returned_scores = (
        lax.all_to_all(
            normed.reshape(devices, per_peer, features),
            "blk",
            split_axis=0,
            concat_axis=0,
            tiled=True,
        ),
        lax.all_to_all(
            scores.reshape(devices, per_peer), "blk", split_axis=0, concat_axis=0, tiled=True
        ),
    )
    neighbour = returned_rows.reshape(rows_dev, features)[inverse]
    dup_score = returned_scores.reshape(rows_dev)[inverse]
    return (neighbour, dup_score)


def solution(mesh):
    placed = (P(("groups", "blk"), None), P(("groups", "blk")))
    devices = mesh.shape["blk"]

    def body(embeddings, cluster_id):
        gathered = embeddings.size * embeddings.dtype.itemsize * devices
        fits = gathered <= GATHER_LIMIT and devices == GRID
        plan = gathered_body if fits else collected_body
        return plan(embeddings, cluster_id)

    return jax.shard_map(
        body,
        mesh=mesh,
        in_specs=placed,
        out_specs=(P(("groups", "blk"), None), P(("groups", "blk"))),
        check_vma=False,
    )
```

```python
import jax
import jax.numpy as jnp
from jax import lax
from jax.experimental import pallas as pl
from jax.experimental.pallas import tpu as pltpu
from jax.sharding import PartitionSpec as P

U_MAX = 8
GATHER_LIMIT = 4 * 1024 * 1024


sharpness = 10.0
epsilon = 1e-06


def normalize_rows(values):
    widened = values.astype(jnp.float32)
    return (
        widened
        * lax.rsqrt(jnp.mean(widened * widened, axis=-1, keepdims=True) + epsilon)
        * widened.shape[-1] ** (-0.5)
    ).astype(jnp.bfloat16)


def as_column(row):
    count = row.shape[1]
    across = lax.broadcasted_iota(jnp.int32, (count, count), 1)
    down = lax.broadcasted_iota(jnp.int32, (count, count), 0)
    return jnp.sum(jnp.where(across == down, row, jnp.zeros_like(row)), axis=1, keepdims=True)


def as_row(column):
    count = column.shape[0]
    across = lax.broadcasted_iota(jnp.int32, (count, count), 1)
    down = lax.broadcasted_iota(jnp.int32, (count, count), 0)
    return jnp.sum(jnp.where(across == down, column, jnp.zeros_like(column)), axis=0, keepdims=True)


def arrange_kernel(ids_hbm, rows_hbm, out_ref, moves_ref, bounds_ref, ids_ref, rows_ref, sems):
    rows_copy = pltpu.make_async_copy(rows_hbm, rows_ref, sems.at[0])
    ids_copy = pltpu.make_async_copy(ids_hbm, ids_ref, sems.at[1])
    rows_copy.start()
    ids_copy.start()
    count = rows_ref.shape[0]
    ids_copy.wait()
    ids_row = ids_ref[...].reshape(1, count)
    ids_column = as_column(ids_row)
    across = lax.broadcasted_iota(jnp.int32, (count, count), 1)
    down = lax.broadcasted_iota(jnp.int32, (count, count), 0)
    before = (ids_column < ids_row) | ((ids_column == ids_row) & (down < across))
    rank_row = jnp.sum(before.astype(jnp.int32), axis=0, keepdims=True)
    moved = down == rank_row
    moves = moved.astype(jnp.bfloat16)
    moves_ref[...] = moves
    label = jnp.sum(jnp.where(moved, ids_row, 0), axis=1, keepdims=True)
    first = jnp.sum((ids_row < label).astype(jnp.int32), axis=1, keepdims=True)
    after = jnp.sum((ids_row <= label).astype(jnp.int32), axis=1, keepdims=True)
    lane = lax.broadcasted_iota(jnp.int32, bounds_ref.shape, 1)
    bounds_ref[...] = jnp.where(lane == 0, first, after)
    rows_copy.wait()
    unit = normalize_rows(rows_ref[...])
    out_ref[...] = jnp.dot(moves, unit, preferred_element_type=jnp.float32).astype(jnp.bfloat16)


def partial_sums(queries, key_blocks, bounds, own, block_rows):
    totals, weighted = 0.0, 0.0
    first, after = bounds[:, 0:1], bounds[:, 1:2]
    for index, keys in enumerate(key_blocks):
        similar = lax.dot_general(
            queries, keys, (((1,), (1,)), ((), ())), preferred_element_type=jnp.float32
        )
        place = lax.rem(lax.broadcasted_iota(jnp.int32, similar.shape, 1), block_rows)
        allowed = (place >= first) & (place < after)
        if own and index == 0:
            allowed = allowed & (place != lax.broadcasted_iota(jnp.int32, similar.shape, 0))
        weights = jnp.where(allowed, jnp.exp(sharpness * (similar - 1.0)), 0.0)
        totals = totals + jnp.sum(weights, axis=1, keepdims=True)
        weighted = weighted + jnp.dot(
            weights.astype(jnp.bfloat16), keys, preferred_element_type=jnp.float32
        )
    return totals, weighted


LANES = 128


def gather_refs(refs):
    return [ref[...] for ref in refs]


def first_kernel(bounds_ref, own_ref, beside_ref, *refs):
    *key_refs, weighted_ref, totals_ref = refs
    queries = jnp.concatenate([own_ref[...], beside_ref[...]], axis=0)
    bounds = jnp.concatenate([bounds_ref[...]] * 2, axis=0)
    totals, weighted = partial_sums(queries, gather_refs(key_refs), bounds, True, own_ref.shape[0])
    weighted_ref[...] = weighted
    totals_ref[...] = jnp.broadcast_to(totals, totals_ref.shape)


def beside_kernel(so_far_ref, totals_so_far_ref, bounds_ref, beside_ref, *refs):
    *key_refs, out_ref = refs
    count = beside_ref.shape[0]
    keys = gather_refs(key_refs)
    totals, weighted = partial_sums(beside_ref[...], keys, bounds_ref[...], False, count)
    totals = totals + totals_so_far_ref[count:, 0:1]
    weighted = (weighted + so_far_ref[count:, :]).astype(jnp.bfloat16)
    columns = weighted.shape[1] // LANES
    for index in range(columns):
        out_ref[index * count : (index + 1) * count, :] = weighted[
            :, index * LANES : (index + 1) * LANES
        ]
    extra = out_ref.shape[0] - columns * count
    totals = jnp.concatenate([as_row(totals), jnp.zeros((1, LANES - count), jnp.float32)], axis=1)
    high = totals.astype(jnp.bfloat16).astype(jnp.float32)
    row = lax.broadcasted_iota(jnp.int32, (extra, LANES), 0)
    out_ref[columns * count :, :] = jnp.where(row == 0, high, totals - high).astype(jnp.bfloat16)


def own_kernel(so_far_ref, totals_so_far_ref, bounds_ref, own_ref, *refs):
    *key_refs, weighted_ref, totals_ref = refs
    count = own_ref.shape[0]
    keys = gather_refs(key_refs)
    totals, weighted = partial_sums(own_ref[...], keys, bounds_ref[...], False, count)
    weighted_ref[...] = weighted + so_far_ref[:count, :]
    totals_ref[...] = as_row(totals + totals_so_far_ref[:count, 0:1])


def finish_kernel(moves_ref, weighted_ref, totals_ref, back_ref, neighbour_hbm, score_hbm, neighbour_ref, score_ref, sems):
    count, features = neighbour_ref.shape
    columns = features // LANES
    back = [
        back_ref[index * count : (index + 1) * count, :].astype(jnp.float32)
        for index in range(columns)
    ]
    weighted = weighted_ref[...] + jnp.concatenate(back, axis=1)
    normed = (
        weighted * lax.rsqrt(jnp.mean(weighted * weighted, axis=-1, keepdims=True) + epsilon)
    ).astype(jnp.bfloat16)
    moves = moves_ref[...]
    neighbour_ref[...] = lax.dot_general(
        moves, normed, (((0,), (0,)), ((), ())), preferred_element_type=jnp.float32
    ).astype(jnp.bfloat16)
    neighbour_copy = pltpu.make_async_copy(neighbour_ref, neighbour_hbm, sems.at[0])
    neighbour_copy.start()
    pair = back_ref[columns * count :, :].astype(jnp.float32)
    totals = totals_ref[...] + (pair[0:1, :count] + pair[1:2, :count])
    scores = jnp.sum(moves.astype(jnp.float32) * as_column(jnp.log(totals)), axis=0, keepdims=True)
    score_ref[...] = scores.astype(jnp.bfloat16).reshape(count)
    score_copy = pltpu.make_async_copy(score_ref, score_hbm, sems.at[1])
    score_copy.start()
    neighbour_copy.wait()
    score_copy.wait()


EXTRA = 16
CORE, ACROSS, NEAR, FAR = 1, 2, 4, 8
GRID = 16


def gathered_body(embeddings, cluster_id):
    rows_dev, features = embeddings.shape
    vmem = pl.BlockSpec(memory_space=pltpu.VMEM)
    stored = pl.BlockSpec(memory_space=pltpu.HBM)

    def swap(value, bits):
        return lax.ppermute(value, "blk", [(device, device ^ bits) for device in range(GRID)])

    def block(kind, *shape):
        return jax.ShapeDtypeStruct(shape, kind)

    def kernel(body, name, out_shape, *inputs, specs=vmem, out_specs=vmem, scratch=()):
        return pl.pallas_call(
            body,
            out_shape=out_shape,
            in_specs=[specs] * len(inputs),
            out_specs=(out_specs,) * len(out_shape),
            scratch_shapes=scratch,
            compiler_params=pltpu.CompilerParams(vmem_limit_bytes=32 * 1024 * 1024),
            name=name,
        )(*inputs)

    rows = block(jnp.bfloat16, rows_dev, features)
    own, moves, bounds = kernel(
        arrange_kernel,
        "arrange",
        (rows, block(jnp.bfloat16, rows_dev, rows_dev), block(jnp.int32, rows_dev, LANES)),
        pltpu.with_memory_space_constraint(cluster_id, pltpu.HBM),
        pltpu.with_memory_space_constraint(embeddings, pltpu.HBM),
        specs=stored,
        scratch=(
            pltpu.VMEM((rows_dev,), jnp.int32),
            pltpu.VMEM((rows_dev, features), jnp.bfloat16),
            pltpu.SemaphoreType.DMA((2,)),
        ),
    )

    far, farther, near, beside, mate = lax.optimization_barrier(
        tuple(swap(own, bits) for bits in (FAR, FAR | NEAR, NEAR, ACROSS, CORE))
    )
    mates = swap(jnp.concatenate([near, far, farther], axis=0), CORE)
    weighted, totals = kernel(
        first_kernel,
        "first",
        (block(jnp.float32, 2 * rows_dev, features), block(jnp.float32, 2 * rows_dev, LANES)),
        *(bounds, own, beside),
        *(own, mate, near, far, farther),
    )
    (partial,) = kernel(
        beside_kernel,
        "beside",
        (block(jnp.bfloat16, rows_dev * features // LANES + EXTRA, LANES),),
        *(weighted, totals, bounds, beside, mates),
    )
    back = swap(partial, ACROSS)
    weighted, totals = kernel(
        own_kernel,
        "own",
        (block(jnp.float32, rows_dev, features), block(jnp.float32, 1, rows_dev)),
        *(weighted, totals, bounds, own, mates),
    )
    return tuple(
        kernel(
            finish_kernel,
            "finish",
            (rows, block(jnp.bfloat16, rows_dev)),
            *(moves, weighted, totals, back),
            out_specs=stored,
            scratch=(
                pltpu.VMEM((rows_dev, features), jnp.bfloat16),
                pltpu.VMEM((rows_dev,), jnp.bfloat16),
                pltpu.SemaphoreType.DMA((2,)),
            ),
        )
    )


def from_behind(value, axis, steps):
    count = lax.axis_size(axis)
    initial, last = (max(0, -steps), min(count, count - steps))
    return lax.ppermute(value, axis, [(source, source + steps) for source in range(initial, last)])


def pair_terms(queries, visiting, allowed):
    similar = jnp.dot(queries, visiting.T, preferred_element_type=jnp.float32)
    return jnp.where(allowed, jnp.exp(sharpness * (similar - 1.0)), jnp.zeros_like(similar))


def finish(weighted, totals):
    normed = (
        weighted * lax.rsqrt(jnp.mean(weighted * weighted, axis=-1, keepdims=True) + epsilon)
    ).astype(jnp.bfloat16)
    return (normed, jnp.log(totals).astype(jnp.bfloat16))


def collected_body(embeddings, cluster_id):
    rows_dev, features = embeddings.shape
    devices = lax.axis_size("blk")
    per_peer = rows_dev // devices
    clusters = devices // 4
    unit_rows = normalize_rows(embeddings)
    labels = jnp.arange(clusters, dtype=jnp.int32)
    counts = jnp.sum((cluster_id[:, None] == labels[None, :]).astype(jnp.int32), axis=0)
    group_ends = jnp.cumsum(counts // per_peer)

    def owner_cluster(device):
        in_range = (device >= 0) & (device < devices)
        return jnp.where(in_range, jnp.sum((device >= group_ends).astype(jnp.int32)), -1)

    position = jnp.arange(rows_dev, dtype=jnp.int32)
    arrange_order = jnp.argsort(cluster_id * rows_dev + position)
    inverse = jnp.argsort(arrange_order)
    arranged = unit_rows[arrange_order].reshape(devices, per_peer, features)
    held_rows = lax.all_to_all(arranged, "blk", split_axis=0, concat_axis=0, tiled=True).reshape(
        rows_dev, features
    )
    self_index = lax.axis_index("blk")
    mine = owner_cluster(self_index)
    weights = pair_terms(held_rows, held_rows, position[:, None] != position[None, :])
    totals = jnp.sum(weights, axis=1)
    weighted = jnp.dot(weights.astype(jnp.bfloat16), held_rows, preferred_element_type=jnp.float32)
    from_lower = held_rows
    from_upper = held_rows
    for distance in range(1, U_MAX):
        from_lower = from_behind(from_lower, "blk", 1)
        from_upper = from_behind(from_upper, "blk", -1)
        for visiting, source in (
            (from_lower, self_index - distance),
            (from_upper, self_index + distance),
        ):
            weights = pair_terms(held_rows, visiting, owner_cluster(source) == mine)
            totals = totals + jnp.sum(weights, axis=1)
            weighted = weighted + jnp.dot(
                weights.astype(jnp.bfloat16), visiting, preferred_element_type=jnp.float32
            )
    normed, scores = finish(weighted, totals)
    returned_rows, returned_scores = (
        lax.all_to_all(
            normed.reshape(devices, per_peer, features),
            "blk",
            split_axis=0,
            concat_axis=0,
            tiled=True,
        ),
        lax.all_to_all(
            scores.reshape(devices, per_peer), "blk", split_axis=0, concat_axis=0, tiled=True
        ),
    )
    neighbour = returned_rows.reshape(rows_dev, features)[inverse]
    dup_score = returned_scores.reshape(rows_dev)[inverse]
    return (neighbour, dup_score)


def solution(mesh):
    placed = (P(("groups", "blk"), None), P(("groups", "blk")))
    devices = mesh.shape["blk"]

    def body(embeddings, cluster_id):
        gathered = embeddings.size * embeddings.dtype.itemsize * devices
        fits = gathered <= GATHER_LIMIT and devices == GRID
        plan = gathered_body if fits else collected_body
        return plan(embeddings, cluster_id)

    return jax.shard_map(
        body,
        mesh=mesh,
        in_specs=placed,
        out_specs=(P(("groups", "blk"), None), P(("groups", "blk"))),
        check_vma=False,
    )
```

```python
import functools

import jax
import jax.numpy as jnp
from jax import lax
from jax.experimental import pallas as pl
from jax.experimental.pallas import tpu as pltpu
from jax.sharding import PartitionSpec as P

U_MAX = 8
GATHER_LIMIT = 4 * 1024 * 1024


sharpness = 10.0
epsilon = 1e-06


def normalize_rows(values):
    widened = values.astype(jnp.float32)
    return (
        widened
        * lax.rsqrt(jnp.mean(widened * widened, axis=-1, keepdims=True) + epsilon)
        * widened.shape[-1] ** (-0.5)
    ).astype(jnp.bfloat16)


def as_column(row):
    count = row.shape[1]
    across = lax.broadcasted_iota(jnp.int32, (count, count), 1)
    down = lax.broadcasted_iota(jnp.int32, (count, count), 0)
    return jnp.sum(jnp.where(across == down, row, jnp.zeros_like(row)), axis=1, keepdims=True)


def as_row(column):
    count = column.shape[0]
    across = lax.broadcasted_iota(jnp.int32, (count, count), 1)
    down = lax.broadcasted_iota(jnp.int32, (count, count), 0)
    return jnp.sum(jnp.where(across == down, column, jnp.zeros_like(column)), axis=0, keepdims=True)


def arrange_kernel(ids_hbm, rows_hbm, out_ref, moves_ref, bounds_ref, ids_ref, rows_ref, sems):
    rows_copy = pltpu.make_async_copy(rows_hbm, rows_ref, sems.at[0])
    ids_copy = pltpu.make_async_copy(ids_hbm, ids_ref, sems.at[1])
    rows_copy.start()
    ids_copy.start()
    count = rows_ref.shape[0]
    ids_copy.wait()
    ids_row = ids_ref[...].reshape(1, count)
    ids_column = as_column(ids_row)
    across = lax.broadcasted_iota(jnp.int32, (count, count), 1)
    down = lax.broadcasted_iota(jnp.int32, (count, count), 0)
    before = (ids_column < ids_row) | ((ids_column == ids_row) & (down < across))
    rank_row = jnp.sum(before.astype(jnp.int32), axis=0, keepdims=True)
    moved = down == rank_row
    moves = moved.astype(jnp.bfloat16)
    moves_ref[...] = moves
    label = jnp.sum(jnp.where(moved, ids_row, 0), axis=1, keepdims=True)
    first = jnp.sum((ids_row < label).astype(jnp.int32), axis=1, keepdims=True)
    after = jnp.sum((ids_row <= label).astype(jnp.int32), axis=1, keepdims=True)
    lane = lax.broadcasted_iota(jnp.int32, bounds_ref.shape, 1)
    bounds_ref[...] = jnp.where(lane == 0, first, after)
    rows_copy.wait()
    unit = normalize_rows(rows_ref[...])
    out_ref[...] = jnp.dot(moves, unit, preferred_element_type=jnp.float32).astype(jnp.bfloat16)


def partial_sums(queries, key_blocks, bounds, own, block_rows):
    totals, weighted = 0.0, 0.0
    first, after = bounds[:, 0:1], bounds[:, 1:2]
    for index, keys in enumerate(key_blocks):
        similar = lax.dot_general(
            queries, keys, (((1,), (1,)), ((), ())), preferred_element_type=jnp.float32
        )
        place = lax.rem(lax.broadcasted_iota(jnp.int32, similar.shape, 1), block_rows)
        allowed = (place >= first) & (place < after)
        if own and index == 0:
            allowed = allowed & (place != lax.broadcasted_iota(jnp.int32, similar.shape, 0))
        weights = jnp.where(allowed, jnp.exp(sharpness * (similar - 1.0)), 0.0)
        totals = totals + jnp.sum(weights, axis=1, keepdims=True)
        weighted = weighted + jnp.dot(
            weights.astype(jnp.bfloat16), keys, preferred_element_type=jnp.float32
        )
    return totals, weighted


LANES = 128


def gather_refs(refs):
    return [ref[...] for ref in refs]


def first_kernel(bounds_ref, own_ref, beside_ref, *refs):
    *key_refs, weighted_ref, totals_ref = refs
    queries = jnp.concatenate([own_ref[...], beside_ref[...]], axis=0)
    bounds = jnp.concatenate([bounds_ref[...]] * 2, axis=0)
    totals, weighted = partial_sums(queries, gather_refs(key_refs), bounds, True, own_ref.shape[0])
    weighted_ref[...] = weighted
    totals_ref[...] = jnp.broadcast_to(totals, totals_ref.shape)


def beside_kernel(turn, so_far_ref, totals_so_far_ref, bounds_ref, beside_ref, *refs):
    out_ref = refs[-1]

    @pl.when((lax.axis_index("blk") & ACROSS) == turn * ACROSS)
    def _():
        beside_sums(so_far_ref, totals_so_far_ref, bounds_ref, beside_ref, refs[0], out_ref)


def beside_sums(so_far_ref, totals_so_far_ref, bounds_ref, beside_ref, *refs):
    *key_refs, out_ref = refs
    count = beside_ref.shape[0]
    keys = gather_refs(key_refs)
    totals, weighted = partial_sums(beside_ref[...], keys, bounds_ref[...], False, count)
    totals = totals + totals_so_far_ref[count:, 0:1]
    weighted = (weighted + so_far_ref[count:, :]).astype(jnp.bfloat16)
    columns = weighted.shape[1] // LANES
    for index in range(columns):
        out_ref[index * count : (index + 1) * count, :] = weighted[
            :, index * LANES : (index + 1) * LANES
        ]
    extra = out_ref.shape[0] - columns * count
    totals = jnp.concatenate([as_row(totals), jnp.zeros((1, LANES - count), jnp.float32)], axis=1)
    high = totals.astype(jnp.bfloat16).astype(jnp.float32)
    row = lax.broadcasted_iota(jnp.int32, (extra, LANES), 0)
    out_ref[columns * count :, :] = jnp.where(row == 0, high, totals - high).astype(jnp.bfloat16)


def own_kernel(so_far_ref, totals_so_far_ref, bounds_ref, own_ref, *refs):
    *key_refs, weighted_ref, totals_ref = refs
    count = own_ref.shape[0]
    keys = gather_refs(key_refs)
    totals, weighted = partial_sums(own_ref[...], keys, bounds_ref[...], False, count)
    weighted_ref[...] = weighted + so_far_ref[:count, :]
    totals_ref[...] = as_row(totals + totals_so_far_ref[:count, 0:1])


def finish_kernel(
    moves_ref,
    weighted_ref,
    totals_ref,
    to_second_ref,
    to_first_ref,
    neighbour_hbm,
    score_hbm,
    neighbour_ref,
    score_ref,
    sems,
):
    count, features = neighbour_ref.shape
    received = (to_first_ref[...] + to_second_ref[...]).astype(jnp.float32)
    columns = features // LANES
    back = [
        received[index * count : (index + 1) * count, :] for index in range(columns)
    ]
    weighted = weighted_ref[...] + jnp.concatenate(back, axis=1)
    normed = (
        weighted * lax.rsqrt(jnp.mean(weighted * weighted, axis=-1, keepdims=True) + epsilon)
    ).astype(jnp.bfloat16)
    moves = moves_ref[...]
    neighbour_ref[...] = lax.dot_general(
        moves, normed, (((0,), (0,)), ((), ())), preferred_element_type=jnp.float32
    ).astype(jnp.bfloat16)
    neighbour_copy = pltpu.make_async_copy(neighbour_ref, neighbour_hbm, sems.at[0])
    neighbour_copy.start()
    pair = received[columns * count :, :]
    totals = totals_ref[...] + (pair[0:1, :count] + pair[1:2, :count])
    scores = jnp.sum(moves.astype(jnp.float32) * as_column(jnp.log(totals)), axis=0, keepdims=True)
    score_ref[...] = scores.astype(jnp.bfloat16).reshape(count)
    score_copy = pltpu.make_async_copy(score_ref, score_hbm, sems.at[1])
    score_copy.start()
    neighbour_copy.wait()
    score_copy.wait()


EXTRA = 16
CORE, ACROSS, NEAR, FAR = 1, 2, 4, 8
GRID = 16


def gathered_body(embeddings, cluster_id):
    rows_dev, features = embeddings.shape
    vmem = pl.BlockSpec(memory_space=pltpu.VMEM)
    stored = pl.BlockSpec(memory_space=pltpu.HBM)

    def swap(value, bits):
        return lax.ppermute(value, "blk", [(device, device ^ bits) for device in range(GRID)])

    def block(kind, *shape):
        return jax.ShapeDtypeStruct(shape, kind)

    def kernel(body, name, out_shape, *inputs, specs=vmem, out_specs=vmem, scratch=()):
        return pl.pallas_call(
            body,
            out_shape=out_shape,
            in_specs=[specs] * len(inputs),
            out_specs=(out_specs,) * len(out_shape),
            scratch_shapes=scratch,
            compiler_params=pltpu.CompilerParams(vmem_limit_bytes=32 * 1024 * 1024),
            name=name,
        )(*inputs)

    rows = block(jnp.bfloat16, rows_dev, features)
    own, moves, bounds = kernel(
        arrange_kernel,
        "arrange",
        (rows, block(jnp.bfloat16, rows_dev, rows_dev), block(jnp.int32, rows_dev, LANES)),
        pltpu.with_memory_space_constraint(cluster_id, pltpu.HBM),
        pltpu.with_memory_space_constraint(embeddings, pltpu.HBM),
        specs=stored,
        scratch=(
            pltpu.VMEM((rows_dev,), jnp.int32),
            pltpu.VMEM((rows_dev, features), jnp.bfloat16),
            pltpu.SemaphoreType.DMA((2,)),
        ),
    )

    far, farther, near, beside, mate = lax.optimization_barrier(
        tuple(swap(own, bits) for bits in (FAR, FAR | NEAR, NEAR, ACROSS, CORE))
    )
    mates = swap(jnp.concatenate([near, far, farther], axis=0), CORE)
    weighted, totals = kernel(
        first_kernel,
        "first",
        (block(jnp.float32, 2 * rows_dev, features), block(jnp.float32, 2 * rows_dev, LANES)),
        *(bounds, own, beside),
        *(own, mate, near, far, farther),
    )
    backs, earlier = [], ()
    for turn in (1, 0):
        (partial,) = kernel(
            functools.partial(beside_kernel, turn),
            f"beside_{turn}",
            (block(jnp.bfloat16, rows_dev * features // LANES + EXTRA, LANES),),
            *(weighted, totals, bounds, beside, mates, *earlier),
        )
        earlier = (partial,)
        senders = [device for device in range(GRID) if (device & ACROSS) == turn * ACROSS]
        backs.append(
            lax.ppermute(partial, "blk", [(device, device ^ ACROSS) for device in senders])
        )
    first_in_x = (lax.axis_index("blk") & ACROSS) == 0
    backs[0] = jnp.where(first_in_x, backs[0], jnp.zeros_like(backs[0]))
    weighted, totals = kernel(
        own_kernel,
        "own",
        (block(jnp.float32, rows_dev, features), block(jnp.float32, 1, rows_dev)),
        *(weighted, totals, bounds, own, mates),
    )
    return tuple(
        kernel(
            finish_kernel,
            "finish",
            (rows, block(jnp.bfloat16, rows_dev)),
            *(moves, weighted, totals, *reversed(backs)),
            out_specs=stored,
            scratch=(
                pltpu.VMEM((rows_dev, features), jnp.bfloat16),
                pltpu.VMEM((rows_dev,), jnp.bfloat16),
                pltpu.SemaphoreType.DMA((2,)),
            ),
        )
    )


def from_behind(value, axis, steps):
    count = lax.axis_size(axis)
    initial, last = (max(0, -steps), min(count, count - steps))
    return lax.ppermute(value, axis, [(source, source + steps) for source in range(initial, last)])


def pair_terms(queries, visiting, allowed):
    similar = jnp.dot(queries, visiting.T, preferred_element_type=jnp.float32)
    return jnp.where(allowed, jnp.exp(sharpness * (similar - 1.0)), jnp.zeros_like(similar))


def finish(weighted, totals):
    normed = (
        weighted * lax.rsqrt(jnp.mean(weighted * weighted, axis=-1, keepdims=True) + epsilon)
    ).astype(jnp.bfloat16)
    return (normed, jnp.log(totals).astype(jnp.bfloat16))


def collected_body(embeddings, cluster_id):
    rows_dev, features = embeddings.shape
    devices = lax.axis_size("blk")
    per_peer = rows_dev // devices
    clusters = devices // 4
    unit_rows = normalize_rows(embeddings)
    labels = jnp.arange(clusters, dtype=jnp.int32)
    counts = jnp.sum((cluster_id[:, None] == labels[None, :]).astype(jnp.int32), axis=0)
    group_ends = jnp.cumsum(counts // per_peer)

    def owner_cluster(device):
        in_range = (device >= 0) & (device < devices)
        return jnp.where(in_range, jnp.sum((device >= group_ends).astype(jnp.int32)), -1)

    position = jnp.arange(rows_dev, dtype=jnp.int32)
    arrange_order = jnp.argsort(cluster_id * rows_dev + position)
    inverse = jnp.argsort(arrange_order)
    arranged = unit_rows[arrange_order].reshape(devices, per_peer, features)
    held_rows = lax.all_to_all(arranged, "blk", split_axis=0, concat_axis=0, tiled=True).reshape(
        rows_dev, features
    )
    self_index = lax.axis_index("blk")
    mine = owner_cluster(self_index)
    weights = pair_terms(held_rows, held_rows, position[:, None] != position[None, :])
    totals = jnp.sum(weights, axis=1)
    weighted = jnp.dot(weights.astype(jnp.bfloat16), held_rows, preferred_element_type=jnp.float32)
    from_lower = held_rows
    from_upper = held_rows
    for distance in range(1, U_MAX):
        from_lower = from_behind(from_lower, "blk", 1)
        from_upper = from_behind(from_upper, "blk", -1)
        for visiting, source in (
            (from_lower, self_index - distance),
            (from_upper, self_index + distance),
        ):
            weights = pair_terms(held_rows, visiting, owner_cluster(source) == mine)
            totals = totals + jnp.sum(weights, axis=1)
            weighted = weighted + jnp.dot(
                weights.astype(jnp.bfloat16), visiting, preferred_element_type=jnp.float32
            )
    normed, scores = finish(weighted, totals)
    returned_rows, returned_scores = (
        lax.all_to_all(
            normed.reshape(devices, per_peer, features),
            "blk",
            split_axis=0,
            concat_axis=0,
            tiled=True,
        ),
        lax.all_to_all(
            scores.reshape(devices, per_peer), "blk", split_axis=0, concat_axis=0, tiled=True
        ),
    )
    neighbour = returned_rows.reshape(rows_dev, features)[inverse]
    dup_score = returned_scores.reshape(rows_dev)[inverse]
    return (neighbour, dup_score)


def solution(mesh):
    placed = (P(("groups", "blk"), None), P(("groups", "blk")))
    devices = mesh.shape["blk"]

    def body(embeddings, cluster_id):
        gathered = embeddings.size * embeddings.dtype.itemsize * devices
        fits = gathered <= GATHER_LIMIT and devices == GRID
        plan = gathered_body if fits else collected_body
        return plan(embeddings, cluster_id)

    return jax.shard_map(
        body,
        mesh=mesh,
        in_specs=placed,
        out_specs=(P(("groups", "blk"), None), P(("groups", "blk"))),
        check_vma=False,
    )
```

```python
import jax
import jax.numpy as jnp
from jax import lax
from jax.experimental import pallas as pl
from jax.experimental.pallas import tpu as pltpu
from jax.sharding import PartitionSpec as P

U_MAX = 8
GATHER_LIMIT = 4 * 1024 * 1024


sharpness = 10.0
epsilon = 1e-06


def normalize_rows(values):
    widened = values.astype(jnp.float32)
    return (
        widened
        * lax.rsqrt(jnp.mean(widened * widened, axis=-1, keepdims=True) + epsilon)
        * widened.shape[-1] ** (-0.5)
    ).astype(jnp.bfloat16)


def as_column(row):
    count = row.shape[1]
    across = lax.broadcasted_iota(jnp.int32, (count, count), 1)
    down = lax.broadcasted_iota(jnp.int32, (count, count), 0)
    return jnp.sum(jnp.where(across == down, row, jnp.zeros_like(row)), axis=1, keepdims=True)


def as_row(column):
    count = column.shape[0]
    across = lax.broadcasted_iota(jnp.int32, (count, count), 1)
    down = lax.broadcasted_iota(jnp.int32, (count, count), 0)
    return jnp.sum(jnp.where(across == down, column, jnp.zeros_like(column)), axis=0, keepdims=True)


LANES = 128


def arrange_kernel(ids_hbm, rows_hbm, out_ref, moves_ref, ids_out_ref, ids_ref, rows_ref, sems):
    ids_copy = pltpu.make_async_copy(ids_hbm, ids_ref, sems.at[0])
    rows_copy = pltpu.make_async_copy(rows_hbm, rows_ref, sems.at[1])
    ids_copy.start()
    rows_copy.start()
    count = rows_ref.shape[0]
    ids_copy.wait()
    ids_row = ids_ref[...].reshape(1, count)
    ids_column = as_column(ids_row)
    across = lax.broadcasted_iota(jnp.int32, (count, count), 1)
    down = lax.broadcasted_iota(jnp.int32, (count, count), 0)
    before = (ids_column < ids_row) | ((ids_column == ids_row) & (down < across))
    rank_row = jnp.sum(before.astype(jnp.int32), axis=0, keepdims=True)
    moves = (down == rank_row).astype(jnp.bfloat16)
    rows_copy.wait()
    unit = normalize_rows(rows_ref[...])
    out_ref[...] = jnp.dot(moves, unit, preferred_element_type=jnp.float32).astype(jnp.bfloat16)
    moves_ref[...] = moves
    ids_out_ref[...] = ids_row


def partial_sums(queries, keys, bounds, own):
    count = bounds.shape[0]
    blocks = queries.shape[0] // count
    similar = lax.dot_general(
        queries, keys, (((1,), (1,)), ((), ())), preferred_element_type=jnp.float32
    )
    bounds = jnp.concatenate([bounds] * blocks, axis=0)
    key = lax.broadcasted_iota(jnp.int32, similar.shape, 1)
    place = lax.rem(key, count)
    allowed = (place >= bounds[:, 0:1]) & (place < bounds[:, 1:2])
    if own:
        query = lax.broadcasted_iota(jnp.int32, similar.shape, 0)
        allowed = allowed & ((key != query) | (key >= count))
    weights = jnp.where(allowed, jnp.exp(sharpness * (similar - 1.0)), 0.0)
    totals = jnp.sum(weights, axis=1, keepdims=True)
    return totals, jnp.dot(weights.astype(jnp.bfloat16), keys, preferred_element_type=jnp.float32)


def first_kernel(moves_ref, ids_ref, own_ref, beside_ref, *refs):
    *key_refs, weighted_ref, totals_ref, bounds_ref = refs
    ids = ids_ref[...]
    label = jnp.sum(jnp.where(moves_ref[...] > 0, ids, 0), axis=1, keepdims=True)
    first = jnp.sum((ids < label).astype(jnp.int32), axis=1, keepdims=True)
    after = jnp.sum((ids <= label).astype(jnp.int32), axis=1, keepdims=True)
    lane = lax.broadcasted_iota(jnp.int32, bounds_ref.shape, 1)
    bounds = jnp.where(lane == 0, first, after)
    bounds_ref[...] = bounds
    queries = jnp.concatenate([own_ref[...], beside_ref[...]], axis=0)
    keys = jnp.concatenate([ref[...] for ref in key_refs], axis=0)
    totals, weighted = partial_sums(queries, keys, bounds, True)
    weighted_ref[...] = weighted
    totals_ref[...] = jnp.broadcast_to(totals, totals_ref.shape)


def beside_kernel(so_far_ref, totals_so_far_ref, bounds_ref, beside_ref, keys_ref, out_ref):
    count = beside_ref.shape[0]
    totals, weighted = partial_sums(beside_ref[...], keys_ref[...], bounds_ref[...], False)
    weighted = (weighted + so_far_ref[count:, :]).astype(jnp.bfloat16)
    columns = weighted.shape[1] // LANES
    for index in range(columns):
        out_ref[index * count : (index + 1) * count, :] = weighted[
            :, index * LANES : (index + 1) * LANES
        ]
    totals = as_row(totals + totals_so_far_ref[count:, 0:1])
    totals = jnp.concatenate([totals, jnp.zeros((1, LANES - count), jnp.float32)], axis=1)
    high = totals.astype(jnp.bfloat16).astype(jnp.float32)
    row = lax.broadcasted_iota(jnp.int32, (EXTRA, LANES), 0)
    out_ref[columns * count :, :] = jnp.where(row == 0, high, totals - high).astype(jnp.bfloat16)


def own_kernel(so_far_ref, totals_so_far_ref, bounds_ref, own_ref, keys_ref, weighted_ref, totals_ref):
    count = own_ref.shape[0]
    totals, weighted = partial_sums(own_ref[...], keys_ref[...], bounds_ref[...], False)
    weighted_ref[...] = weighted + so_far_ref[:count, :]
    totals_ref[...] = as_row(totals + totals_so_far_ref[:count, 0:1])


def finish_kernel(
    moves_ref,
    weighted_ref,
    totals_ref,
    back_ref,
    neighbour_hbm,
    score_hbm,
    neighbour_ref,
    score_ref,
    sems,
):
    count, features = neighbour_ref.shape
    columns = features // LANES
    back = [
        back_ref[index * count : (index + 1) * count, :].astype(jnp.float32)
        for index in range(columns)
    ]
    weighted = weighted_ref[...] + jnp.concatenate(back, axis=1)
    normed = (
        weighted * lax.rsqrt(jnp.mean(weighted * weighted, axis=-1, keepdims=True) + epsilon)
    ).astype(jnp.bfloat16)
    moves = moves_ref[...]
    copies = []
    for half in range(2):
        part = slice(half * features // 2, (half + 1) * features // 2)
        neighbour_ref[:, part] = lax.dot_general(
            moves, normed[:, part], (((0,), (0,)), ((), ())), preferred_element_type=jnp.float32
        ).astype(jnp.bfloat16)
        copies.append(
            pltpu.make_async_copy(
                neighbour_ref.at[:, part], neighbour_hbm.at[:, part], sems.at[half]
            )
        )
        copies[-1].start()
    pair = back_ref[columns * count :, :].astype(jnp.float32)
    totals = totals_ref[...] + (pair[0:1, :count] + pair[1:2, :count])
    scores = jnp.sum(moves.astype(jnp.float32) * as_column(jnp.log(totals)), axis=0, keepdims=True)
    score_ref[...] = scores.astype(jnp.bfloat16).reshape(count)
    copies.append(pltpu.make_async_copy(score_ref, score_hbm, sems.at[2]))
    copies[-1].start()
    for copy in copies:
        copy.wait()


EXTRA = 16
CORE, ACROSS, NEAR, FAR = 1, 2, 4, 8
GRID = 16


def gathered_body(embeddings, cluster_id):
    rows_dev, features = embeddings.shape
    vmem = pl.BlockSpec(memory_space=pltpu.VMEM)
    stored = pl.BlockSpec(memory_space=pltpu.HBM)

    def swap(value, bits):
        return lax.ppermute(value, "blk", [(device, device ^ bits) for device in range(GRID)])

    def block(kind, *shape):
        return jax.ShapeDtypeStruct(shape, kind)

    def kernel(body, name, out_shape, *inputs, specs=vmem, out_specs=vmem, scratch=()):
        return pl.pallas_call(
            body,
            out_shape=out_shape,
            in_specs=[specs] * len(inputs),
            out_specs=(out_specs,) * len(out_shape),
            scratch_shapes=scratch,
            compiler_params=pltpu.CompilerParams(vmem_limit_bytes=32 * 1024 * 1024),
            name=name,
        )(*inputs)

    rows = block(jnp.bfloat16, rows_dev, features)
    own, moves, ids = kernel(
        arrange_kernel,
        "arrange",
        (rows, block(jnp.bfloat16, rows_dev, rows_dev), block(jnp.int32, 1, rows_dev)),
        pltpu.with_memory_space_constraint(cluster_id, pltpu.HBM),
        pltpu.with_memory_space_constraint(embeddings, pltpu.HBM),
        specs=stored,
        scratch=(
            pltpu.VMEM((rows_dev,), jnp.int32),
            pltpu.VMEM((rows_dev, features), jnp.bfloat16),
            pltpu.SemaphoreType.DMA((2,)),
        ),
    )

    far, farther, near, beside, mate = lax.optimization_barrier(
        tuple(swap(own, bits) for bits in (FAR, FAR | NEAR, NEAR, ACROSS, CORE))
    )
    mates = swap(jnp.concatenate([near, far, farther], axis=0), CORE)
    *so_far, bounds = kernel(
        first_kernel,
        "first",
        (
            block(jnp.float32, 2 * rows_dev, features),
            block(jnp.float32, 2 * rows_dev, LANES),
            block(jnp.int32, rows_dev, LANES),
        ),
        *(moves, ids, own, beside),
        *(own, mate, near, far, farther),
    )
    (partial,) = kernel(
        beside_kernel,
        "beside",
        (block(jnp.bfloat16, rows_dev * features // LANES + EXTRA, LANES),),
        *(*so_far, bounds, beside, mates),
    )
    back = swap(partial, ACROSS)
    weighted, totals = kernel(
        own_kernel,
        "own",
        (block(jnp.float32, rows_dev, features), block(jnp.float32, 1, rows_dev)),
        *(*so_far, bounds, own, mates),
    )
    return tuple(
        kernel(
            finish_kernel,
            "finish",
            (rows, block(jnp.bfloat16, rows_dev)),
            *(moves, weighted, totals, back),
            out_specs=stored,
            scratch=(
                pltpu.VMEM((rows_dev, features), jnp.bfloat16),
                pltpu.VMEM((rows_dev,), jnp.bfloat16),
                pltpu.SemaphoreType.DMA((3,)),
            ),
        )
    )


def from_behind(value, axis, steps):
    count = lax.axis_size(axis)
    initial, last = (max(0, -steps), min(count, count - steps))
    return lax.ppermute(value, axis, [(source, source + steps) for source in range(initial, last)])


def pair_terms(queries, visiting, allowed):
    similar = jnp.dot(queries, visiting.T, preferred_element_type=jnp.float32)
    return jnp.where(allowed, jnp.exp(sharpness * (similar - 1.0)), jnp.zeros_like(similar))


def finish(weighted, totals):
    normed = (
        weighted * lax.rsqrt(jnp.mean(weighted * weighted, axis=-1, keepdims=True) + epsilon)
    ).astype(jnp.bfloat16)
    return (normed, jnp.log(totals).astype(jnp.bfloat16))


def collected_body(embeddings, cluster_id):
    rows_dev, features = embeddings.shape
    devices = lax.axis_size("blk")
    per_peer = rows_dev // devices
    clusters = devices // 4
    unit_rows = normalize_rows(embeddings)
    labels = jnp.arange(clusters, dtype=jnp.int32)
    counts = jnp.sum((cluster_id[:, None] == labels[None, :]).astype(jnp.int32), axis=0)
    group_ends = jnp.cumsum(counts // per_peer)

    def owner_cluster(device):
        in_range = (device >= 0) & (device < devices)
        return jnp.where(in_range, jnp.sum((device >= group_ends).astype(jnp.int32)), -1)

    position = jnp.arange(rows_dev, dtype=jnp.int32)
    arrange_order = jnp.argsort(cluster_id * rows_dev + position)
    inverse = jnp.argsort(arrange_order)
    arranged = unit_rows[arrange_order].reshape(devices, per_peer, features)
    held_rows = lax.all_to_all(arranged, "blk", split_axis=0, concat_axis=0, tiled=True).reshape(
        rows_dev, features
    )
    self_index = lax.axis_index("blk")
    mine = owner_cluster(self_index)
    weights = pair_terms(held_rows, held_rows, position[:, None] != position[None, :])
    totals = jnp.sum(weights, axis=1)
    weighted = jnp.dot(weights.astype(jnp.bfloat16), held_rows, preferred_element_type=jnp.float32)
    from_lower = held_rows
    from_upper = held_rows
    for distance in range(1, U_MAX):
        from_lower = from_behind(from_lower, "blk", 1)
        from_upper = from_behind(from_upper, "blk", -1)
        for visiting, source in (
            (from_lower, self_index - distance),
            (from_upper, self_index + distance),
        ):
            weights = pair_terms(held_rows, visiting, owner_cluster(source) == mine)
            totals = totals + jnp.sum(weights, axis=1)
            weighted = weighted + jnp.dot(
                weights.astype(jnp.bfloat16), visiting, preferred_element_type=jnp.float32
            )
    normed, scores = finish(weighted, totals)
    returned_rows, returned_scores = (
        lax.all_to_all(
            normed.reshape(devices, per_peer, features),
            "blk",
            split_axis=0,
            concat_axis=0,
            tiled=True,
        ),
        lax.all_to_all(
            scores.reshape(devices, per_peer), "blk", split_axis=0, concat_axis=0, tiled=True
        ),
    )
    neighbour = returned_rows.reshape(rows_dev, features)[inverse]
    dup_score = returned_scores.reshape(rows_dev)[inverse]
    return (neighbour, dup_score)


def solution(mesh):
    placed = (P(("groups", "blk"), None), P(("groups", "blk")))
    devices = mesh.shape["blk"]

    def body(embeddings, cluster_id):
        gathered = embeddings.size * embeddings.dtype.itemsize * devices
        fits = gathered <= GATHER_LIMIT and devices == GRID
        plan = gathered_body if fits else collected_body
        return plan(embeddings, cluster_id)

    return jax.shard_map(
        body,
        mesh=mesh,
        in_specs=placed,
        out_specs=(P(("groups", "blk"), None), P(("groups", "blk"))),
        check_vma=False,
    )
```

```python
import jax
import jax.numpy as jnp
from jax import lax
from jax.experimental import pallas as pl
from jax.experimental.pallas import tpu as pltpu
from jax.sharding import PartitionSpec as P

U_MAX = 8
GATHER_LIMIT = 4 * 1024 * 1024


sharpness = 10.0
epsilon = 1e-06


def normalize_rows(values):
    widened = values.astype(jnp.float32)
    return (
        widened
        * lax.rsqrt(jnp.mean(widened * widened, axis=-1, keepdims=True) + epsilon)
        * widened.shape[-1] ** (-0.5)
    ).astype(jnp.bfloat16)


def as_column(row):
    count = row.shape[1]
    across = lax.broadcasted_iota(jnp.int32, (count, count), 1)
    down = lax.broadcasted_iota(jnp.int32, (count, count), 0)
    return jnp.sum(jnp.where(across == down, row, jnp.zeros_like(row)), axis=1, keepdims=True)


def as_row(column):
    count = column.shape[0]
    across = lax.broadcasted_iota(jnp.int32, (count, count), 1)
    down = lax.broadcasted_iota(jnp.int32, (count, count), 0)
    return jnp.sum(jnp.where(across == down, column, jnp.zeros_like(column)), axis=0, keepdims=True)


LANES = 128


def arrange_kernel(ids_hbm, rows_hbm, out_ref, moves_ref, ids_out_ref, ids_ref, rows_ref, sems):
    ids_copy = pltpu.make_async_copy(ids_hbm, ids_ref, sems.at[0])
    rows_copy = pltpu.make_async_copy(rows_hbm, rows_ref, sems.at[1])
    ids_copy.start()
    rows_copy.start()
    count = rows_ref.shape[0]
    ids_copy.wait()
    ids_row = ids_ref[...].reshape(1, count)
    ids_column = as_column(ids_row)
    across = lax.broadcasted_iota(jnp.int32, (count, count), 1)
    down = lax.broadcasted_iota(jnp.int32, (count, count), 0)
    before = (ids_column < ids_row) | ((ids_column == ids_row) & (down < across))
    rank_row = jnp.sum(before.astype(jnp.int32), axis=0, keepdims=True)
    moves = (down == rank_row).astype(jnp.bfloat16)
    rows_copy.wait()
    unit = normalize_rows(rows_ref[...])
    out_ref[...] = jnp.dot(moves, unit, preferred_element_type=jnp.float32).astype(jnp.bfloat16)
    moves_ref[...] = moves
    ids_out_ref[...] = ids_row


def pack(out_ref, weighted, totals):
    count = weighted.shape[0]
    weighted = weighted.astype(jnp.bfloat16)
    columns = weighted.shape[1] // LANES
    for index in range(columns):
        out_ref[index * count : (index + 1) * count, :] = weighted[
            :, index * LANES : (index + 1) * LANES
        ]
    totals = as_row(totals)
    totals = jnp.concatenate([totals, jnp.zeros((1, LANES - count), jnp.float32)], axis=1)
    high = totals.astype(jnp.bfloat16).astype(jnp.float32)
    row = lax.broadcasted_iota(jnp.int32, (EXTRA, LANES), 0)
    out_ref[columns * count :, :] = jnp.where(row == 0, high, totals - high).astype(jnp.bfloat16)


def unpack(packed_ref, count):
    columns = packed_ref.shape[0] // count
    block = [
        packed_ref[index * count : (index + 1) * count, :].astype(jnp.float32)
        for index in range(columns)
    ]
    pair = packed_ref[columns * count :, :].astype(jnp.float32)
    return jnp.concatenate(block, axis=1), pair[0:1, :count] + pair[1:2, :count]


def partial_sums(queries, keys, bounds, own):
    count = bounds.shape[0]
    blocks = queries.shape[0] // count
    similar = lax.dot_general(
        queries, keys, (((1,), (1,)), ((), ())), preferred_element_type=jnp.float32
    )
    bounds = jnp.concatenate([bounds] * blocks, axis=0)
    key = lax.broadcasted_iota(jnp.int32, similar.shape, 1)
    place = lax.rem(key, count)
    allowed = (place >= bounds[:, 0:1]) & (place < bounds[:, 1:2])
    if own:
        query = lax.broadcasted_iota(jnp.int32, similar.shape, 0)
        allowed = allowed & ((key != query) | (key >= count))
    weights = jnp.where(allowed, jnp.exp(sharpness * (similar - 1.0)), 0.0)
    totals = jnp.sum(weights, axis=1, keepdims=True)
    return totals, jnp.dot(weights.astype(jnp.bfloat16), keys, preferred_element_type=jnp.float32)


def visitor_kernel(moves_ref, ids_ref, visitor_ref, own_ref, beside_ref, mates_ref, out_ref, bounds_ref):
    ids = ids_ref[...]
    label = jnp.sum(jnp.where(moves_ref[...] > 0, ids, 0), axis=1, keepdims=True)
    first = jnp.sum((ids < label).astype(jnp.int32), axis=1, keepdims=True)
    after = jnp.sum((ids <= label).astype(jnp.int32), axis=1, keepdims=True)
    lane = lax.broadcasted_iota(jnp.int32, bounds_ref.shape, 1)
    bounds = jnp.where(lane == 0, first, after)
    bounds_ref[...] = bounds
    keys = jnp.concatenate([own_ref[...], beside_ref[...], mates_ref[...]], axis=0)
    totals, weighted = partial_sums(visitor_ref[...], keys, bounds, False)
    pack(out_ref, weighted, totals)


def first_kernel(bounds_ref, own_ref, beside_ref, mates_ref, *refs):
    *key_refs, weighted_ref, totals_ref = refs
    own = own_ref[...]
    queries = jnp.concatenate([own, beside_ref[...]], axis=0)
    mate = mates_ref[: own.shape[0], :]
    keys = jnp.concatenate([own, mate, *(ref[...] for ref in key_refs)], axis=0)
    totals, weighted = partial_sums(queries, keys, bounds_ref[...], True)
    weighted_ref[...] = weighted
    totals_ref[...] = jnp.broadcast_to(totals, totals_ref.shape)


def beside_kernel(so_far_ref, totals_so_far_ref, bounds_ref, beside_ref, keys_ref, out_ref):
    count = beside_ref.shape[0]
    totals, weighted = partial_sums(beside_ref[...], keys_ref[...], bounds_ref[...], False)
    pack(out_ref, weighted + so_far_ref[count:, :], totals + totals_so_far_ref[count:, 0:1])


def own_kernel(so_far_ref, totals_so_far_ref, bounds_ref, own_ref, keys_ref, weighted_ref, totals_ref):
    count = own_ref.shape[0]
    totals, weighted = partial_sums(own_ref[...], keys_ref[...], bounds_ref[...], False)
    weighted_ref[...] = weighted + so_far_ref[:count, :]
    totals_ref[...] = as_row(totals + totals_so_far_ref[:count, 0:1])


def finish_kernel(moves_ref, weighted_ref, totals_ref, *refs):
    *back_refs, neighbour_hbm, score_hbm, neighbour_ref, score_ref, sems = refs
    count = neighbour_ref.shape[0]
    weighted, totals = weighted_ref[...], totals_ref[...]
    for back_ref in back_refs:
        back, back_totals = unpack(back_ref, count)
        weighted = weighted + back
        totals = totals + back_totals
    normed = (
        weighted * lax.rsqrt(jnp.mean(weighted * weighted, axis=-1, keepdims=True) + epsilon)
    ).astype(jnp.bfloat16)
    moves = moves_ref[...]
    neighbour_ref[...] = lax.dot_general(
        moves, normed, (((0,), (0,)), ((), ())), preferred_element_type=jnp.float32
    ).astype(jnp.bfloat16)
    neighbour_copy = pltpu.make_async_copy(neighbour_ref, neighbour_hbm, sems.at[0])
    neighbour_copy.start()
    scores = jnp.sum(moves.astype(jnp.float32) * as_column(jnp.log(totals)), axis=0, keepdims=True)
    score_ref[...] = scores.astype(jnp.bfloat16).reshape(count)
    score_copy = pltpu.make_async_copy(score_ref, score_hbm, sems.at[1])
    score_copy.start()
    neighbour_copy.wait()
    score_copy.wait()


EXTRA = 16
CORE, ACROSS, NEAR = 1, 2, 4
PLANE, GRID = 4, 16
NEXT = (3, 2, 0, 1)


def gathered_body(embeddings, cluster_id):
    rows_dev, features = embeddings.shape
    vmem = pl.BlockSpec(memory_space=pltpu.VMEM)
    stored = pl.BlockSpec(memory_space=pltpu.HBM)

    def swap(value, bits):
        return lax.ppermute(value, "blk", [(device, device ^ bits) for device in range(GRID)])

    def visit(value, home):
        pairs = [
            (device, NEXT[device // PLANE] * PLANE + device % PLANE) for device in range(GRID)
        ]
        return lax.ppermute(value, "blk", [pair[::-1] for pair in pairs] if home else pairs)

    def block(kind, *shape):
        return jax.ShapeDtypeStruct(shape, kind)

    def kernel(body, name, out_shape, *inputs, specs=vmem, out_specs=vmem, scratch=()):
        return pl.pallas_call(
            body,
            out_shape=out_shape,
            in_specs=[specs] * len(inputs),
            out_specs=(out_specs,) * len(out_shape),
            scratch_shapes=scratch,
            compiler_params=pltpu.CompilerParams(vmem_limit_bytes=32 * 1024 * 1024),
            name=name,
        )(*inputs)

    rows = block(jnp.bfloat16, rows_dev, features)
    own, moves, ids = kernel(
        arrange_kernel,
        "arrange",
        (rows, block(jnp.bfloat16, rows_dev, rows_dev), block(jnp.int32, 1, rows_dev)),
        pltpu.with_memory_space_constraint(cluster_id, pltpu.HBM),
        pltpu.with_memory_space_constraint(embeddings, pltpu.HBM),
        specs=stored,
        scratch=(
            pltpu.VMEM((rows_dev,), jnp.int32),
            pltpu.VMEM((rows_dev, features), jnp.bfloat16),
            pltpu.SemaphoreType.DMA((2,)),
        ),
    )

    packed = block(jnp.bfloat16, rows_dev * features // LANES + EXTRA, LANES)
    visitor = visit(own, home=False)
    beside = swap(own, ACROSS)
    near = swap(own, NEAR)
    mates = swap(jnp.concatenate([own, beside], axis=0), CORE)
    visitor, near = lax.optimization_barrier((visitor, near))
    later = swap(jnp.concatenate([near, visitor], axis=0), CORE)
    partial, bounds = kernel(
        visitor_kernel,
        "visitor",
        (packed, block(jnp.int32, rows_dev, LANES)),
        *(moves, ids, visitor, own, beside, mates),
    )
    back_home = visit(partial, home=True)
    so_far = kernel(
        first_kernel,
        "first",
        (block(jnp.float32, 2 * rows_dev, features), block(jnp.float32, 2 * rows_dev, LANES)),
        *(bounds, own, beside, mates, near, visitor),
    )
    (partial,) = kernel(beside_kernel, "beside", (packed,), *so_far, bounds, beside, later)
    back = swap(partial, ACROSS)
    weighted, totals = kernel(
        own_kernel,
        "own",
        (block(jnp.float32, rows_dev, features), block(jnp.float32, 1, rows_dev)),
        *(*so_far, bounds, own, later),
    )
    weighted, back_home = lax.optimization_barrier((weighted, back_home))
    return tuple(
        kernel(
            finish_kernel,
            "finish",
            (rows, block(jnp.bfloat16, rows_dev)),
            *(moves, weighted, totals, back, back_home),
            out_specs=stored,
            scratch=(
                pltpu.VMEM((rows_dev, features), jnp.bfloat16),
                pltpu.VMEM((rows_dev,), jnp.bfloat16),
                pltpu.SemaphoreType.DMA((2,)),
            ),
        )
    )


def from_behind(value, axis, steps):
    count = lax.axis_size(axis)
    initial, last = (max(0, -steps), min(count, count - steps))
    return lax.ppermute(value, axis, [(source, source + steps) for source in range(initial, last)])


def pair_terms(queries, visiting, allowed):
    similar = jnp.dot(queries, visiting.T, preferred_element_type=jnp.float32)
    return jnp.where(allowed, jnp.exp(sharpness * (similar - 1.0)), jnp.zeros_like(similar))


def finish(weighted, totals):
    normed = (
        weighted * lax.rsqrt(jnp.mean(weighted * weighted, axis=-1, keepdims=True) + epsilon)
    ).astype(jnp.bfloat16)
    return (normed, jnp.log(totals).astype(jnp.bfloat16))


def collected_body(embeddings, cluster_id):
    rows_dev, features = embeddings.shape
    devices = lax.axis_size("blk")
    per_peer = rows_dev // devices
    clusters = devices // 4
    unit_rows = normalize_rows(embeddings)
    labels = jnp.arange(clusters, dtype=jnp.int32)
    counts = jnp.sum((cluster_id[:, None] == labels[None, :]).astype(jnp.int32), axis=0)
    group_ends = jnp.cumsum(counts // per_peer)

    def owner_cluster(device):
        in_range = (device >= 0) & (device < devices)
        return jnp.where(in_range, jnp.sum((device >= group_ends).astype(jnp.int32)), -1)

    position = jnp.arange(rows_dev, dtype=jnp.int32)
    arrange_order = jnp.argsort(cluster_id * rows_dev + position)
    inverse = jnp.argsort(arrange_order)
    arranged = unit_rows[arrange_order].reshape(devices, per_peer, features)
    held_rows = lax.all_to_all(arranged, "blk", split_axis=0, concat_axis=0, tiled=True).reshape(
        rows_dev, features
    )
    self_index = lax.axis_index("blk")
    mine = owner_cluster(self_index)
    weights = pair_terms(held_rows, held_rows, position[:, None] != position[None, :])
    totals = jnp.sum(weights, axis=1)
    weighted = jnp.dot(weights.astype(jnp.bfloat16), held_rows, preferred_element_type=jnp.float32)
    from_lower = held_rows
    from_upper = held_rows
    for distance in range(1, U_MAX):
        from_lower = from_behind(from_lower, "blk", 1)
        from_upper = from_behind(from_upper, "blk", -1)
        for visiting, source in (
            (from_lower, self_index - distance),
            (from_upper, self_index + distance),
        ):
            weights = pair_terms(held_rows, visiting, owner_cluster(source) == mine)
            totals = totals + jnp.sum(weights, axis=1)
            weighted = weighted + jnp.dot(
                weights.astype(jnp.bfloat16), visiting, preferred_element_type=jnp.float32
            )
    normed, scores = finish(weighted, totals)
    returned_rows, returned_scores = (
        lax.all_to_all(
            normed.reshape(devices, per_peer, features),
            "blk",
            split_axis=0,
            concat_axis=0,
            tiled=True,
        ),
        lax.all_to_all(
            scores.reshape(devices, per_peer), "blk", split_axis=0, concat_axis=0, tiled=True
        ),
    )
    neighbour = returned_rows.reshape(rows_dev, features)[inverse]
    dup_score = returned_scores.reshape(rows_dev)[inverse]
    return (neighbour, dup_score)


def solution(mesh):
    placed = (P(("groups", "blk"), None), P(("groups", "blk")))
    devices = mesh.shape["blk"]

    def body(embeddings, cluster_id):
        gathered = embeddings.size * embeddings.dtype.itemsize * devices
        fits = gathered <= GATHER_LIMIT and devices == GRID
        plan = gathered_body if fits else collected_body
        return plan(embeddings, cluster_id)

    return jax.shard_map(
        body,
        mesh=mesh,
        in_specs=placed,
        out_specs=(P(("groups", "blk"), None), P(("groups", "blk"))),
        check_vma=False,
    )
```

```python
import jax
import jax.numpy as jnp
from jax import lax
from jax.experimental import pallas as pl
from jax.experimental.pallas import tpu as pltpu
from jax.sharding import PartitionSpec as P

U_MAX = 8
GATHER_LIMIT = 4 * 1024 * 1024


sharpness = 10.0
epsilon = 1e-06


def normalize_rows(values):
    widened = values.astype(jnp.float32)
    return (
        widened
        * lax.rsqrt(jnp.mean(widened * widened, axis=-1, keepdims=True) + epsilon)
        * widened.shape[-1] ** (-0.5)
    ).astype(jnp.bfloat16)


def as_column(row):
    count = row.shape[1]
    across = lax.broadcasted_iota(jnp.int32, (count, count), 1)
    down = lax.broadcasted_iota(jnp.int32, (count, count), 0)
    return jnp.sum(jnp.where(across == down, row, jnp.zeros_like(row)), axis=1, keepdims=True)


def as_row(column):
    count = column.shape[0]
    across = lax.broadcasted_iota(jnp.int32, (count, count), 1)
    down = lax.broadcasted_iota(jnp.int32, (count, count), 0)
    return jnp.sum(jnp.where(across == down, column, jnp.zeros_like(column)), axis=0, keepdims=True)


LANES = 128


def arrange_kernel(ids_hbm, rows_hbm, out_ref, moves_ref, ids_out_ref, ids_ref, rows_ref, sems):
    ids_copy = pltpu.make_async_copy(ids_hbm, ids_ref, sems.at[0])
    rows_copy = pltpu.make_async_copy(rows_hbm, rows_ref, sems.at[1])
    ids_copy.start()
    rows_copy.start()
    count = rows_ref.shape[0]
    ids_copy.wait()
    ids_row = ids_ref[...].reshape(1, count)
    ids_column = as_column(ids_row)
    across = lax.broadcasted_iota(jnp.int32, (count, count), 1)
    down = lax.broadcasted_iota(jnp.int32, (count, count), 0)
    before = (ids_column < ids_row) | ((ids_column == ids_row) & (down < across))
    rank_row = jnp.sum(before.astype(jnp.int32), axis=0, keepdims=True)
    moves = (down == rank_row).astype(jnp.bfloat16)
    rows_copy.wait()
    unit = normalize_rows(rows_ref[...])
    out_ref[...] = jnp.dot(moves, unit, preferred_element_type=jnp.float32).astype(jnp.bfloat16)
    moves_ref[...] = moves
    ids_out_ref[...] = ids_row


def pack(out_ref, weighted, totals):
    count = weighted.shape[0]
    weighted = weighted.astype(jnp.bfloat16)
    columns = weighted.shape[1] // LANES
    for index in range(columns):
        out_ref[index * count : (index + 1) * count, :] = weighted[
            :, index * LANES : (index + 1) * LANES
        ]
    totals = as_row(totals)
    totals = jnp.concatenate([totals, jnp.zeros((1, LANES - count), jnp.float32)], axis=1)
    high = totals.astype(jnp.bfloat16).astype(jnp.float32)
    row = lax.broadcasted_iota(jnp.int32, (EXTRA, LANES), 0)
    out_ref[columns * count :, :] = jnp.where(row == 0, high, totals - high).astype(jnp.bfloat16)


def unpack(packed_ref, count):
    columns = packed_ref.shape[0] // count
    block = [
        packed_ref[index * count : (index + 1) * count, :].astype(jnp.float32)
        for index in range(columns)
    ]
    pair = packed_ref[columns * count :, :].astype(jnp.float32)
    return jnp.concatenate(block, axis=1), pair[0:1, :count] + pair[1:2, :count]


def partial_sums(queries, keys, bounds, own):
    count = bounds.shape[0]
    blocks = queries.shape[0] // count
    similar = lax.dot_general(
        queries, keys, (((1,), (1,)), ((), ())), preferred_element_type=jnp.float32
    )
    bounds = jnp.concatenate([bounds] * blocks, axis=0)
    key = lax.broadcasted_iota(jnp.int32, similar.shape, 1)
    place = lax.rem(key, count)
    allowed = (place >= bounds[:, 0:1]) & (place < bounds[:, 1:2])
    if own:
        query = lax.broadcasted_iota(jnp.int32, similar.shape, 0)
        allowed = allowed & ((key != query) | (key >= count))
    weights = jnp.where(allowed, jnp.exp(sharpness * (similar - 1.0)), 0.0)
    totals = jnp.sum(weights, axis=1, keepdims=True)
    return totals, jnp.dot(weights.astype(jnp.bfloat16), keys, preferred_element_type=jnp.float32)


def visitor_kernel(moves_ref, ids_ref, visitor_ref, own_ref, beside_ref, mates_ref, out_ref, bounds_ref):
    ids = ids_ref[...]
    label = jnp.sum(jnp.where(moves_ref[...] > 0, ids, 0), axis=1, keepdims=True)
    first = jnp.sum((ids < label).astype(jnp.int32), axis=1, keepdims=True)
    after = jnp.sum((ids <= label).astype(jnp.int32), axis=1, keepdims=True)
    lane = lax.broadcasted_iota(jnp.int32, bounds_ref.shape, 1)
    bounds = jnp.where(lane == 0, first, after)
    bounds_ref[...] = bounds
    keys = jnp.concatenate([own_ref[...], beside_ref[...], mates_ref[...]], axis=0)
    totals, weighted = partial_sums(visitor_ref[...], keys, bounds, False)
    pack(out_ref, weighted, totals)


def first_kernel(bounds_ref, own_ref, beside_ref, mates_ref, *refs):
    *key_refs, weighted_ref, totals_ref = refs
    own = own_ref[...]
    queries = jnp.concatenate([own, beside_ref[...]], axis=0)
    mate = mates_ref[: own.shape[0], :]
    keys = jnp.concatenate([own, mate, *(ref[...] for ref in key_refs)], axis=0)
    totals, weighted = partial_sums(queries, keys, bounds_ref[...], True)
    weighted_ref[...] = weighted
    totals_ref[...] = jnp.broadcast_to(totals, totals_ref.shape)


def beside_kernel(so_far_ref, totals_so_far_ref, bounds_ref, beside_ref, keys_ref, out_ref):
    count = beside_ref.shape[0]
    totals, weighted = partial_sums(beside_ref[...], keys_ref[...], bounds_ref[...], False)
    pack(out_ref, weighted + so_far_ref[count:, :], totals + totals_so_far_ref[count:, 0:1])


def own_kernel(so_far_ref, totals_so_far_ref, bounds_ref, own_ref, keys_ref, weighted_ref, totals_ref):
    count = own_ref.shape[0]
    totals, weighted = partial_sums(own_ref[...], keys_ref[...], bounds_ref[...], False)
    weighted_ref[...] = weighted + so_far_ref[:count, :]
    totals_ref[...] = as_row(totals + totals_so_far_ref[:count, 0:1])


def finish_kernel(moves_ref, weighted_ref, totals_ref, *refs):
    *back_refs, neighbour_hbm, score_hbm, neighbour_ref, score_ref, sems = refs
    count = neighbour_ref.shape[0]
    weighted, totals = weighted_ref[...], totals_ref[...]
    for back_ref in back_refs:
        back, back_totals = unpack(back_ref, count)
        weighted = weighted + back
        totals = totals + back_totals
    normed = (
        weighted * lax.rsqrt(jnp.mean(weighted * weighted, axis=-1, keepdims=True) + epsilon)
    ).astype(jnp.bfloat16)
    moves = moves_ref[...]
    neighbour_ref[...] = lax.dot_general(
        moves, normed, (((0,), (0,)), ((), ())), preferred_element_type=jnp.float32
    ).astype(jnp.bfloat16)
    neighbour_copy = pltpu.make_async_copy(neighbour_ref, neighbour_hbm, sems.at[0])
    neighbour_copy.start()
    scores = jnp.sum(moves.astype(jnp.float32) * as_column(jnp.log(totals)), axis=0, keepdims=True)
    score_ref[...] = scores.astype(jnp.bfloat16).reshape(count)
    score_copy = pltpu.make_async_copy(score_ref, score_hbm, sems.at[1])
    score_copy.start()
    neighbour_copy.wait()
    score_copy.wait()


EXTRA = 16
CORE, ACROSS, NEAR = 1, 2, 4
PLANE, GRID = 4, 16
NEXT = (2, 3, 1, 0)


def gathered_body(embeddings, cluster_id):
    rows_dev, features = embeddings.shape
    vmem = pl.BlockSpec(memory_space=pltpu.VMEM)
    stored = pl.BlockSpec(memory_space=pltpu.HBM)

    def swap(value, bits):
        return lax.ppermute(value, "blk", [(device, device ^ bits) for device in range(GRID)])

    def visit(value, home):
        pairs = [
            (device, NEXT[device // PLANE] * PLANE + device % PLANE) for device in range(GRID)
        ]
        return lax.ppermute(value, "blk", [pair[::-1] for pair in pairs] if home else pairs)

    def block(kind, *shape):
        return jax.ShapeDtypeStruct(shape, kind)

    def kernel(body, name, out_shape, *inputs, specs=vmem, out_specs=vmem, scratch=()):
        return pl.pallas_call(
            body,
            out_shape=out_shape,
            in_specs=[specs] * len(inputs),
            out_specs=(out_specs,) * len(out_shape),
            scratch_shapes=scratch,
            compiler_params=pltpu.CompilerParams(vmem_limit_bytes=32 * 1024 * 1024),
            name=name,
        )(*inputs)

    rows = block(jnp.bfloat16, rows_dev, features)
    own, moves, ids = kernel(
        arrange_kernel,
        "arrange",
        (rows, block(jnp.bfloat16, rows_dev, rows_dev), block(jnp.int32, 1, rows_dev)),
        pltpu.with_memory_space_constraint(cluster_id, pltpu.HBM),
        pltpu.with_memory_space_constraint(embeddings, pltpu.HBM),
        specs=stored,
        scratch=(
            pltpu.VMEM((rows_dev,), jnp.int32),
            pltpu.VMEM((rows_dev, features), jnp.bfloat16),
            pltpu.SemaphoreType.DMA((2,)),
        ),
    )

    packed = block(jnp.bfloat16, rows_dev * features // LANES + EXTRA, LANES)
    near = swap(own, NEAR)
    visitor, beside = lax.optimization_barrier((visit(own, home=False), swap(own, ACROSS)))
    mates = swap(jnp.concatenate([own, beside], axis=0), CORE)
    later = swap(jnp.concatenate([near, visitor], axis=0), CORE)
    partial, bounds = kernel(
        visitor_kernel,
        "visitor",
        (packed, block(jnp.int32, rows_dev, LANES)),
        *(moves, ids, visitor, own, beside, mates),
    )
    back_home = visit(partial, home=True)
    so_far = kernel(
        first_kernel,
        "first",
        (block(jnp.float32, 2 * rows_dev, features), block(jnp.float32, 2 * rows_dev, LANES)),
        *(bounds, own, beside, mates, near, visitor),
    )
    (partial,) = kernel(beside_kernel, "beside", (packed,), *so_far, bounds, beside, later)
    back = swap(partial, ACROSS)
    weighted, totals = kernel(
        own_kernel,
        "own",
        (block(jnp.float32, rows_dev, features), block(jnp.float32, 1, rows_dev)),
        *(*so_far, bounds, own, later),
    )
    weighted, back_home = lax.optimization_barrier((weighted, back_home))
    return tuple(
        kernel(
            finish_kernel,
            "finish",
            (rows, block(jnp.bfloat16, rows_dev)),
            *(moves, weighted, totals, back, back_home),
            out_specs=stored,
            scratch=(
                pltpu.VMEM((rows_dev, features), jnp.bfloat16),
                pltpu.VMEM((rows_dev,), jnp.bfloat16),
                pltpu.SemaphoreType.DMA((2,)),
            ),
        )
    )


def from_behind(value, axis, steps):
    count = lax.axis_size(axis)
    initial, last = (max(0, -steps), min(count, count - steps))
    return lax.ppermute(value, axis, [(source, source + steps) for source in range(initial, last)])


def pair_terms(queries, visiting, allowed):
    similar = jnp.dot(queries, visiting.T, preferred_element_type=jnp.float32)
    return jnp.where(allowed, jnp.exp(sharpness * (similar - 1.0)), jnp.zeros_like(similar))


def finish(weighted, totals):
    normed = (
        weighted * lax.rsqrt(jnp.mean(weighted * weighted, axis=-1, keepdims=True) + epsilon)
    ).astype(jnp.bfloat16)
    return (normed, jnp.log(totals).astype(jnp.bfloat16))


def collected_body(embeddings, cluster_id):
    rows_dev, features = embeddings.shape
    devices = lax.axis_size("blk")
    per_peer = rows_dev // devices
    clusters = devices // 4
    unit_rows = normalize_rows(embeddings)
    labels = jnp.arange(clusters, dtype=jnp.int32)
    counts = jnp.sum((cluster_id[:, None] == labels[None, :]).astype(jnp.int32), axis=0)
    group_ends = jnp.cumsum(counts // per_peer)

    def owner_cluster(device):
        in_range = (device >= 0) & (device < devices)
        return jnp.where(in_range, jnp.sum((device >= group_ends).astype(jnp.int32)), -1)

    position = jnp.arange(rows_dev, dtype=jnp.int32)
    arrange_order = jnp.argsort(cluster_id * rows_dev + position)
    inverse = jnp.argsort(arrange_order)
    arranged = unit_rows[arrange_order].reshape(devices, per_peer, features)
    held_rows = lax.all_to_all(arranged, "blk", split_axis=0, concat_axis=0, tiled=True).reshape(
        rows_dev, features
    )
    self_index = lax.axis_index("blk")
    mine = owner_cluster(self_index)
    weights = pair_terms(held_rows, held_rows, position[:, None] != position[None, :])
    totals = jnp.sum(weights, axis=1)
    weighted = jnp.dot(weights.astype(jnp.bfloat16), held_rows, preferred_element_type=jnp.float32)
    from_lower = held_rows
    from_upper = held_rows
    for distance in range(1, U_MAX):
        from_lower = from_behind(from_lower, "blk", 1)
        from_upper = from_behind(from_upper, "blk", -1)
        for visiting, source in (
            (from_lower, self_index - distance),
            (from_upper, self_index + distance),
        ):
            weights = pair_terms(held_rows, visiting, owner_cluster(source) == mine)
            totals = totals + jnp.sum(weights, axis=1)
            weighted = weighted + jnp.dot(
                weights.astype(jnp.bfloat16), visiting, preferred_element_type=jnp.float32
            )
    normed, scores = finish(weighted, totals)
    returned_rows, returned_scores = (
        lax.all_to_all(
            normed.reshape(devices, per_peer, features),
            "blk",
            split_axis=0,
            concat_axis=0,
            tiled=True,
        ),
        lax.all_to_all(
            scores.reshape(devices, per_peer), "blk", split_axis=0, concat_axis=0, tiled=True
        ),
    )
    neighbour = returned_rows.reshape(rows_dev, features)[inverse]
    dup_score = returned_scores.reshape(rows_dev)[inverse]
    return (neighbour, dup_score)


def solution(mesh):
    placed = (P(("groups", "blk"), None), P(("groups", "blk")))
    devices = mesh.shape["blk"]

    def body(embeddings, cluster_id):
        gathered = embeddings.size * embeddings.dtype.itemsize * devices
        fits = gathered <= GATHER_LIMIT and devices == GRID
        plan = gathered_body if fits else collected_body
        return plan(embeddings, cluster_id)

    return jax.shard_map(
        body,
        mesh=mesh,
        in_specs=placed,
        out_specs=(P(("groups", "blk"), None), P(("groups", "blk"))),
        check_vma=False,
    )
```

```python
import jax
import jax.numpy as jnp
from jax import lax
from jax.experimental import pallas as pl
from jax.experimental.pallas import tpu as pltpu
from jax.sharding import PartitionSpec as P

U_MAX = 8
GATHER_LIMIT = 4 * 1024 * 1024


sharpness = 10.0
epsilon = 1e-06


def normalize_rows(values):
    widened = values.astype(jnp.float32)
    return (
        widened
        * lax.rsqrt(jnp.mean(widened * widened, axis=-1, keepdims=True) + epsilon)
        * widened.shape[-1] ** (-0.5)
    ).astype(jnp.bfloat16)


def as_column(row):
    count = row.shape[1]
    across = lax.broadcasted_iota(jnp.int32, (count, count), 1)
    down = lax.broadcasted_iota(jnp.int32, (count, count), 0)
    return jnp.sum(jnp.where(across == down, row, jnp.zeros_like(row)), axis=1, keepdims=True)


def as_row(column):
    count = column.shape[0]
    across = lax.broadcasted_iota(jnp.int32, (count, count), 1)
    down = lax.broadcasted_iota(jnp.int32, (count, count), 0)
    return jnp.sum(jnp.where(across == down, column, jnp.zeros_like(column)), axis=0, keepdims=True)


LANES = 128


def arrange_kernel(ids_hbm, rows_hbm, out_ref, moves_ref, ids_out_ref, ids_ref, rows_ref, sems):
    ids_copy = pltpu.make_async_copy(ids_hbm, ids_ref, sems.at[0])
    rows_copy = pltpu.make_async_copy(rows_hbm, rows_ref, sems.at[1])
    ids_copy.start()
    rows_copy.start()
    count = rows_ref.shape[0]
    ids_copy.wait()
    ids_row = ids_ref[...].reshape(1, count)
    ids_column = as_column(ids_row)
    across = lax.broadcasted_iota(jnp.int32, (count, count), 1)
    down = lax.broadcasted_iota(jnp.int32, (count, count), 0)
    before = (ids_column < ids_row) | ((ids_column == ids_row) & (down < across))
    rank_row = jnp.sum(before.astype(jnp.int32), axis=0, keepdims=True)
    moves = (down == rank_row).astype(jnp.bfloat16)
    rows_copy.wait()
    unit = normalize_rows(rows_ref[...])
    out_ref[...] = jnp.dot(moves, unit, preferred_element_type=jnp.float32).astype(jnp.bfloat16)
    moves_ref[...] = moves
    ids_out_ref[...] = ids_row


def pack(out_ref, weighted, totals):
    count = weighted.shape[0]
    weighted = weighted.astype(jnp.bfloat16)
    columns = weighted.shape[1] // LANES
    for index in range(columns):
        out_ref[index * count : (index + 1) * count, :] = weighted[
            :, index * LANES : (index + 1) * LANES
        ]
    totals = as_row(totals)
    totals = jnp.concatenate([totals, jnp.zeros((1, LANES - count), jnp.float32)], axis=1)
    high = totals.astype(jnp.bfloat16).astype(jnp.float32)
    row = lax.broadcasted_iota(jnp.int32, (EXTRA, LANES), 0)
    out_ref[columns * count :, :] = jnp.where(row == 0, high, totals - high).astype(jnp.bfloat16)


def unpack(packed_ref, count):
    columns = packed_ref.shape[0] // count
    block = [
        packed_ref[index * count : (index + 1) * count, :].astype(jnp.float32)
        for index in range(columns)
    ]
    pair = packed_ref[columns * count :, :].astype(jnp.float32)
    return jnp.concatenate(block, axis=1), pair[0:1, :count] + pair[1:2, :count]


def partial_sums(queries, keys, bounds, own):
    count = bounds.shape[0]
    blocks = queries.shape[0] // count
    similar = lax.dot_general(
        queries, keys, (((1,), (1,)), ((), ())), preferred_element_type=jnp.float32
    )
    bounds = jnp.concatenate([bounds] * blocks, axis=0)
    key = lax.broadcasted_iota(jnp.int32, similar.shape, 1)
    place = lax.rem(key, count)
    allowed = (place >= bounds[:, 0:1]) & (place < bounds[:, 1:2])
    if own:
        query = lax.broadcasted_iota(jnp.int32, similar.shape, 0)
        allowed = allowed & ((key != query) | (key >= count))
    weights = jnp.where(allowed, jnp.exp(sharpness * (similar - 1.0)), 0.0)
    totals = jnp.sum(weights, axis=1, keepdims=True)
    return totals, jnp.dot(weights.astype(jnp.bfloat16), keys, preferred_element_type=jnp.float32)


def visitor_kernel(moves_ref, ids_ref, visitor_ref, own_ref, beside_ref, mates_ref, out_ref, bounds_ref):
    ids = ids_ref[...]
    label = jnp.sum(jnp.where(moves_ref[...] > 0, ids, 0), axis=1, keepdims=True)
    first = jnp.sum((ids < label).astype(jnp.int32), axis=1, keepdims=True)
    after = jnp.sum((ids <= label).astype(jnp.int32), axis=1, keepdims=True)
    lane = lax.broadcasted_iota(jnp.int32, bounds_ref.shape, 1)
    bounds = jnp.where(lane == 0, first, after)
    bounds_ref[...] = bounds
    keys = jnp.concatenate([own_ref[...], beside_ref[...], mates_ref[...]], axis=0)
    totals, weighted = partial_sums(visitor_ref[...], keys, bounds, False)
    pack(out_ref, weighted, totals)


def first_kernel(bounds_ref, own_ref, beside_ref, mates_ref, *refs):
    *key_refs, weighted_ref, totals_ref = refs
    own = own_ref[...]
    queries = jnp.concatenate([own, beside_ref[...]], axis=0)
    mate = mates_ref[: own.shape[0], :]
    keys = jnp.concatenate([own, mate, *(ref[...] for ref in key_refs)], axis=0)
    totals, weighted = partial_sums(queries, keys, bounds_ref[...], True)
    weighted_ref[...] = weighted
    totals_ref[...] = jnp.broadcast_to(totals, totals_ref.shape)


def beside_kernel(so_far_ref, totals_so_far_ref, bounds_ref, beside_ref, keys_ref, out_ref):
    count = beside_ref.shape[0]
    totals, weighted = partial_sums(beside_ref[...], keys_ref[...], bounds_ref[...], False)
    pack(out_ref, weighted + so_far_ref[count:, :], totals + totals_so_far_ref[count:, 0:1])


def own_kernel(so_far_ref, totals_so_far_ref, bounds_ref, own_ref, keys_ref, weighted_ref, totals_ref):
    count = own_ref.shape[0]
    totals, weighted = partial_sums(own_ref[...], keys_ref[...], bounds_ref[...], False)
    weighted_ref[...] = weighted + so_far_ref[:count, :]
    totals_ref[...] = as_row(totals + totals_so_far_ref[:count, 0:1])


def finish_kernel(moves_ref, weighted_ref, totals_ref, *refs):
    *back_refs, neighbour_hbm, score_hbm, neighbour_ref, score_ref, sems = refs
    count = neighbour_ref.shape[0]
    weighted, totals = weighted_ref[...], totals_ref[...]
    for back_ref in back_refs:
        back, back_totals = unpack(back_ref, count)
        weighted = weighted + back
        totals = totals + back_totals
    normed = (
        weighted * lax.rsqrt(jnp.mean(weighted * weighted, axis=-1, keepdims=True) + epsilon)
    ).astype(jnp.bfloat16)
    moves = moves_ref[...]
    neighbour_ref[...] = lax.dot_general(
        moves, normed, (((0,), (0,)), ((), ())), preferred_element_type=jnp.float32
    ).astype(jnp.bfloat16)
    neighbour_copy = pltpu.make_async_copy(neighbour_ref, neighbour_hbm, sems.at[0])
    neighbour_copy.start()
    scores = jnp.sum(moves.astype(jnp.float32) * as_column(jnp.log(totals)), axis=0, keepdims=True)
    score_ref[...] = scores.astype(jnp.bfloat16).reshape(count)
    score_copy = pltpu.make_async_copy(score_ref, score_hbm, sems.at[1])
    score_copy.start()
    neighbour_copy.wait()
    score_copy.wait()


EXTRA = 16
CORE, ACROSS, MIRROR = 1, 2, 12
PLANE, GRID = 4, 16
NEXT = (2, 0, 3, 1)


def gathered_body(embeddings, cluster_id):
    rows_dev, features = embeddings.shape
    vmem = pl.BlockSpec(memory_space=pltpu.VMEM)
    stored = pl.BlockSpec(memory_space=pltpu.HBM)

    def swap(value, bits):
        return lax.ppermute(value, "blk", [(device, device ^ bits) for device in range(GRID)])

    def visit(value, home):
        pairs = [
            (device, NEXT[device // PLANE] * PLANE + device % PLANE) for device in range(GRID)
        ]
        return lax.ppermute(value, "blk", [pair[::-1] for pair in pairs] if home else pairs)

    def block(kind, *shape):
        return jax.ShapeDtypeStruct(shape, kind)

    def kernel(body, name, out_shape, *inputs, specs=vmem, out_specs=vmem, scratch=()):
        return pl.pallas_call(
            body,
            out_shape=out_shape,
            in_specs=[specs] * len(inputs),
            out_specs=(out_specs,) * len(out_shape),
            scratch_shapes=scratch,
            compiler_params=pltpu.CompilerParams(vmem_limit_bytes=32 * 1024 * 1024),
            name=name,
        )(*inputs)

    rows = block(jnp.bfloat16, rows_dev, features)
    own, moves, ids = kernel(
        arrange_kernel,
        "arrange",
        (rows, block(jnp.bfloat16, rows_dev, rows_dev), block(jnp.int32, 1, rows_dev)),
        pltpu.with_memory_space_constraint(cluster_id, pltpu.HBM),
        pltpu.with_memory_space_constraint(embeddings, pltpu.HBM),
        specs=stored,
        scratch=(
            pltpu.VMEM((rows_dev,), jnp.int32),
            pltpu.VMEM((rows_dev, features), jnp.bfloat16),
            pltpu.SemaphoreType.DMA((2,)),
        ),
    )

    packed = block(jnp.bfloat16, rows_dev * features // LANES + EXTRA, LANES)
    mirror, beside = lax.optimization_barrier((swap(own, MIRROR), swap(own, ACROSS)))
    visitor = visit(own, home=False)
    mates = swap(jnp.concatenate([own, beside], axis=0), CORE)
    later = swap(jnp.concatenate([mirror, visitor], axis=0), CORE)
    partial, bounds = kernel(
        visitor_kernel,
        "visitor",
        (packed, block(jnp.int32, rows_dev, LANES)),
        *(moves, ids, visitor, own, beside, mates),
    )
    back_home = visit(partial, home=True)
    so_far = kernel(
        first_kernel,
        "first",
        (block(jnp.float32, 2 * rows_dev, features), block(jnp.float32, 2 * rows_dev, LANES)),
        *(bounds, own, beside, mates, mirror, visitor),
    )
    (partial,) = kernel(beside_kernel, "beside", (packed,), *so_far, bounds, beside, later)
    back = swap(partial, ACROSS)
    weighted, totals = kernel(
        own_kernel,
        "own",
        (block(jnp.float32, rows_dev, features), block(jnp.float32, 1, rows_dev)),
        *(*so_far, bounds, own, later),
    )
    weighted, back_home = lax.optimization_barrier((weighted, back_home))
    return tuple(
        kernel(
            finish_kernel,
            "finish",
            (rows, block(jnp.bfloat16, rows_dev)),
            *(moves, weighted, totals, back, back_home),
            out_specs=stored,
            scratch=(
                pltpu.VMEM((rows_dev, features), jnp.bfloat16),
                pltpu.VMEM((rows_dev,), jnp.bfloat16),
                pltpu.SemaphoreType.DMA((2,)),
            ),
        )
    )


def from_behind(value, axis, steps):
    count = lax.axis_size(axis)
    initial, last = (max(0, -steps), min(count, count - steps))
    return lax.ppermute(value, axis, [(source, source + steps) for source in range(initial, last)])


def pair_terms(queries, visiting, allowed):
    similar = jnp.dot(queries, visiting.T, preferred_element_type=jnp.float32)
    return jnp.where(allowed, jnp.exp(sharpness * (similar - 1.0)), jnp.zeros_like(similar))


def finish(weighted, totals):
    normed = (
        weighted * lax.rsqrt(jnp.mean(weighted * weighted, axis=-1, keepdims=True) + epsilon)
    ).astype(jnp.bfloat16)
    return (normed, jnp.log(totals).astype(jnp.bfloat16))


def collected_body(embeddings, cluster_id):
    rows_dev, features = embeddings.shape
    devices = lax.axis_size("blk")
    per_peer = rows_dev // devices
    clusters = devices // 4
    unit_rows = normalize_rows(embeddings)
    labels = jnp.arange(clusters, dtype=jnp.int32)
    counts = jnp.sum((cluster_id[:, None] == labels[None, :]).astype(jnp.int32), axis=0)
    group_ends = jnp.cumsum(counts // per_peer)

    def owner_cluster(device):
        in_range = (device >= 0) & (device < devices)
        return jnp.where(in_range, jnp.sum((device >= group_ends).astype(jnp.int32)), -1)

    position = jnp.arange(rows_dev, dtype=jnp.int32)
    arrange_order = jnp.argsort(cluster_id * rows_dev + position)
    inverse = jnp.argsort(arrange_order)
    arranged = unit_rows[arrange_order].reshape(devices, per_peer, features)
    held_rows = lax.all_to_all(arranged, "blk", split_axis=0, concat_axis=0, tiled=True).reshape(
        rows_dev, features
    )
    self_index = lax.axis_index("blk")
    mine = owner_cluster(self_index)
    weights = pair_terms(held_rows, held_rows, position[:, None] != position[None, :])
    totals = jnp.sum(weights, axis=1)
    weighted = jnp.dot(weights.astype(jnp.bfloat16), held_rows, preferred_element_type=jnp.float32)
    from_lower = held_rows
    from_upper = held_rows
    for distance in range(1, U_MAX):
        from_lower = from_behind(from_lower, "blk", 1)
        from_upper = from_behind(from_upper, "blk", -1)
        for visiting, source in (
            (from_lower, self_index - distance),
            (from_upper, self_index + distance),
        ):
            weights = pair_terms(held_rows, visiting, owner_cluster(source) == mine)
            totals = totals + jnp.sum(weights, axis=1)
            weighted = weighted + jnp.dot(
                weights.astype(jnp.bfloat16), visiting, preferred_element_type=jnp.float32
            )
    normed, scores = finish(weighted, totals)
    returned_rows, returned_scores = (
        lax.all_to_all(
            normed.reshape(devices, per_peer, features),
            "blk",
            split_axis=0,
            concat_axis=0,
            tiled=True,
        ),
        lax.all_to_all(
            scores.reshape(devices, per_peer), "blk", split_axis=0, concat_axis=0, tiled=True
        ),
    )
    neighbour = returned_rows.reshape(rows_dev, features)[inverse]
    dup_score = returned_scores.reshape(rows_dev)[inverse]
    return (neighbour, dup_score)


def solution(mesh):
    placed = (P(("groups", "blk"), None), P(("groups", "blk")))
    devices = mesh.shape["blk"]

    def body(embeddings, cluster_id):
        gathered = embeddings.size * embeddings.dtype.itemsize * devices
        fits = gathered <= GATHER_LIMIT and devices == GRID
        plan = gathered_body if fits else collected_body
        return plan(embeddings, cluster_id)

    return jax.shard_map(
        body,
        mesh=mesh,
        in_specs=placed,
        out_specs=(P(("groups", "blk"), None), P(("groups", "blk"))),
        check_vma=False,
    )
```

```python
import jax
import jax.numpy as jnp
from jax import lax
from jax.experimental import pallas as pl
from jax.experimental.pallas import tpu as pltpu
from jax.sharding import PartitionSpec as P

U_MAX = 8
GATHER_LIMIT = 4 * 1024 * 1024


sharpness = 10.0
epsilon = 1e-06


def normalize_rows(values):
    widened = values.astype(jnp.float32)
    return (
        widened
        * lax.rsqrt(jnp.mean(widened * widened, axis=-1, keepdims=True) + epsilon)
        * widened.shape[-1] ** (-0.5)
    ).astype(jnp.bfloat16)


def as_column(row):
    count = row.shape[1]
    across = lax.broadcasted_iota(jnp.int32, (count, count), 1)
    down = lax.broadcasted_iota(jnp.int32, (count, count), 0)
    return jnp.sum(jnp.where(across == down, row, jnp.zeros_like(row)), axis=1, keepdims=True)


def as_row(column):
    count = column.shape[0]
    across = lax.broadcasted_iota(jnp.int32, (count, count), 1)
    down = lax.broadcasted_iota(jnp.int32, (count, count), 0)
    return jnp.sum(jnp.where(across == down, column, jnp.zeros_like(column)), axis=0, keepdims=True)


LANES = 128


def arrange_kernel(ids_hbm, rows_hbm, out_ref, moves_ref, ids_out_ref, ids_ref, rows_ref, sems):
    ids_copy = pltpu.make_async_copy(ids_hbm, ids_ref, sems.at[0])
    rows_copy = pltpu.make_async_copy(rows_hbm, rows_ref, sems.at[1])
    ids_copy.start()
    rows_copy.start()
    count = rows_ref.shape[0]
    ids_copy.wait()
    ids_row = ids_ref[...].reshape(1, count)
    ids_column = as_column(ids_row)
    across = lax.broadcasted_iota(jnp.int32, (count, count), 1)
    down = lax.broadcasted_iota(jnp.int32, (count, count), 0)
    before = (ids_column < ids_row) | ((ids_column == ids_row) & (down < across))
    rank_row = jnp.sum(before.astype(jnp.int32), axis=0, keepdims=True)
    moves = (down == rank_row).astype(jnp.bfloat16)
    rows_copy.wait()
    unit = normalize_rows(rows_ref[...])
    out_ref[...] = jnp.dot(moves, unit, preferred_element_type=jnp.float32).astype(jnp.bfloat16)
    moves_ref[...] = moves
    ids_out_ref[...] = ids_row


def pack(out_ref, weighted, totals):
    count = weighted.shape[0]
    weighted = weighted.astype(jnp.bfloat16)
    columns = weighted.shape[1] // LANES
    for index in range(columns):
        out_ref[index * count : (index + 1) * count, :] = weighted[
            :, index * LANES : (index + 1) * LANES
        ]
    totals = as_row(totals)
    totals = jnp.concatenate([totals, jnp.zeros((1, LANES - count), jnp.float32)], axis=1)
    high = totals.astype(jnp.bfloat16).astype(jnp.float32)
    row = lax.broadcasted_iota(jnp.int32, (EXTRA, LANES), 0)
    out_ref[columns * count :, :] = jnp.where(row == 0, high, totals - high).astype(jnp.bfloat16)


def unpack(packed_ref, count):
    columns = packed_ref.shape[0] // count
    block = [
        packed_ref[index * count : (index + 1) * count, :].astype(jnp.float32)
        for index in range(columns)
    ]
    pair = packed_ref[columns * count :, :].astype(jnp.float32)
    return jnp.concatenate(block, axis=1), pair[0:1, :count] + pair[1:2, :count]


def partial_sums(queries, keys, bounds, own):
    count = bounds.shape[0]
    blocks = queries.shape[0] // count
    similar = lax.dot_general(
        queries, keys, (((1,), (1,)), ((), ())), preferred_element_type=jnp.float32
    )
    bounds = jnp.concatenate([bounds] * blocks, axis=0)
    key = lax.broadcasted_iota(jnp.int32, similar.shape, 1)
    place = lax.rem(key, count)
    allowed = (place >= bounds[:, 0:1]) & (place < bounds[:, 1:2])
    if own:
        query = lax.broadcasted_iota(jnp.int32, similar.shape, 0)
        allowed = allowed & ((key != query) | (key >= count))
    weights = jnp.where(allowed, jnp.exp(sharpness * (similar - 1.0)), 0.0)
    totals = jnp.sum(weights, axis=1, keepdims=True)
    return totals, jnp.dot(weights.astype(jnp.bfloat16), keys, preferred_element_type=jnp.float32)


def visitor_kernel(moves_ref, ids_ref, visitor_ref, own_ref, beside_ref, mates_ref, out_ref, bounds_ref):
    ids = ids_ref[...]
    label = jnp.sum(jnp.where(moves_ref[...] > 0, ids, 0), axis=1, keepdims=True)
    first = jnp.sum((ids < label).astype(jnp.int32), axis=1, keepdims=True)
    after = jnp.sum((ids <= label).astype(jnp.int32), axis=1, keepdims=True)
    lane = lax.broadcasted_iota(jnp.int32, bounds_ref.shape, 1)
    bounds = jnp.where(lane == 0, first, after)
    bounds_ref[...] = bounds
    keys = jnp.concatenate([own_ref[...], beside_ref[...], mates_ref[...]], axis=0)
    totals, weighted = partial_sums(visitor_ref[...], keys, bounds, False)
    pack(out_ref, weighted, totals)


def first_kernel(bounds_ref, own_ref, beside_ref, mates_ref, *refs):
    *key_refs, weighted_ref, totals_ref = refs
    own = own_ref[...]
    queries = jnp.concatenate([own, beside_ref[...]], axis=0)
    mate = mates_ref[: own.shape[0], :]
    keys = jnp.concatenate([own, mate, *(ref[...] for ref in key_refs)], axis=0)
    totals, weighted = partial_sums(queries, keys, bounds_ref[...], True)
    weighted_ref[...] = weighted
    totals_ref[...] = jnp.broadcast_to(totals, totals_ref.shape)


def beside_kernel(so_far_ref, totals_so_far_ref, bounds_ref, beside_ref, keys_ref, out_ref):
    count = beside_ref.shape[0]
    totals, weighted = partial_sums(beside_ref[...], keys_ref[...], bounds_ref[...], False)
    pack(out_ref, weighted + so_far_ref[count:, :], totals + totals_so_far_ref[count:, 0:1])


def own_kernel(so_far_ref, totals_so_far_ref, bounds_ref, own_ref, keys_ref, weighted_ref, totals_ref):
    count = own_ref.shape[0]
    totals, weighted = partial_sums(own_ref[...], keys_ref[...], bounds_ref[...], False)
    weighted_ref[...] = weighted + so_far_ref[:count, :]
    totals_ref[...] = as_row(totals + totals_so_far_ref[:count, 0:1])


def finish_kernel(moves_ref, weighted_ref, totals_ref, *refs):
    *back_refs, neighbour_hbm, score_hbm, neighbour_ref, score_ref, sems = refs
    count = neighbour_ref.shape[0]
    weighted, totals = weighted_ref[...], totals_ref[...]
    for back_ref in back_refs:
        back, back_totals = unpack(back_ref, count)
        weighted = weighted + back
        totals = totals + back_totals
    normed = (
        weighted * lax.rsqrt(jnp.mean(weighted * weighted, axis=-1, keepdims=True) + epsilon)
    ).astype(jnp.bfloat16)
    moves = moves_ref[...]
    neighbour_ref[...] = lax.dot_general(
        moves, normed, (((0,), (0,)), ((), ())), preferred_element_type=jnp.float32
    ).astype(jnp.bfloat16)
    neighbour_copy = pltpu.make_async_copy(neighbour_ref, neighbour_hbm, sems.at[0])
    neighbour_copy.start()
    scores = jnp.sum(moves.astype(jnp.float32) * as_column(jnp.log(totals)), axis=0, keepdims=True)
    score_ref[...] = scores.astype(jnp.bfloat16).reshape(count)
    score_copy = pltpu.make_async_copy(score_ref, score_hbm, sems.at[1])
    score_copy.start()
    neighbour_copy.wait()
    score_copy.wait()


EXTRA = 16
CORE, ACROSS, MIRROR = 1, 2, 12
PLANE, GRID = 4, 16
NEXT = (2, 0, 3, 1)


def gathered_body(embeddings, cluster_id):
    rows_dev, features = embeddings.shape
    vmem = pl.BlockSpec(memory_space=pltpu.VMEM)
    stored = pl.BlockSpec(memory_space=pltpu.HBM)

    def swap(value, bits):
        return lax.ppermute(value, "blk", [(device, device ^ bits) for device in range(GRID)])

    def visit(value, home):
        pairs = [
            (device, NEXT[device // PLANE] * PLANE + device % PLANE) for device in range(GRID)
        ]
        return lax.ppermute(value, "blk", [pair[::-1] for pair in pairs] if home else pairs)

    def block(kind, *shape):
        return jax.ShapeDtypeStruct(shape, kind)

    def kernel(body, name, out_shape, *inputs, specs=vmem, out_specs=vmem, scratch=()):
        return pl.pallas_call(
            body,
            out_shape=out_shape,
            in_specs=[specs] * len(inputs),
            out_specs=(out_specs,) * len(out_shape),
            scratch_shapes=scratch,
            compiler_params=pltpu.CompilerParams(vmem_limit_bytes=32 * 1024 * 1024),
            name=name,
        )(*inputs)

    rows = block(jnp.bfloat16, rows_dev, features)
    own, moves, ids = kernel(
        arrange_kernel,
        "arrange",
        (rows, block(jnp.bfloat16, rows_dev, rows_dev), block(jnp.int32, 1, rows_dev)),
        pltpu.with_memory_space_constraint(cluster_id, pltpu.HBM),
        pltpu.with_memory_space_constraint(embeddings, pltpu.HBM),
        specs=stored,
        scratch=(
            pltpu.VMEM((rows_dev,), jnp.int32),
            pltpu.VMEM((rows_dev, features), jnp.bfloat16),
            pltpu.SemaphoreType.DMA((2,)),
        ),
    )

    packed = block(jnp.bfloat16, rows_dev * features // LANES + EXTRA, LANES)
    beside = swap(own, ACROSS)
    mates = swap(jnp.concatenate([own, beside], axis=0), CORE)
    mirror, visitor = lax.optimization_barrier((swap(own, MIRROR), visit(own, home=False)))
    later = swap(jnp.concatenate([mirror, visitor], axis=0), CORE)
    partial, bounds = kernel(
        visitor_kernel,
        "visitor",
        (packed, block(jnp.int32, rows_dev, LANES)),
        *(moves, ids, visitor, own, beside, mates),
    )
    back_home = visit(partial, home=True)
    so_far = kernel(
        first_kernel,
        "first",
        (block(jnp.float32, 2 * rows_dev, features), block(jnp.float32, 2 * rows_dev, LANES)),
        *(bounds, own, beside, mates, mirror, visitor),
    )
    (partial,) = kernel(beside_kernel, "beside", (packed,), *so_far, bounds, beside, later)
    back = swap(partial, ACROSS)
    weighted, totals = kernel(
        own_kernel,
        "own",
        (block(jnp.float32, rows_dev, features), block(jnp.float32, 1, rows_dev)),
        *(*so_far, bounds, own, later),
    )
    weighted, back_home = lax.optimization_barrier((weighted, back_home))
    return tuple(
        kernel(
            finish_kernel,
            "finish",
            (rows, block(jnp.bfloat16, rows_dev)),
            *(moves, weighted, totals, back, back_home),
            out_specs=stored,
            scratch=(
                pltpu.VMEM((rows_dev, features), jnp.bfloat16),
                pltpu.VMEM((rows_dev,), jnp.bfloat16),
                pltpu.SemaphoreType.DMA((2,)),
            ),
        )
    )


def from_behind(value, axis, steps):
    count = lax.axis_size(axis)
    initial, last = (max(0, -steps), min(count, count - steps))
    return lax.ppermute(value, axis, [(source, source + steps) for source in range(initial, last)])


def pair_terms(queries, visiting, allowed):
    similar = jnp.dot(queries, visiting.T, preferred_element_type=jnp.float32)
    return jnp.where(allowed, jnp.exp(sharpness * (similar - 1.0)), jnp.zeros_like(similar))


def finish(weighted, totals):
    normed = (
        weighted * lax.rsqrt(jnp.mean(weighted * weighted, axis=-1, keepdims=True) + epsilon)
    ).astype(jnp.bfloat16)
    return (normed, jnp.log(totals).astype(jnp.bfloat16))


def collected_body(embeddings, cluster_id):
    rows_dev, features = embeddings.shape
    devices = lax.axis_size("blk")
    per_peer = rows_dev // devices
    clusters = devices // 4
    unit_rows = normalize_rows(embeddings)
    labels = jnp.arange(clusters, dtype=jnp.int32)
    counts = jnp.sum((cluster_id[:, None] == labels[None, :]).astype(jnp.int32), axis=0)
    group_ends = jnp.cumsum(counts // per_peer)

    def owner_cluster(device):
        in_range = (device >= 0) & (device < devices)
        return jnp.where(in_range, jnp.sum((device >= group_ends).astype(jnp.int32)), -1)

    position = jnp.arange(rows_dev, dtype=jnp.int32)
    arrange_order = jnp.argsort(cluster_id * rows_dev + position)
    inverse = jnp.argsort(arrange_order)
    arranged = unit_rows[arrange_order].reshape(devices, per_peer, features)
    held_rows = lax.all_to_all(arranged, "blk", split_axis=0, concat_axis=0, tiled=True).reshape(
        rows_dev, features
    )
    self_index = lax.axis_index("blk")
    mine = owner_cluster(self_index)
    weights = pair_terms(held_rows, held_rows, position[:, None] != position[None, :])
    totals = jnp.sum(weights, axis=1)
    weighted = jnp.dot(weights.astype(jnp.bfloat16), held_rows, preferred_element_type=jnp.float32)
    from_lower = held_rows
    from_upper = held_rows
    for distance in range(1, U_MAX):
        from_lower = from_behind(from_lower, "blk", 1)
        from_upper = from_behind(from_upper, "blk", -1)
        for visiting, source in (
            (from_lower, self_index - distance),
            (from_upper, self_index + distance),
        ):
            weights = pair_terms(held_rows, visiting, owner_cluster(source) == mine)
            totals = totals + jnp.sum(weights, axis=1)
            weighted = weighted + jnp.dot(
                weights.astype(jnp.bfloat16), visiting, preferred_element_type=jnp.float32
            )
    normed, scores = finish(weighted, totals)
    returned_rows, returned_scores = (
        lax.all_to_all(
            normed.reshape(devices, per_peer, features),
            "blk",
            split_axis=0,
            concat_axis=0,
            tiled=True,
        ),
        lax.all_to_all(
            scores.reshape(devices, per_peer), "blk", split_axis=0, concat_axis=0, tiled=True
        ),
    )
    neighbour = returned_rows.reshape(rows_dev, features)[inverse]
    dup_score = returned_scores.reshape(rows_dev)[inverse]
    return (neighbour, dup_score)


def solution(mesh):
    placed = (P(("groups", "blk"), None), P(("groups", "blk")))
    devices = mesh.shape["blk"]

    def body(embeddings, cluster_id):
        gathered = embeddings.size * embeddings.dtype.itemsize * devices
        fits = gathered <= GATHER_LIMIT and devices == GRID
        plan = gathered_body if fits else collected_body
        return plan(embeddings, cluster_id)

    return jax.shard_map(
        body,
        mesh=mesh,
        in_specs=placed,
        out_specs=(P(("groups", "blk"), None), P(("groups", "blk"))),
        check_vma=False,
    )
```

```python
import jax
import jax.numpy as jnp
from jax import lax
from jax.experimental import pallas as pl
from jax.experimental.pallas import tpu as pltpu
from jax.sharding import PartitionSpec as P

U_MAX = 8
GATHER_LIMIT = 4 * 1024 * 1024


sharpness = 10.0
epsilon = 1e-06


def normalize_rows(values):
    widened = values.astype(jnp.float32)
    return (
        widened
        * lax.rsqrt(jnp.mean(widened * widened, axis=-1, keepdims=True) + epsilon)
        * widened.shape[-1] ** (-0.5)
    ).astype(jnp.bfloat16)


def as_column(row):
    count = row.shape[1]
    across = lax.broadcasted_iota(jnp.int32, (count, count), 1)
    down = lax.broadcasted_iota(jnp.int32, (count, count), 0)
    return jnp.sum(jnp.where(across == down, row, jnp.zeros_like(row)), axis=1, keepdims=True)


def as_row(column):
    count = column.shape[0]
    across = lax.broadcasted_iota(jnp.int32, (count, count), 1)
    down = lax.broadcasted_iota(jnp.int32, (count, count), 0)
    return jnp.sum(jnp.where(across == down, column, jnp.zeros_like(column)), axis=0, keepdims=True)


LANES = 128
PART = 16


def row_parts(count):
    return [pl.ds(start, PART) for start in range(0, count, PART)]


def arrange_kernel(ids_hbm, rows_hbm, out_ref, moves_ref, ids_out_ref, ids_ref, rows_ref, sems):
    count = rows_ref.shape[0]
    ids_copy = pltpu.make_async_copy(ids_hbm, ids_ref, sems.at[0])
    rows_copies = [
        pltpu.make_async_copy(rows_hbm.at[part], rows_ref.at[part], sems.at[index + 1])
        for index, part in enumerate(row_parts(count))
    ]
    for copy in (ids_copy, *rows_copies):
        copy.start()
    ids_copy.wait()
    ids_row = ids_ref[...].reshape(1, count)
    ids_column = as_column(ids_row)
    across = lax.broadcasted_iota(jnp.int32, (count, count), 1)
    down = lax.broadcasted_iota(jnp.int32, (count, count), 0)
    before = (ids_column < ids_row) | ((ids_column == ids_row) & (down < across))
    rank_row = jnp.sum(before.astype(jnp.int32), axis=0, keepdims=True)
    moves = (down == rank_row).astype(jnp.bfloat16)
    unit = []
    for copy, part in zip(rows_copies, row_parts(count)):
        copy.wait()
        unit.append(normalize_rows(rows_ref[part, :]))
    unit = jnp.concatenate(unit, axis=0)
    out_ref[...] = jnp.dot(moves, unit, preferred_element_type=jnp.float32).astype(jnp.bfloat16)
    moves_ref[...] = moves
    ids_out_ref[...] = ids_row


def partial_sums(queries, keys, bounds, own):
    count = bounds.shape[0]
    blocks = queries.shape[0] // count
    similar = lax.dot_general(
        queries, keys, (((1,), (1,)), ((), ())), preferred_element_type=jnp.float32
    )
    bounds = jnp.concatenate([bounds] * blocks, axis=0)
    key = lax.broadcasted_iota(jnp.int32, similar.shape, 1)
    place = lax.rem(key, count)
    allowed = (place >= bounds[:, 0:1]) & (place < bounds[:, 1:2])
    if own:
        query = lax.broadcasted_iota(jnp.int32, similar.shape, 0)
        allowed = allowed & ((key != query) | (key >= count))
    weights = jnp.where(allowed, jnp.exp(sharpness * (similar - 1.0)), 0.0)
    totals = jnp.sum(weights, axis=1, keepdims=True)
    return totals, jnp.dot(weights.astype(jnp.bfloat16), keys, preferred_element_type=jnp.float32)


def first_kernel(moves_ref, ids_ref, own_ref, beside_ref, *refs):
    *key_refs, weighted_ref, totals_ref, bounds_ref = refs
    ids = ids_ref[...]
    label = jnp.sum(jnp.where(moves_ref[...] > 0, ids, 0), axis=1, keepdims=True)
    first = jnp.sum((ids < label).astype(jnp.int32), axis=1, keepdims=True)
    after = jnp.sum((ids <= label).astype(jnp.int32), axis=1, keepdims=True)
    lane = lax.broadcasted_iota(jnp.int32, bounds_ref.shape, 1)
    bounds = jnp.where(lane == 0, first, after)
    bounds_ref[...] = bounds
    queries = jnp.concatenate([own_ref[...], beside_ref[...]], axis=0)
    keys = jnp.concatenate([ref[...] for ref in key_refs], axis=0)
    totals, weighted = partial_sums(queries, keys, bounds, True)
    weighted_ref[...] = weighted
    totals_ref[...] = jnp.broadcast_to(totals, totals_ref.shape)


def beside_kernel(so_far_ref, totals_so_far_ref, bounds_ref, beside_ref, keys_ref, out_ref):
    count = beside_ref.shape[0]
    totals, weighted = partial_sums(beside_ref[...], keys_ref[...], bounds_ref[...], False)
    weighted = (weighted + so_far_ref[count:, :]).astype(jnp.bfloat16)
    columns = weighted.shape[1] // LANES
    for index in range(columns):
        out_ref[index * count : (index + 1) * count, :] = weighted[
            :, index * LANES : (index + 1) * LANES
        ]
    totals = as_row(totals + totals_so_far_ref[count:, 0:1])
    totals = jnp.concatenate([totals, jnp.zeros((1, LANES - count), jnp.float32)], axis=1)
    high = totals.astype(jnp.bfloat16).astype(jnp.float32)
    row = lax.broadcasted_iota(jnp.int32, (EXTRA, LANES), 0)
    out_ref[columns * count :, :] = jnp.where(row == 0, high, totals - high).astype(jnp.bfloat16)


def own_kernel(so_far_ref, totals_so_far_ref, bounds_ref, own_ref, keys_ref, weighted_ref, totals_ref):
    count = own_ref.shape[0]
    totals, weighted = partial_sums(own_ref[...], keys_ref[...], bounds_ref[...], False)
    weighted_ref[...] = weighted + so_far_ref[:count, :]
    totals_ref[...] = as_row(totals + totals_so_far_ref[:count, 0:1])


def finish_kernel(
    moves_ref,
    weighted_ref,
    totals_ref,
    back_ref,
    neighbour_hbm,
    score_hbm,
    neighbour_ref,
    score_ref,
    sems,
):
    count, features = neighbour_ref.shape
    columns = features // LANES
    back = [
        back_ref[index * count : (index + 1) * count, :].astype(jnp.float32)
        for index in range(columns)
    ]
    weighted = weighted_ref[...] + jnp.concatenate(back, axis=1)
    normed = (
        weighted * lax.rsqrt(jnp.mean(weighted * weighted, axis=-1, keepdims=True) + epsilon)
    ).astype(jnp.bfloat16)
    moves = moves_ref[...]
    neighbour_ref[...] = lax.dot_general(
        moves, normed, (((0,), (0,)), ((), ())), preferred_element_type=jnp.float32
    ).astype(jnp.bfloat16)
    copies = [
        pltpu.make_async_copy(neighbour_ref.at[part], neighbour_hbm.at[part], sems.at[index])
        for index, part in enumerate(row_parts(count))
    ]
    for copy in copies:
        copy.start()
    pair = back_ref[columns * count :, :].astype(jnp.float32)
    totals = totals_ref[...] + (pair[0:1, :count] + pair[1:2, :count])
    scores = jnp.sum(moves.astype(jnp.float32) * as_column(jnp.log(totals)), axis=0, keepdims=True)
    score_ref[...] = scores.astype(jnp.bfloat16).reshape(count)
    copies.append(pltpu.make_async_copy(score_ref, score_hbm, sems.at[len(copies)]))
    copies[-1].start()
    for copy in copies:
        copy.wait()


EXTRA = 16
CORE, ACROSS, NEAR, FAR = 1, 2, 4, 8
GRID = 16


def gathered_body(embeddings, cluster_id):
    rows_dev, features = embeddings.shape
    vmem = pl.BlockSpec(memory_space=pltpu.VMEM)
    stored = pl.BlockSpec(memory_space=pltpu.HBM)

    def swap(value, bits):
        return lax.ppermute(value, "blk", [(device, device ^ bits) for device in range(GRID)])

    def block(kind, *shape):
        return jax.ShapeDtypeStruct(shape, kind)

    def kernel(body, name, out_shape, *inputs, specs=vmem, out_specs=vmem, scratch=()):
        return pl.pallas_call(
            body,
            out_shape=out_shape,
            in_specs=[specs] * len(inputs),
            out_specs=(out_specs,) * len(out_shape),
            scratch_shapes=scratch,
            compiler_params=pltpu.CompilerParams(vmem_limit_bytes=32 * 1024 * 1024),
            name=name,
        )(*inputs)

    rows = block(jnp.bfloat16, rows_dev, features)
    own, moves, ids = kernel(
        arrange_kernel,
        "arrange",
        (rows, block(jnp.bfloat16, rows_dev, rows_dev), block(jnp.int32, 1, rows_dev)),
        pltpu.with_memory_space_constraint(cluster_id, pltpu.HBM),
        pltpu.with_memory_space_constraint(embeddings, pltpu.HBM),
        specs=stored,
        scratch=(
            pltpu.VMEM((rows_dev,), jnp.int32),
            pltpu.VMEM((rows_dev, features), jnp.bfloat16),
            pltpu.SemaphoreType.DMA((1 + rows_dev // PART,)),
        ),
    )

    far, farther, near, beside, mate = lax.optimization_barrier(
        tuple(swap(own, bits) for bits in (FAR, FAR | NEAR, NEAR, ACROSS, CORE))
    )
    mates = swap(jnp.concatenate([near, far, farther], axis=0), CORE)
    *so_far, bounds = kernel(
        first_kernel,
        "first",
        (
            block(jnp.float32, 2 * rows_dev, features),
            block(jnp.float32, 2 * rows_dev, LANES),
            block(jnp.int32, rows_dev, LANES),
        ),
        *(moves, ids, own, beside),
        *(own, mate, near, far, farther),
    )
    (partial,) = kernel(
        beside_kernel,
        "beside",
        (block(jnp.bfloat16, rows_dev * features // LANES + EXTRA, LANES),),
        *(*so_far, bounds, beside, mates),
    )
    back = swap(partial, ACROSS)
    weighted, totals = kernel(
        own_kernel,
        "own",
        (block(jnp.float32, rows_dev, features), block(jnp.float32, 1, rows_dev)),
        *(*so_far, bounds, own, mates),
    )
    return tuple(
        kernel(
            finish_kernel,
            "finish",
            (rows, block(jnp.bfloat16, rows_dev)),
            *(moves, weighted, totals, back),
            out_specs=stored,
            scratch=(
                pltpu.VMEM((rows_dev, features), jnp.bfloat16),
                pltpu.VMEM((rows_dev,), jnp.bfloat16),
                pltpu.SemaphoreType.DMA((1 + rows_dev // PART,)),
            ),
        )
    )


def from_behind(value, axis, steps):
    count = lax.axis_size(axis)
    initial, last = (max(0, -steps), min(count, count - steps))
    return lax.ppermute(value, axis, [(source, source + steps) for source in range(initial, last)])


def pair_terms(queries, visiting, allowed):
    similar = jnp.dot(queries, visiting.T, preferred_element_type=jnp.float32)
    return jnp.where(allowed, jnp.exp(sharpness * (similar - 1.0)), jnp.zeros_like(similar))


def finish(weighted, totals):
    normed = (
        weighted * lax.rsqrt(jnp.mean(weighted * weighted, axis=-1, keepdims=True) + epsilon)
    ).astype(jnp.bfloat16)
    return (normed, jnp.log(totals).astype(jnp.bfloat16))


def collected_body(embeddings, cluster_id):
    rows_dev, features = embeddings.shape
    devices = lax.axis_size("blk")
    per_peer = rows_dev // devices
    clusters = devices // 4
    unit_rows = normalize_rows(embeddings)
    labels = jnp.arange(clusters, dtype=jnp.int32)
    counts = jnp.sum((cluster_id[:, None] == labels[None, :]).astype(jnp.int32), axis=0)
    group_ends = jnp.cumsum(counts // per_peer)

    def owner_cluster(device):
        in_range = (device >= 0) & (device < devices)
        return jnp.where(in_range, jnp.sum((device >= group_ends).astype(jnp.int32)), -1)

    position = jnp.arange(rows_dev, dtype=jnp.int32)
    arrange_order = jnp.argsort(cluster_id * rows_dev + position)
    inverse = jnp.argsort(arrange_order)
    arranged = unit_rows[arrange_order].reshape(devices, per_peer, features)
    held_rows = lax.all_to_all(arranged, "blk", split_axis=0, concat_axis=0, tiled=True).reshape(
        rows_dev, features
    )
    self_index = lax.axis_index("blk")
    mine = owner_cluster(self_index)
    weights = pair_terms(held_rows, held_rows, position[:, None] != position[None, :])
    totals = jnp.sum(weights, axis=1)
    weighted = jnp.dot(weights.astype(jnp.bfloat16), held_rows, preferred_element_type=jnp.float32)
    from_lower = held_rows
    from_upper = held_rows
    for distance in range(1, U_MAX):
        from_lower = from_behind(from_lower, "blk", 1)
        from_upper = from_behind(from_upper, "blk", -1)
        for visiting, source in (
            (from_lower, self_index - distance),
            (from_upper, self_index + distance),
        ):
            weights = pair_terms(held_rows, visiting, owner_cluster(source) == mine)
            totals = totals + jnp.sum(weights, axis=1)
            weighted = weighted + jnp.dot(
                weights.astype(jnp.bfloat16), visiting, preferred_element_type=jnp.float32
            )
    normed, scores = finish(weighted, totals)
    returned_rows, returned_scores = (
        lax.all_to_all(
            normed.reshape(devices, per_peer, features),
            "blk",
            split_axis=0,
            concat_axis=0,
            tiled=True,
        ),
        lax.all_to_all(
            scores.reshape(devices, per_peer), "blk", split_axis=0, concat_axis=0, tiled=True
        ),
    )
    neighbour = returned_rows.reshape(rows_dev, features)[inverse]
    dup_score = returned_scores.reshape(rows_dev)[inverse]
    return (neighbour, dup_score)


def solution(mesh):
    placed = (P(("groups", "blk"), None), P(("groups", "blk")))
    devices = mesh.shape["blk"]

    def body(embeddings, cluster_id):
        gathered = embeddings.size * embeddings.dtype.itemsize * devices
        fits = gathered <= GATHER_LIMIT and devices == GRID and embeddings.shape[0] % PART == 0
        plan = gathered_body if fits else collected_body
        return plan(embeddings, cluster_id)

    return jax.shard_map(
        body,
        mesh=mesh,
        in_specs=placed,
        out_specs=(P(("groups", "blk"), None), P(("groups", "blk"))),
        check_vma=False,
    )
```

```python
import jax
import jax.numpy as jnp
from jax import lax
from jax.experimental import pallas as pl
from jax.experimental.pallas import tpu as pltpu
from jax.sharding import PartitionSpec as P

U_MAX = 8
GATHER_LIMIT = 4 * 1024 * 1024


sharpness = 10.0
epsilon = 1e-06


def normalize_rows(values):
    widened = values.astype(jnp.float32)
    return (
        widened
        * lax.rsqrt(jnp.mean(widened * widened, axis=-1, keepdims=True) + epsilon)
        * widened.shape[-1] ** (-0.5)
    ).astype(jnp.bfloat16)


def as_column(row):
    count = row.shape[1]
    across = lax.broadcasted_iota(jnp.int32, (count, count), 1)
    down = lax.broadcasted_iota(jnp.int32, (count, count), 0)
    return jnp.sum(jnp.where(across == down, row, jnp.zeros_like(row)), axis=1, keepdims=True)


def as_row(column):
    count = column.shape[0]
    across = lax.broadcasted_iota(jnp.int32, (count, count), 1)
    down = lax.broadcasted_iota(jnp.int32, (count, count), 0)
    return jnp.sum(jnp.where(across == down, column, jnp.zeros_like(column)), axis=0, keepdims=True)


LANES = 128


def arrange_kernel(ids_hbm, rows_hbm, out_ref, moves_ref, ids_out_ref, ids_ref, rows_ref, sems):
    ids_copy = pltpu.make_async_copy(ids_hbm, ids_ref, sems.at[0])
    rows_copy = pltpu.make_async_copy(rows_hbm, rows_ref, sems.at[1])
    ids_copy.start()
    rows_copy.start()
    count = rows_ref.shape[0]
    ids_copy.wait()
    ids_row = ids_ref[...].reshape(1, count)
    ids_column = as_column(ids_row)
    across = lax.broadcasted_iota(jnp.int32, (count, count), 1)
    down = lax.broadcasted_iota(jnp.int32, (count, count), 0)
    before = (ids_column < ids_row) | ((ids_column == ids_row) & (down < across))
    rank_row = jnp.sum(before.astype(jnp.int32), axis=0, keepdims=True)
    moves = (down == rank_row).astype(jnp.bfloat16)
    rows_copy.wait()
    unit = normalize_rows(rows_ref[...])
    out_ref[...] = jnp.dot(moves, unit, preferred_element_type=jnp.float32).astype(jnp.bfloat16)
    moves_ref[...] = moves
    ids_out_ref[...] = ids_row


def pack(out_ref, weighted, totals):
    count = weighted.shape[0]
    weighted = weighted.astype(jnp.bfloat16)
    columns = weighted.shape[1] // LANES
    for index in range(columns):
        out_ref[index * count : (index + 1) * count, :] = weighted[
            :, index * LANES : (index + 1) * LANES
        ]
    totals = as_row(totals)
    totals = jnp.concatenate([totals, jnp.zeros((1, LANES - count), jnp.float32)], axis=1)
    high = totals.astype(jnp.bfloat16).astype(jnp.float32)
    row = lax.broadcasted_iota(jnp.int32, (EXTRA, LANES), 0)
    out_ref[columns * count :, :] = jnp.where(row == 0, high, totals - high).astype(jnp.bfloat16)


def unpack(packed_ref, count):
    columns = packed_ref.shape[0] // count
    block = [
        packed_ref[index * count : (index + 1) * count, :].astype(jnp.float32)
        for index in range(columns)
    ]
    pair = packed_ref[columns * count :, :].astype(jnp.float32)
    return jnp.concatenate(block, axis=1), pair[0:1, :count] + pair[1:2, :count]


def partial_sums(queries, keys, bounds, own):
    count = bounds.shape[0]
    blocks = queries.shape[0] // count
    similar = lax.dot_general(
        queries, keys, (((1,), (1,)), ((), ())), preferred_element_type=jnp.float32
    )
    bounds = jnp.concatenate([bounds] * blocks, axis=0)
    key = lax.broadcasted_iota(jnp.int32, similar.shape, 1)
    place = lax.rem(key, count)
    allowed = (place >= bounds[:, 0:1]) & (place < bounds[:, 1:2])
    if own:
        query = lax.broadcasted_iota(jnp.int32, similar.shape, 0)
        allowed = allowed & ((key != query) | (key >= count))
    weights = jnp.where(allowed, jnp.exp(sharpness * (similar - 1.0)), 0.0)
    totals = jnp.sum(weights, axis=1, keepdims=True)
    return totals, jnp.dot(weights.astype(jnp.bfloat16), keys, preferred_element_type=jnp.float32)


def visitor_kernel(moves_ref, ids_ref, visitor_ref, own_ref, beside_ref, mates_ref, out_ref, bounds_ref):
    ids = ids_ref[...]
    label = jnp.sum(jnp.where(moves_ref[...] > 0, ids, 0), axis=1, keepdims=True)
    first = jnp.sum((ids < label).astype(jnp.int32), axis=1, keepdims=True)
    after = jnp.sum((ids <= label).astype(jnp.int32), axis=1, keepdims=True)
    lane = lax.broadcasted_iota(jnp.int32, bounds_ref.shape, 1)
    bounds = jnp.where(lane == 0, first, after)
    bounds_ref[...] = bounds
    keys = jnp.concatenate([own_ref[...], beside_ref[...], mates_ref[...]], axis=0)
    totals, weighted = partial_sums(visitor_ref[...], keys, bounds, False)
    pack(out_ref, weighted, totals)


def first_kernel(bounds_ref, own_ref, beside_ref, mates_ref, *refs):
    *key_refs, weighted_ref, totals_ref = refs
    own = own_ref[...]
    queries = jnp.concatenate([own, beside_ref[...]], axis=0)
    mate = mates_ref[: own.shape[0], :]
    keys = jnp.concatenate([own, mate, *(ref[...] for ref in key_refs)], axis=0)
    totals, weighted = partial_sums(queries, keys, bounds_ref[...], True)
    weighted_ref[...] = weighted
    totals_ref[...] = jnp.broadcast_to(totals, totals_ref.shape)


def beside_kernel(so_far_ref, totals_so_far_ref, bounds_ref, beside_ref, keys_ref, out_ref):
    count = beside_ref.shape[0]
    totals, weighted = partial_sums(beside_ref[...], keys_ref[...], bounds_ref[...], False)
    pack(out_ref, weighted + so_far_ref[count:, :], totals + totals_so_far_ref[count:, 0:1])


def own_kernel(so_far_ref, totals_so_far_ref, bounds_ref, own_ref, keys_ref, weighted_ref, totals_ref):
    count = own_ref.shape[0]
    totals, weighted = partial_sums(own_ref[...], keys_ref[...], bounds_ref[...], False)
    weighted_ref[...] = weighted + so_far_ref[:count, :]
    totals_ref[...] = as_row(totals + totals_so_far_ref[:count, 0:1])


def finish_kernel(moves_ref, weighted_ref, totals_ref, *refs):
    *back_refs, neighbour_hbm, score_hbm, neighbour_ref, score_ref, sems = refs
    count = neighbour_ref.shape[0]
    weighted, totals = weighted_ref[...], totals_ref[...]
    for back_ref in back_refs:
        back, back_totals = unpack(back_ref, count)
        weighted = weighted + back
        totals = totals + back_totals
    normed = (
        weighted * lax.rsqrt(jnp.mean(weighted * weighted, axis=-1, keepdims=True) + epsilon)
    ).astype(jnp.bfloat16)
    moves = moves_ref[...]
    neighbour_ref[...] = lax.dot_general(
        moves, normed, (((0,), (0,)), ((), ())), preferred_element_type=jnp.float32
    ).astype(jnp.bfloat16)
    neighbour_copy = pltpu.make_async_copy(neighbour_ref, neighbour_hbm, sems.at[0])
    neighbour_copy.start()
    scores = jnp.sum(moves.astype(jnp.float32) * as_column(jnp.log(totals)), axis=0, keepdims=True)
    score_ref[...] = scores.astype(jnp.bfloat16).reshape(count)
    score_copy = pltpu.make_async_copy(score_ref, score_hbm, sems.at[1])
    score_copy.start()
    neighbour_copy.wait()
    score_copy.wait()


EXTRA = 16
CORE, ACROSS, MIRROR = 1, 2, 12
PLANE, GRID = 4, 16
LOW, HIGH = (0, 1), (2, 3)
NEXT = (2, 0, 3, 1)


def gathered_body(embeddings, cluster_id):
    rows_dev, features = embeddings.shape
    vmem = pl.BlockSpec(memory_space=pltpu.VMEM)
    stored = pl.BlockSpec(memory_space=pltpu.HBM)

    def swap(value, bits):
        return lax.ppermute(value, "blk", [(device, device ^ bits) for device in range(GRID)])

    def swap_some(value, bits, planes):
        pairs = [
            (device, device ^ bits if device // PLANE in planes else device)
            for device in range(GRID)
        ]
        return lax.ppermute(value, "blk", pairs)

    def visit(value, home):
        pairs = [
            (device, NEXT[device // PLANE] * PLANE + device % PLANE) for device in range(GRID)
        ]
        return lax.ppermute(value, "blk", [pair[::-1] for pair in pairs] if home else pairs)

    def block(kind, *shape):
        return jax.ShapeDtypeStruct(shape, kind)

    def kernel(body, name, out_shape, *inputs, specs=vmem, out_specs=vmem, scratch=()):
        return pl.pallas_call(
            body,
            out_shape=out_shape,
            in_specs=[specs] * len(inputs),
            out_specs=(out_specs,) * len(out_shape),
            scratch_shapes=scratch,
            compiler_params=pltpu.CompilerParams(vmem_limit_bytes=32 * 1024 * 1024),
            name=name,
        )(*inputs)

    rows = block(jnp.bfloat16, rows_dev, features)
    own, moves, ids = kernel(
        arrange_kernel,
        "arrange",
        (rows, block(jnp.bfloat16, rows_dev, rows_dev), block(jnp.int32, 1, rows_dev)),
        pltpu.with_memory_space_constraint(cluster_id, pltpu.HBM),
        pltpu.with_memory_space_constraint(embeddings, pltpu.HBM),
        specs=stored,
        scratch=(
            pltpu.VMEM((rows_dev,), jnp.int32),
            pltpu.VMEM((rows_dev, features), jnp.bfloat16),
            pltpu.SemaphoreType.DMA((2,)),
        ),
    )

    packed = block(jnp.bfloat16, rows_dev * features // LANES + EXTRA, LANES)
    half = swap_some(own, ACROSS, LOW)
    visitor, mirror, beside = lax.optimization_barrier((visit(own, home=False), swap(own, MIRROR), swap_some(half, ACROSS, HIGH)))
    mates = swap(jnp.concatenate([own, beside], axis=0), CORE)
    later = swap(jnp.concatenate([mirror, visitor], axis=0), CORE)
    partial, bounds = kernel(
        visitor_kernel,
        "visitor",
        (packed, block(jnp.int32, rows_dev, LANES)),
        *(moves, ids, visitor, own, beside, mates),
    )
    back_home = visit(partial, home=True)
    so_far = kernel(
        first_kernel,
        "first",
        (block(jnp.float32, 2 * rows_dev, features), block(jnp.float32, 2 * rows_dev, LANES)),
        *(bounds, own, beside, mates, mirror, visitor),
    )
    (partial,) = kernel(beside_kernel, "beside", (packed,), *so_far, bounds, beside, later)
    back = swap(partial, ACROSS)
    weighted, totals = kernel(
        own_kernel,
        "own",
        (block(jnp.float32, rows_dev, features), block(jnp.float32, 1, rows_dev)),
        *(*so_far, bounds, own, later),
    )
    weighted, back_home = lax.optimization_barrier((weighted, back_home))
    return tuple(
        kernel(
            finish_kernel,
            "finish",
            (rows, block(jnp.bfloat16, rows_dev)),
            *(moves, weighted, totals, back, back_home),
            out_specs=stored,
            scratch=(
                pltpu.VMEM((rows_dev, features), jnp.bfloat16),
                pltpu.VMEM((rows_dev,), jnp.bfloat16),
                pltpu.SemaphoreType.DMA((2,)),
            ),
        )
    )


def from_behind(value, axis, steps):
    count = lax.axis_size(axis)
    initial, last = (max(0, -steps), min(count, count - steps))
    return lax.ppermute(value, axis, [(source, source + steps) for source in range(initial, last)])


def pair_terms(queries, visiting, allowed):
    similar = jnp.dot(queries, visiting.T, preferred_element_type=jnp.float32)
    return jnp.where(allowed, jnp.exp(sharpness * (similar - 1.0)), jnp.zeros_like(similar))


def finish(weighted, totals):
    normed = (
        weighted * lax.rsqrt(jnp.mean(weighted * weighted, axis=-1, keepdims=True) + epsilon)
    ).astype(jnp.bfloat16)
    return (normed, jnp.log(totals).astype(jnp.bfloat16))


def collected_body(embeddings, cluster_id):
    rows_dev, features = embeddings.shape
    devices = lax.axis_size("blk")
    per_peer = rows_dev // devices
    clusters = devices // 4
    unit_rows = normalize_rows(embeddings)
    labels = jnp.arange(clusters, dtype=jnp.int32)
    counts = jnp.sum((cluster_id[:, None] == labels[None, :]).astype(jnp.int32), axis=0)
    group_ends = jnp.cumsum(counts // per_peer)

    def owner_cluster(device):
        in_range = (device >= 0) & (device < devices)
        return jnp.where(in_range, jnp.sum((device >= group_ends).astype(jnp.int32)), -1)

    position = jnp.arange(rows_dev, dtype=jnp.int32)
    arrange_order = jnp.argsort(cluster_id * rows_dev + position)
    inverse = jnp.argsort(arrange_order)
    arranged = unit_rows[arrange_order].reshape(devices, per_peer, features)
    held_rows = lax.all_to_all(arranged, "blk", split_axis=0, concat_axis=0, tiled=True).reshape(
        rows_dev, features
    )
    self_index = lax.axis_index("blk")
    mine = owner_cluster(self_index)
    weights = pair_terms(held_rows, held_rows, position[:, None] != position[None, :])
    totals = jnp.sum(weights, axis=1)
    weighted = jnp.dot(weights.astype(jnp.bfloat16), held_rows, preferred_element_type=jnp.float32)
    from_lower = held_rows
    from_upper = held_rows
    for distance in range(1, U_MAX):
        from_lower = from_behind(from_lower, "blk", 1)
        from_upper = from_behind(from_upper, "blk", -1)
        for visiting, source in (
            (from_lower, self_index - distance),
            (from_upper, self_index + distance),
        ):
            weights = pair_terms(held_rows, visiting, owner_cluster(source) == mine)
            totals = totals + jnp.sum(weights, axis=1)
            weighted = weighted + jnp.dot(
                weights.astype(jnp.bfloat16), visiting, preferred_element_type=jnp.float32
            )
    normed, scores = finish(weighted, totals)
    returned_rows, returned_scores = (
        lax.all_to_all(
            normed.reshape(devices, per_peer, features),
            "blk",
            split_axis=0,
            concat_axis=0,
            tiled=True,
        ),
        lax.all_to_all(
            scores.reshape(devices, per_peer), "blk", split_axis=0, concat_axis=0, tiled=True
        ),
    )
    neighbour = returned_rows.reshape(rows_dev, features)[inverse]
    dup_score = returned_scores.reshape(rows_dev)[inverse]
    return (neighbour, dup_score)


def solution(mesh):
    placed = (P(("groups", "blk"), None), P(("groups", "blk")))
    devices = mesh.shape["blk"]

    def body(embeddings, cluster_id):
        gathered = embeddings.size * embeddings.dtype.itemsize * devices
        fits = gathered <= GATHER_LIMIT and devices == GRID
        plan = gathered_body if fits else collected_body
        return plan(embeddings, cluster_id)

    return jax.shard_map(
        body,
        mesh=mesh,
        in_specs=placed,
        out_specs=(P(("groups", "blk"), None), P(("groups", "blk"))),
        check_vma=False,
    )
```

```python
import jax
import jax.numpy as jnp
from jax import lax
from jax.experimental import pallas as pl
from jax.experimental.pallas import tpu as pltpu
from jax.sharding import PartitionSpec as P

U_MAX = 8
GATHER_LIMIT = 4 * 1024 * 1024


sharpness = 10.0
epsilon = 1e-06


def normalize_rows(values):
    widened = values.astype(jnp.float32)
    return (
        widened
        * lax.rsqrt(jnp.mean(widened * widened, axis=-1, keepdims=True) + epsilon)
        * widened.shape[-1] ** (-0.5)
    ).astype(jnp.bfloat16)


def as_column(row):
    count = row.shape[1]
    across = lax.broadcasted_iota(jnp.int32, (count, count), 1)
    down = lax.broadcasted_iota(jnp.int32, (count, count), 0)
    return jnp.sum(jnp.where(across == down, row, jnp.zeros_like(row)), axis=1, keepdims=True)


def as_row(column):
    count = column.shape[0]
    across = lax.broadcasted_iota(jnp.int32, (count, count), 1)
    down = lax.broadcasted_iota(jnp.int32, (count, count), 0)
    return jnp.sum(jnp.where(across == down, column, jnp.zeros_like(column)), axis=0, keepdims=True)


LANES = 128


def arrange_kernel(ids_hbm, rows_hbm, out_ref, moves_ref, ids_out_ref, ids_ref, rows_ref, sems):
    ids_copy = pltpu.make_async_copy(ids_hbm, ids_ref, sems.at[0])
    rows_copy = pltpu.make_async_copy(rows_hbm, rows_ref, sems.at[1])
    ids_copy.start()
    rows_copy.start()
    count = rows_ref.shape[0]
    ids_copy.wait()
    ids_row = ids_ref[...].reshape(1, count)
    ids_column = as_column(ids_row)
    across = lax.broadcasted_iota(jnp.int32, (count, count), 1)
    down = lax.broadcasted_iota(jnp.int32, (count, count), 0)
    before = (ids_column < ids_row) | ((ids_column == ids_row) & (down < across))
    rank_row = jnp.sum(before.astype(jnp.int32), axis=0, keepdims=True)
    moves = (down == rank_row).astype(jnp.bfloat16)
    rows_copy.wait()
    unit = normalize_rows(rows_ref[...])
    out_ref[...] = jnp.dot(moves, unit, preferred_element_type=jnp.float32).astype(jnp.bfloat16)
    moves_ref[...] = moves
    ids_out_ref[...] = ids_row


def partial_sums(queries, keys, bounds, own):
    count = bounds.shape[0]
    blocks = queries.shape[0] // count
    similar = lax.dot_general(
        queries, keys, (((1,), (1,)), ((), ())), preferred_element_type=jnp.float32
    )
    bounds = jnp.concatenate([bounds] * blocks, axis=0)
    key = lax.broadcasted_iota(jnp.int32, similar.shape, 1)
    place = lax.rem(key, count)
    allowed = (place >= bounds[:, 0:1]) & (place < bounds[:, 1:2])
    if own:
        query = lax.broadcasted_iota(jnp.int32, similar.shape, 0)
        allowed = allowed & ((key != query) | (key >= count))
    weights = jnp.where(allowed, jnp.exp(sharpness * (similar - 1.0)), 0.0)
    totals = jnp.sum(weights, axis=1, keepdims=True)
    return totals, jnp.dot(weights.astype(jnp.bfloat16), keys, preferred_element_type=jnp.float32)


def first_kernel(moves_ref, ids_ref, own_ref, beside_ref, *refs):
    *key_refs, weighted_ref, totals_ref, bounds_ref = refs
    ids = ids_ref[...]
    label = jnp.sum(jnp.where(moves_ref[...] > 0, ids, 0), axis=1, keepdims=True)
    first = jnp.sum((ids < label).astype(jnp.int32), axis=1, keepdims=True)
    after = jnp.sum((ids <= label).astype(jnp.int32), axis=1, keepdims=True)
    lane = lax.broadcasted_iota(jnp.int32, bounds_ref.shape, 1)
    bounds = jnp.where(lane == 0, first, after)
    bounds_ref[...] = bounds
    queries = jnp.concatenate([own_ref[...], beside_ref[...]], axis=0)
    keys = jnp.concatenate([ref[...] for ref in key_refs], axis=0)
    totals, weighted = partial_sums(queries, keys, bounds, True)
    weighted_ref[...] = weighted
    totals_ref[...] = jnp.broadcast_to(totals, totals_ref.shape)


def beside_kernel(so_far_ref, totals_so_far_ref, bounds_ref, beside_ref, keys_ref, out_ref):
    count = beside_ref.shape[0]
    totals, weighted = partial_sums(beside_ref[...], keys_ref[...], bounds_ref[...], False)
    weighted = (weighted + so_far_ref[count:, :]).astype(jnp.bfloat16)
    columns = weighted.shape[1] // LANES
    for index in range(columns):
        out_ref[index * count : (index + 1) * count, :] = weighted[
            :, index * LANES : (index + 1) * LANES
        ]
    totals = as_row(totals + totals_so_far_ref[count:, 0:1])
    totals = jnp.concatenate([totals, jnp.zeros((1, LANES - count), jnp.float32)], axis=1)
    high = totals.astype(jnp.bfloat16).astype(jnp.float32)
    row = lax.broadcasted_iota(jnp.int32, (EXTRA, LANES), 0)
    out_ref[columns * count :, :] = jnp.where(row == 0, high, totals - high).astype(jnp.bfloat16)


def own_kernel(so_far_ref, totals_so_far_ref, bounds_ref, own_ref, keys_ref, weighted_ref, totals_ref):
    count = own_ref.shape[0]
    totals, weighted = partial_sums(own_ref[...], keys_ref[...], bounds_ref[...], False)
    weighted_ref[...] = weighted + so_far_ref[:count, :]
    totals_ref[...] = as_row(totals + totals_so_far_ref[:count, 0:1])


def finish_kernel(
    moves_ref,
    weighted_ref,
    totals_ref,
    back_ref,
    neighbour_hbm,
    score_hbm,
    neighbour_ref,
    score_ref,
    sems,
):
    count, features = neighbour_ref.shape
    columns = features // LANES
    back = [
        back_ref[index * count : (index + 1) * count, :].astype(jnp.float32)
        for index in range(columns)
    ]
    weighted = weighted_ref[...] + jnp.concatenate(back, axis=1)
    normed = (
        weighted * lax.rsqrt(jnp.mean(weighted * weighted, axis=-1, keepdims=True) + epsilon)
    ).astype(jnp.bfloat16)
    moves = moves_ref[...]
    copies = []
    for half in range(2):
        part = slice(half * features // 2, (half + 1) * features // 2)
        neighbour_ref[:, part] = lax.dot_general(
            moves, normed[:, part], (((0,), (0,)), ((), ())), preferred_element_type=jnp.float32
        ).astype(jnp.bfloat16)
        copies.append(
            pltpu.make_async_copy(
                neighbour_ref.at[:, part], neighbour_hbm.at[:, part], sems.at[half]
            )
        )
        copies[-1].start()
    pair = back_ref[columns * count :, :].astype(jnp.float32)
    totals = totals_ref[...] + (pair[0:1, :count] + pair[1:2, :count])
    scores = jnp.sum(moves.astype(jnp.float32) * as_column(jnp.log(totals)), axis=0, keepdims=True)
    score_ref[...] = scores.astype(jnp.bfloat16).reshape(count)
    copies.append(pltpu.make_async_copy(score_ref, score_hbm, sems.at[2]))
    copies[-1].start()
    for copy in copies:
        copy.wait()


EXTRA = 16
CORE, ACROSS, NEAR, FAR = 1, 2, 4, 8
GRID = 16
Z_TURNS = ((FAR, FAR | NEAR, NEAR), (FAR | NEAR, NEAR, FAR))


def gathered_body(embeddings, cluster_id):
    rows_dev, features = embeddings.shape
    vmem = pl.BlockSpec(memory_space=pltpu.VMEM)
    stored = pl.BlockSpec(memory_space=pltpu.HBM)

    def swap(value, bits):
        pairs = [(device, device ^ bits[device & CORE]) for device in range(GRID)]
        return lax.ppermute(value, "blk", pairs)

    def block(kind, *shape):
        return jax.ShapeDtypeStruct(shape, kind)

    def kernel(body, name, out_shape, *inputs, specs=vmem, out_specs=vmem, scratch=()):
        return pl.pallas_call(
            body,
            out_shape=out_shape,
            in_specs=[specs] * len(inputs),
            out_specs=(out_specs,) * len(out_shape),
            scratch_shapes=scratch,
            compiler_params=pltpu.CompilerParams(vmem_limit_bytes=32 * 1024 * 1024),
            name=name,
        )(*inputs)

    rows = block(jnp.bfloat16, rows_dev, features)
    own, moves, ids = kernel(
        arrange_kernel,
        "arrange",
        (rows, block(jnp.bfloat16, rows_dev, rows_dev), block(jnp.int32, 1, rows_dev)),
        pltpu.with_memory_space_constraint(cluster_id, pltpu.HBM),
        pltpu.with_memory_space_constraint(embeddings, pltpu.HBM),
        specs=stored,
        scratch=(
            pltpu.VMEM((rows_dev,), jnp.int32),
            pltpu.VMEM((rows_dev, features), jnp.bfloat16),
            pltpu.SemaphoreType.DMA((2,)),
        ),
    )

    *visiting, beside, mate = lax.optimization_barrier(
        (*(swap(own, turn) for turn in zip(*Z_TURNS)), swap(own, (ACROSS,) * 2), swap(own, (CORE,) * 2))
    )
    mates = swap(jnp.concatenate(visiting, axis=0), (CORE,) * 2)
    *so_far, bounds = kernel(
        first_kernel,
        "first",
        (
            block(jnp.float32, 2 * rows_dev, features),
            block(jnp.float32, 2 * rows_dev, LANES),
            block(jnp.int32, rows_dev, LANES),
        ),
        *(moves, ids, own, beside),
        *(own, mate, *visiting),
    )
    (partial,) = kernel(
        beside_kernel,
        "beside",
        (block(jnp.bfloat16, rows_dev * features // LANES + EXTRA, LANES),),
        *(*so_far, bounds, beside, mates),
    )
    back = swap(partial, (ACROSS,) * 2)
    weighted, totals = kernel(
        own_kernel,
        "own",
        (block(jnp.float32, rows_dev, features), block(jnp.float32, 1, rows_dev)),
        *(*so_far, bounds, own, mates),
    )
    return tuple(
        kernel(
            finish_kernel,
            "finish",
            (rows, block(jnp.bfloat16, rows_dev)),
            *(moves, weighted, totals, back),
            out_specs=stored,
            scratch=(
                pltpu.VMEM((rows_dev, features), jnp.bfloat16),
                pltpu.VMEM((rows_dev,), jnp.bfloat16),
                pltpu.SemaphoreType.DMA((3,)),
            ),
        )
    )


def from_behind(value, axis, steps):
    count = lax.axis_size(axis)
    initial, last = (max(0, -steps), min(count, count - steps))
    return lax.ppermute(value, axis, [(source, source + steps) for source in range(initial, last)])


def pair_terms(queries, visiting, allowed):
    similar = jnp.dot(queries, visiting.T, preferred_element_type=jnp.float32)
    return jnp.where(allowed, jnp.exp(sharpness * (similar - 1.0)), jnp.zeros_like(similar))


def finish(weighted, totals):
    normed = (
        weighted * lax.rsqrt(jnp.mean(weighted * weighted, axis=-1, keepdims=True) + epsilon)
    ).astype(jnp.bfloat16)
    return (normed, jnp.log(totals).astype(jnp.bfloat16))


def collected_body(embeddings, cluster_id):
    rows_dev, features = embeddings.shape
    devices = lax.axis_size("blk")
    per_peer = rows_dev // devices
    clusters = devices // 4
    unit_rows = normalize_rows(embeddings)
    labels = jnp.arange(clusters, dtype=jnp.int32)
    counts = jnp.sum((cluster_id[:, None] == labels[None, :]).astype(jnp.int32), axis=0)
    group_ends = jnp.cumsum(counts // per_peer)

    def owner_cluster(device):
        in_range = (device >= 0) & (device < devices)
        return jnp.where(in_range, jnp.sum((device >= group_ends).astype(jnp.int32)), -1)

    position = jnp.arange(rows_dev, dtype=jnp.int32)
    arrange_order = jnp.argsort(cluster_id * rows_dev + position)
    inverse = jnp.argsort(arrange_order)
    arranged = unit_rows[arrange_order].reshape(devices, per_peer, features)
    held_rows = lax.all_to_all(arranged, "blk", split_axis=0, concat_axis=0, tiled=True).reshape(
        rows_dev, features
    )
    self_index = lax.axis_index("blk")
    mine = owner_cluster(self_index)
    weights = pair_terms(held_rows, held_rows, position[:, None] != position[None, :])
    totals = jnp.sum(weights, axis=1)
    weighted = jnp.dot(weights.astype(jnp.bfloat16), held_rows, preferred_element_type=jnp.float32)
    from_lower = held_rows
    from_upper = held_rows
    for distance in range(1, U_MAX):
        from_lower = from_behind(from_lower, "blk", 1)
        from_upper = from_behind(from_upper, "blk", -1)
        for visiting, source in (
            (from_lower, self_index - distance),
            (from_upper, self_index + distance),
        ):
            weights = pair_terms(held_rows, visiting, owner_cluster(source) == mine)
            totals = totals + jnp.sum(weights, axis=1)
            weighted = weighted + jnp.dot(
                weights.astype(jnp.bfloat16), visiting, preferred_element_type=jnp.float32
            )
    normed, scores = finish(weighted, totals)
    returned_rows, returned_scores = (
        lax.all_to_all(
            normed.reshape(devices, per_peer, features),
            "blk",
            split_axis=0,
            concat_axis=0,
            tiled=True,
        ),
        lax.all_to_all(
            scores.reshape(devices, per_peer), "blk", split_axis=0, concat_axis=0, tiled=True
        ),
    )
    neighbour = returned_rows.reshape(rows_dev, features)[inverse]
    dup_score = returned_scores.reshape(rows_dev)[inverse]
    return (neighbour, dup_score)


def solution(mesh):
    placed = (P(("groups", "blk"), None), P(("groups", "blk")))
    devices = mesh.shape["blk"]

    def body(embeddings, cluster_id):
        gathered = embeddings.size * embeddings.dtype.itemsize * devices
        fits = gathered <= GATHER_LIMIT and devices == GRID and embeddings.shape[0] % 16 == 0
        plan = gathered_body if fits else collected_body
        return plan(embeddings, cluster_id)

    return jax.shard_map(
        body,
        mesh=mesh,
        in_specs=placed,
        out_specs=(P(("groups", "blk"), None), P(("groups", "blk"))),
        check_vma=False,
    )
```

```python
import jax
import jax.numpy as jnp
from jax import lax
from jax.experimental import pallas as pl
from jax.experimental.pallas import tpu as pltpu
from jax.sharding import PartitionSpec as P

U_MAX = 8
GATHER_LIMIT = 4 * 1024 * 1024


sharpness = 10.0
epsilon = 1e-06


def normalize_rows(values):
    widened = values.astype(jnp.float32)
    return (
        widened
        * lax.rsqrt(jnp.mean(widened * widened, axis=-1, keepdims=True) + epsilon)
        * widened.shape[-1] ** (-0.5)
    ).astype(jnp.bfloat16)


def as_column(row):
    count = row.shape[1]
    across = lax.broadcasted_iota(jnp.int32, (count, count), 1)
    down = lax.broadcasted_iota(jnp.int32, (count, count), 0)
    return jnp.sum(jnp.where(across == down, row, jnp.zeros_like(row)), axis=1, keepdims=True)


def as_row(column):
    count = column.shape[0]
    across = lax.broadcasted_iota(jnp.int32, (count, count), 1)
    down = lax.broadcasted_iota(jnp.int32, (count, count), 0)
    return jnp.sum(jnp.where(across == down, column, jnp.zeros_like(column)), axis=0, keepdims=True)


LANES = 128


def arrange_kernel(ids_hbm, rows_hbm, out_ref, moves_ref, ids_out_ref, ids_ref, rows_ref, sems):
    ids_copy = pltpu.make_async_copy(ids_hbm, ids_ref, sems.at[0])
    rows_copy = pltpu.make_async_copy(rows_hbm, rows_ref, sems.at[1])
    ids_copy.start()
    rows_copy.start()
    count = rows_ref.shape[0]
    ids_copy.wait()
    ids_row = ids_ref[...].reshape(1, count)
    ids_column = as_column(ids_row)
    across = lax.broadcasted_iota(jnp.int32, (count, count), 1)
    down = lax.broadcasted_iota(jnp.int32, (count, count), 0)
    before = (ids_column < ids_row) | ((ids_column == ids_row) & (down < across))
    rank_row = jnp.sum(before.astype(jnp.int32), axis=0, keepdims=True)
    moves = (down == rank_row).astype(jnp.bfloat16)
    rows_copy.wait()
    unit = normalize_rows(rows_ref[...])
    out_ref[...] = jnp.dot(moves, unit, preferred_element_type=jnp.float32).astype(jnp.bfloat16)
    moves_ref[...] = moves
    ids_out_ref[...] = ids_row


def partial_sums(queries, keys, bounds, own):
    count = bounds.shape[0]
    blocks = queries.shape[0] // count
    similar = lax.dot_general(
        queries, keys, (((1,), (1,)), ((), ())), preferred_element_type=jnp.float32
    )
    bounds = jnp.concatenate([bounds] * blocks, axis=0)
    key = lax.broadcasted_iota(jnp.int32, similar.shape, 1)
    place = lax.rem(key, count)
    allowed = (place >= bounds[:, 0:1]) & (place < bounds[:, 1:2])
    if own:
        query = lax.broadcasted_iota(jnp.int32, similar.shape, 0)
        allowed = allowed & ((key != query) | (key >= count))
    weights = jnp.where(allowed, jnp.exp(sharpness * (similar - 1.0)), 0.0)
    totals = jnp.sum(weights, axis=1, keepdims=True)
    return totals, jnp.dot(weights.astype(jnp.bfloat16), keys, preferred_element_type=jnp.float32)


def first_kernel(moves_ref, ids_ref, own_ref, beside_ref, *refs):
    *key_refs, weighted_ref, totals_ref, bounds_ref = refs
    ids = ids_ref[...]
    label = jnp.sum(jnp.where(moves_ref[...] > 0, ids, 0), axis=1, keepdims=True)
    first = jnp.sum((ids < label).astype(jnp.int32), axis=1, keepdims=True)
    after = jnp.sum((ids <= label).astype(jnp.int32), axis=1, keepdims=True)
    lane = lax.broadcasted_iota(jnp.int32, bounds_ref.shape, 1)
    bounds = jnp.where(lane == 0, first, after)
    bounds_ref[...] = bounds
    queries = jnp.concatenate([own_ref[...], beside_ref[...]], axis=0)
    keys = jnp.concatenate([ref[...] for ref in key_refs], axis=0)
    totals, weighted = partial_sums(queries, keys, bounds, True)
    weighted_ref[...] = weighted
    totals_ref[...] = jnp.broadcast_to(totals, totals_ref.shape)


def beside_kernel(so_far_ref, totals_so_far_ref, bounds_ref, beside_ref, keys_ref, out_ref):
    count = beside_ref.shape[0]
    totals, weighted = partial_sums(beside_ref[...], keys_ref[...], bounds_ref[...], False)
    weighted = (weighted + so_far_ref[count:, :]).astype(jnp.bfloat16)
    columns = weighted.shape[1] // LANES
    for index in range(columns):
        out_ref[index * count : (index + 1) * count, :] = weighted[
            :, index * LANES : (index + 1) * LANES
        ]
    totals = as_row(totals + totals_so_far_ref[count:, 0:1])
    totals = jnp.concatenate([totals, jnp.zeros((1, LANES - count), jnp.float32)], axis=1)
    high = totals.astype(jnp.bfloat16).astype(jnp.float32)
    row = lax.broadcasted_iota(jnp.int32, (EXTRA, LANES), 0)
    out_ref[columns * count :, :] = jnp.where(row == 0, high, totals - high).astype(jnp.bfloat16)


def own_kernel(so_far_ref, totals_so_far_ref, bounds_ref, own_ref, keys_ref, weighted_ref, totals_ref):
    count = own_ref.shape[0]
    totals, weighted = partial_sums(own_ref[...], keys_ref[...], bounds_ref[...], False)
    weighted_ref[...] = weighted + so_far_ref[:count, :]
    totals_ref[...] = as_row(totals + totals_so_far_ref[:count, 0:1])


def finish_kernel(
    moves_ref,
    weighted_ref,
    totals_ref,
    back_ref,
    neighbour_hbm,
    score_hbm,
    neighbour_ref,
    score_ref,
    sems,
):
    count, features = neighbour_ref.shape
    columns = features // LANES
    back = [
        back_ref[index * count : (index + 1) * count, :].astype(jnp.float32)
        for index in range(columns)
    ]
    weighted = weighted_ref[...] + jnp.concatenate(back, axis=1)
    normed = (
        weighted * lax.rsqrt(jnp.mean(weighted * weighted, axis=-1, keepdims=True) + epsilon)
    ).astype(jnp.bfloat16)
    moves = moves_ref[...]
    copies = []
    for half in range(2):
        part = slice(half * features // 2, (half + 1) * features // 2)
        neighbour_ref[:, part] = lax.dot_general(
            moves, normed[:, part], (((0,), (0,)), ((), ())), preferred_element_type=jnp.float32
        ).astype(jnp.bfloat16)
        copies.append(
            pltpu.make_async_copy(
                neighbour_ref.at[:, part], neighbour_hbm.at[:, part], sems.at[half]
            )
        )
        copies[-1].start()
    pair = back_ref[columns * count :, :].astype(jnp.float32)
    totals = totals_ref[...] + (pair[0:1, :count] + pair[1:2, :count])
    scores = jnp.sum(moves.astype(jnp.float32) * as_column(jnp.log(totals)), axis=0, keepdims=True)
    score_ref[...] = scores.astype(jnp.bfloat16).reshape(count)
    copies.append(pltpu.make_async_copy(score_ref, score_hbm, sems.at[2]))
    copies[-1].start()
    for copy in copies:
        copy.wait()


EXTRA = 16
CORE, ACROSS = 1, 2
PLANE, GRID = 4, 16
Z_TURNS = ((2, 0, 3, 1), (3, 2, 1, 0), (1, 3, 0, 2))


def gathered_body(embeddings, cluster_id):
    rows_dev, features = embeddings.shape
    vmem = pl.BlockSpec(memory_space=pltpu.VMEM)
    stored = pl.BlockSpec(memory_space=pltpu.HBM)

    def swap(value, bits):
        return lax.ppermute(value, "blk", [(device, device ^ bits) for device in range(GRID)])

    def visit(value, planes):
        pairs = [
            (device, planes[device // PLANE] * PLANE + device % PLANE) for device in range(GRID)
        ]
        return lax.ppermute(value, "blk", pairs)

    def block(kind, *shape):
        return jax.ShapeDtypeStruct(shape, kind)

    def kernel(body, name, out_shape, *inputs, specs=vmem, out_specs=vmem, scratch=()):
        return pl.pallas_call(
            body,
            out_shape=out_shape,
            in_specs=[specs] * len(inputs),
            out_specs=(out_specs,) * len(out_shape),
            scratch_shapes=scratch,
            compiler_params=pltpu.CompilerParams(vmem_limit_bytes=32 * 1024 * 1024),
            name=name,
        )(*inputs)

    rows = block(jnp.bfloat16, rows_dev, features)
    own, moves, ids = kernel(
        arrange_kernel,
        "arrange",
        (rows, block(jnp.bfloat16, rows_dev, rows_dev), block(jnp.int32, 1, rows_dev)),
        pltpu.with_memory_space_constraint(cluster_id, pltpu.HBM),
        pltpu.with_memory_space_constraint(embeddings, pltpu.HBM),
        specs=stored,
        scratch=(
            pltpu.VMEM((rows_dev,), jnp.int32),
            pltpu.VMEM((rows_dev, features), jnp.bfloat16),
            pltpu.SemaphoreType.DMA((2,)),
        ),
    )

    *visiting, beside, mate = lax.optimization_barrier(
        (*(visit(own, planes) for planes in Z_TURNS), swap(own, ACROSS), swap(own, CORE))
    )
    mates = swap(jnp.concatenate(visiting, axis=0), CORE)
    *so_far, bounds = kernel(
        first_kernel,
        "first",
        (
            block(jnp.float32, 2 * rows_dev, features),
            block(jnp.float32, 2 * rows_dev, LANES),
            block(jnp.int32, rows_dev, LANES),
        ),
        *(moves, ids, own, beside),
        *(own, mate, *visiting),
    )
    (partial,) = kernel(
        beside_kernel,
        "beside",
        (block(jnp.bfloat16, rows_dev * features // LANES + EXTRA, LANES),),
        *(*so_far, bounds, beside, mates),
    )
    back = swap(partial, ACROSS)
    weighted, totals = kernel(
        own_kernel,
        "own",
        (block(jnp.float32, rows_dev, features), block(jnp.float32, 1, rows_dev)),
        *(*so_far, bounds, own, mates),
    )
    return tuple(
        kernel(
            finish_kernel,
            "finish",
            (rows, block(jnp.bfloat16, rows_dev)),
            *(moves, weighted, totals, back),
            out_specs=stored,
            scratch=(
                pltpu.VMEM((rows_dev, features), jnp.bfloat16),
                pltpu.VMEM((rows_dev,), jnp.bfloat16),
                pltpu.SemaphoreType.DMA((3,)),
            ),
        )
    )


def from_behind(value, axis, steps):
    count = lax.axis_size(axis)
    initial, last = (max(0, -steps), min(count, count - steps))
    return lax.ppermute(value, axis, [(source, source + steps) for source in range(initial, last)])


def pair_terms(queries, visiting, allowed):
    similar = jnp.dot(queries, visiting.T, preferred_element_type=jnp.float32)
    return jnp.where(allowed, jnp.exp(sharpness * (similar - 1.0)), jnp.zeros_like(similar))


def finish(weighted, totals):
    normed = (
        weighted * lax.rsqrt(jnp.mean(weighted * weighted, axis=-1, keepdims=True) + epsilon)
    ).astype(jnp.bfloat16)
    return (normed, jnp.log(totals).astype(jnp.bfloat16))


def collected_body(embeddings, cluster_id):
    rows_dev, features = embeddings.shape
    devices = lax.axis_size("blk")
    per_peer = rows_dev // devices
    clusters = devices // 4
    unit_rows = normalize_rows(embeddings)
    labels = jnp.arange(clusters, dtype=jnp.int32)
    counts = jnp.sum((cluster_id[:, None] == labels[None, :]).astype(jnp.int32), axis=0)
    group_ends = jnp.cumsum(counts // per_peer)

    def owner_cluster(device):
        in_range = (device >= 0) & (device < devices)
        return jnp.where(in_range, jnp.sum((device >= group_ends).astype(jnp.int32)), -1)

    position = jnp.arange(rows_dev, dtype=jnp.int32)
    arrange_order = jnp.argsort(cluster_id * rows_dev + position)
    inverse = jnp.argsort(arrange_order)
    arranged = unit_rows[arrange_order].reshape(devices, per_peer, features)
    held_rows = lax.all_to_all(arranged, "blk", split_axis=0, concat_axis=0, tiled=True).reshape(
        rows_dev, features
    )
    self_index = lax.axis_index("blk")
    mine = owner_cluster(self_index)
    weights = pair_terms(held_rows, held_rows, position[:, None] != position[None, :])
    totals = jnp.sum(weights, axis=1)
    weighted = jnp.dot(weights.astype(jnp.bfloat16), held_rows, preferred_element_type=jnp.float32)
    from_lower = held_rows
    from_upper = held_rows
    for distance in range(1, U_MAX):
        from_lower = from_behind(from_lower, "blk", 1)
        from_upper = from_behind(from_upper, "blk", -1)
        for visiting, source in (
            (from_lower, self_index - distance),
            (from_upper, self_index + distance),
        ):
            weights = pair_terms(held_rows, visiting, owner_cluster(source) == mine)
            totals = totals + jnp.sum(weights, axis=1)
            weighted = weighted + jnp.dot(
                weights.astype(jnp.bfloat16), visiting, preferred_element_type=jnp.float32
            )
    normed, scores = finish(weighted, totals)
    returned_rows, returned_scores = (
        lax.all_to_all(
            normed.reshape(devices, per_peer, features),
            "blk",
            split_axis=0,
            concat_axis=0,
            tiled=True,
        ),
        lax.all_to_all(
            scores.reshape(devices, per_peer), "blk", split_axis=0, concat_axis=0, tiled=True
        ),
    )
    neighbour = returned_rows.reshape(rows_dev, features)[inverse]
    dup_score = returned_scores.reshape(rows_dev)[inverse]
    return (neighbour, dup_score)


def solution(mesh):
    placed = (P(("groups", "blk"), None), P(("groups", "blk")))
    devices = mesh.shape["blk"]

    def body(embeddings, cluster_id):
        gathered = embeddings.size * embeddings.dtype.itemsize * devices
        fits = gathered <= GATHER_LIMIT and devices == GRID and embeddings.shape[0] % 16 == 0
        plan = gathered_body if fits else collected_body
        return plan(embeddings, cluster_id)

    return jax.shard_map(
        body,
        mesh=mesh,
        in_specs=placed,
        out_specs=(P(("groups", "blk"), None), P(("groups", "blk"))),
        check_vma=False,
    )
```

```python
import jax
import jax.numpy as jnp
from jax import lax
from jax.experimental import pallas as pl
from jax.experimental.pallas import tpu as pltpu
from jax.sharding import PartitionSpec as P

U_MAX = 8
GATHER_LIMIT = 4 * 1024 * 1024


sharpness = 10.0
epsilon = 1e-06


def normalize_rows(values):
    widened = values.astype(jnp.float32)
    return (
        widened
        * lax.rsqrt(jnp.mean(widened * widened, axis=-1, keepdims=True) + epsilon)
        * widened.shape[-1] ** (-0.5)
    ).astype(jnp.bfloat16)


def as_column(row):
    count = row.shape[1]
    across = lax.broadcasted_iota(jnp.int32, (count, count), 1)
    down = lax.broadcasted_iota(jnp.int32, (count, count), 0)
    return jnp.sum(jnp.where(across == down, row, jnp.zeros_like(row)), axis=1, keepdims=True)


def as_row(column):
    count = column.shape[0]
    across = lax.broadcasted_iota(jnp.int32, (count, count), 1)
    down = lax.broadcasted_iota(jnp.int32, (count, count), 0)
    return jnp.sum(jnp.where(across == down, column, jnp.zeros_like(column)), axis=0, keepdims=True)


LANES = 128


def arrange_kernel(ids_hbm, rows_hbm, out_ref, moves_ref, ids_out_ref, ids_ref, rows_ref, sems):
    ids_copy = pltpu.make_async_copy(ids_hbm, ids_ref, sems.at[0])
    rows_copy = pltpu.make_async_copy(rows_hbm, rows_ref, sems.at[1])
    ids_copy.start()
    rows_copy.start()
    count = rows_ref.shape[0]
    ids_copy.wait()
    ids_row = ids_ref[...].reshape(1, count)
    ids_column = as_column(ids_row)
    across = lax.broadcasted_iota(jnp.int32, (count, count), 1)
    down = lax.broadcasted_iota(jnp.int32, (count, count), 0)
    before = (ids_column < ids_row) | ((ids_column == ids_row) & (down < across))
    rank_row = jnp.sum(before.astype(jnp.int32), axis=0, keepdims=True)
    moves = (down == rank_row).astype(jnp.bfloat16)
    rows_copy.wait()
    unit = normalize_rows(rows_ref[...])
    out_ref[...] = jnp.dot(moves, unit, preferred_element_type=jnp.float32).astype(jnp.bfloat16)
    moves_ref[...] = moves
    ids_out_ref[...] = ids_row


def partial_sums(queries, keys, bounds, own):
    count = bounds.shape[0]
    blocks = queries.shape[0] // count
    similar = lax.dot_general(
        queries, keys, (((1,), (1,)), ((), ())), preferred_element_type=jnp.float32
    )
    bounds = jnp.concatenate([bounds] * blocks, axis=0)
    key = lax.broadcasted_iota(jnp.int32, similar.shape, 1)
    place = lax.rem(key, count)
    allowed = (place >= bounds[:, 0:1]) & (place < bounds[:, 1:2])
    if own:
        query = lax.broadcasted_iota(jnp.int32, similar.shape, 0)
        allowed = allowed & ((key != query) | (key >= count))
    weights = jnp.where(allowed, jnp.exp(sharpness * (similar - 1.0)), 0.0)
    totals = jnp.sum(weights, axis=1, keepdims=True)
    return totals, jnp.dot(weights.astype(jnp.bfloat16), keys, preferred_element_type=jnp.float32)


def first_kernel(moves_ref, ids_ref, own_ref, beside_ref, *refs):
    *key_refs, weighted_ref, totals_ref, bounds_ref = refs
    ids = ids_ref[...]
    label = jnp.sum(jnp.where(moves_ref[...] > 0, ids, 0), axis=1, keepdims=True)
    first = jnp.sum((ids < label).astype(jnp.int32), axis=1, keepdims=True)
    after = jnp.sum((ids <= label).astype(jnp.int32), axis=1, keepdims=True)
    lane = lax.broadcasted_iota(jnp.int32, bounds_ref.shape, 1)
    bounds = jnp.where(lane == 0, first, after)
    bounds_ref[...] = bounds
    queries = jnp.concatenate([own_ref[...], beside_ref[...]], axis=0)
    keys = jnp.concatenate([ref[...] for ref in key_refs], axis=0)
    totals, weighted = partial_sums(queries, keys, bounds, True)
    weighted_ref[...] = weighted
    totals_ref[...] = jnp.broadcast_to(totals, totals_ref.shape)


def beside_kernel(so_far_ref, totals_so_far_ref, bounds_ref, beside_ref, keys_ref, out_ref):
    count = beside_ref.shape[0]
    totals, weighted = partial_sums(beside_ref[...], keys_ref[...], bounds_ref[...], False)
    weighted = (weighted + so_far_ref[count:, :]).astype(jnp.bfloat16)
    columns = weighted.shape[1] // LANES
    for index in range(columns):
        out_ref[index * count : (index + 1) * count, :] = weighted[
            :, index * LANES : (index + 1) * LANES
        ]
    totals = as_row(totals + totals_so_far_ref[count:, 0:1])
    totals = jnp.concatenate([totals, jnp.zeros((1, LANES - count), jnp.float32)], axis=1)
    high = totals.astype(jnp.bfloat16).astype(jnp.float32)
    row = lax.broadcasted_iota(jnp.int32, (EXTRA, LANES), 0)
    out_ref[columns * count :, :] = jnp.where(row == 0, high, totals - high).astype(jnp.bfloat16)


def own_kernel(so_far_ref, totals_so_far_ref, bounds_ref, own_ref, keys_ref, weighted_ref, totals_ref):
    count = own_ref.shape[0]
    totals, weighted = partial_sums(own_ref[...], keys_ref[...], bounds_ref[...], False)
    weighted_ref[...] = weighted + so_far_ref[:count, :]
    totals_ref[...] = as_row(totals + totals_so_far_ref[:count, 0:1])


def finish_kernel(
    moves_ref,
    weighted_ref,
    totals_ref,
    back_ref,
    neighbour_hbm,
    score_hbm,
    neighbour_ref,
    score_ref,
    sems,
):
    count, features = neighbour_ref.shape
    columns = features // LANES
    back = [
        back_ref[index * count : (index + 1) * count, :].astype(jnp.float32)
        for index in range(columns)
    ]
    weighted = weighted_ref[...] + jnp.concatenate(back, axis=1)
    normed = (
        weighted * lax.rsqrt(jnp.mean(weighted * weighted, axis=-1, keepdims=True) + epsilon)
    ).astype(jnp.bfloat16)
    moves = moves_ref[...]
    copies = []
    for half in range(2):
        part = slice(half * features // 2, (half + 1) * features // 2)
        neighbour_ref[:, part] = lax.dot_general(
            moves, normed[:, part], (((0,), (0,)), ((), ())), preferred_element_type=jnp.float32
        ).astype(jnp.bfloat16)
        copies.append(
            pltpu.make_async_copy(
                neighbour_ref.at[:, part], neighbour_hbm.at[:, part], sems.at[half]
            )
        )
        copies[-1].start()
    pair = back_ref[columns * count :, :].astype(jnp.float32)
    totals = totals_ref[...] + (pair[0:1, :count] + pair[1:2, :count])
    scores = jnp.sum(moves.astype(jnp.float32) * as_column(jnp.log(totals)), axis=0, keepdims=True)
    score_ref[...] = scores.astype(jnp.bfloat16).reshape(count)
    copies.append(pltpu.make_async_copy(score_ref, score_hbm, sems.at[2]))
    copies[-1].start()
    for copy in copies:
        copy.wait()


EXTRA = 16
CORE, ACROSS = 1, 2
PLANE, GRID = 4, 16
Z_TURNS = ((1, 3, 0, 2), (3, 2, 1, 0), (2, 0, 3, 1))


def gathered_body(embeddings, cluster_id):
    rows_dev, features = embeddings.shape
    vmem = pl.BlockSpec(memory_space=pltpu.VMEM)
    stored = pl.BlockSpec(memory_space=pltpu.HBM)

    def swap(value, bits):
        return lax.ppermute(value, "blk", [(device, device ^ bits) for device in range(GRID)])

    def visit(value, planes):
        pairs = [
            (device, planes[device // PLANE] * PLANE + device % PLANE) for device in range(GRID)
        ]
        return lax.ppermute(value, "blk", pairs)

    def block(kind, *shape):
        return jax.ShapeDtypeStruct(shape, kind)

    def kernel(body, name, out_shape, *inputs, specs=vmem, out_specs=vmem, scratch=()):
        return pl.pallas_call(
            body,
            out_shape=out_shape,
            in_specs=[specs] * len(inputs),
            out_specs=(out_specs,) * len(out_shape),
            scratch_shapes=scratch,
            compiler_params=pltpu.CompilerParams(vmem_limit_bytes=32 * 1024 * 1024),
            name=name,
        )(*inputs)

    rows = block(jnp.bfloat16, rows_dev, features)
    own, moves, ids = kernel(
        arrange_kernel,
        "arrange",
        (rows, block(jnp.bfloat16, rows_dev, rows_dev), block(jnp.int32, 1, rows_dev)),
        pltpu.with_memory_space_constraint(cluster_id, pltpu.HBM),
        pltpu.with_memory_space_constraint(embeddings, pltpu.HBM),
        specs=stored,
        scratch=(
            pltpu.VMEM((rows_dev,), jnp.int32),
            pltpu.VMEM((rows_dev, features), jnp.bfloat16),
            pltpu.SemaphoreType.DMA((2,)),
        ),
    )

    *visiting, beside, mate = lax.optimization_barrier(
        (*(visit(own, planes) for planes in Z_TURNS), swap(own, ACROSS), swap(own, CORE))
    )
    mates = swap(jnp.concatenate(visiting, axis=0), CORE)
    *so_far, bounds = kernel(
        first_kernel,
        "first",
        (
            block(jnp.float32, 2 * rows_dev, features),
            block(jnp.float32, 2 * rows_dev, LANES),
            block(jnp.int32, rows_dev, LANES),
        ),
        *(moves, ids, own, beside),
        *(own, mate, *visiting),
    )
    (partial,) = kernel(
        beside_kernel,
        "beside",
        (block(jnp.bfloat16, rows_dev * features // LANES + EXTRA, LANES),),
        *(*so_far, bounds, beside, mates),
    )
    back = swap(partial, ACROSS)
    weighted, totals = kernel(
        own_kernel,
        "own",
        (block(jnp.float32, rows_dev, features), block(jnp.float32, 1, rows_dev)),
        *(*so_far, bounds, own, mates),
    )
    return tuple(
        kernel(
            finish_kernel,
            "finish",
            (rows, block(jnp.bfloat16, rows_dev)),
            *(moves, weighted, totals, back),
            out_specs=stored,
            scratch=(
                pltpu.VMEM((rows_dev, features), jnp.bfloat16),
                pltpu.VMEM((rows_dev,), jnp.bfloat16),
                pltpu.SemaphoreType.DMA((3,)),
            ),
        )
    )


def from_behind(value, axis, steps):
    count = lax.axis_size(axis)
    initial, last = (max(0, -steps), min(count, count - steps))
    return lax.ppermute(value, axis, [(source, source + steps) for source in range(initial, last)])


def pair_terms(queries, visiting, allowed):
    similar = jnp.dot(queries, visiting.T, preferred_element_type=jnp.float32)
    return jnp.where(allowed, jnp.exp(sharpness * (similar - 1.0)), jnp.zeros_like(similar))


def finish(weighted, totals):
    normed = (
        weighted * lax.rsqrt(jnp.mean(weighted * weighted, axis=-1, keepdims=True) + epsilon)
    ).astype(jnp.bfloat16)
    return (normed, jnp.log(totals).astype(jnp.bfloat16))


def collected_body(embeddings, cluster_id):
    rows_dev, features = embeddings.shape
    devices = lax.axis_size("blk")
    per_peer = rows_dev // devices
    clusters = devices // 4
    unit_rows = normalize_rows(embeddings)
    labels = jnp.arange(clusters, dtype=jnp.int32)
    counts = jnp.sum((cluster_id[:, None] == labels[None, :]).astype(jnp.int32), axis=0)
    group_ends = jnp.cumsum(counts // per_peer)

    def owner_cluster(device):
        in_range = (device >= 0) & (device < devices)
        return jnp.where(in_range, jnp.sum((device >= group_ends).astype(jnp.int32)), -1)

    position = jnp.arange(rows_dev, dtype=jnp.int32)
    arrange_order = jnp.argsort(cluster_id * rows_dev + position)
    inverse = jnp.argsort(arrange_order)
    arranged = unit_rows[arrange_order].reshape(devices, per_peer, features)
    held_rows = lax.all_to_all(arranged, "blk", split_axis=0, concat_axis=0, tiled=True).reshape(
        rows_dev, features
    )
    self_index = lax.axis_index("blk")
    mine = owner_cluster(self_index)
    weights = pair_terms(held_rows, held_rows, position[:, None] != position[None, :])
    totals = jnp.sum(weights, axis=1)
    weighted = jnp.dot(weights.astype(jnp.bfloat16), held_rows, preferred_element_type=jnp.float32)
    from_lower = held_rows
    from_upper = held_rows
    for distance in range(1, U_MAX):
        from_lower = from_behind(from_lower, "blk", 1)
        from_upper = from_behind(from_upper, "blk", -1)
        for visiting, source in (
            (from_lower, self_index - distance),
            (from_upper, self_index + distance),
        ):
            weights = pair_terms(held_rows, visiting, owner_cluster(source) == mine)
            totals = totals + jnp.sum(weights, axis=1)
            weighted = weighted + jnp.dot(
                weights.astype(jnp.bfloat16), visiting, preferred_element_type=jnp.float32
            )
    normed, scores = finish(weighted, totals)
    returned_rows, returned_scores = (
        lax.all_to_all(
            normed.reshape(devices, per_peer, features),
            "blk",
            split_axis=0,
            concat_axis=0,
            tiled=True,
        ),
        lax.all_to_all(
            scores.reshape(devices, per_peer), "blk", split_axis=0, concat_axis=0, tiled=True
        ),
    )
    neighbour = returned_rows.reshape(rows_dev, features)[inverse]
    dup_score = returned_scores.reshape(rows_dev)[inverse]
    return (neighbour, dup_score)


def solution(mesh):
    placed = (P(("groups", "blk"), None), P(("groups", "blk")))
    devices = mesh.shape["blk"]

    def body(embeddings, cluster_id):
        gathered = embeddings.size * embeddings.dtype.itemsize * devices
        fits = gathered <= GATHER_LIMIT and devices == GRID and embeddings.shape[0] % 16 == 0
        plan = gathered_body if fits else collected_body
        return plan(embeddings, cluster_id)

    return jax.shard_map(
        body,
        mesh=mesh,
        in_specs=placed,
        out_specs=(P(("groups", "blk"), None), P(("groups", "blk"))),
        check_vma=False,
    )
```

```python
import jax
import jax.numpy as jnp
from jax import lax
from jax.experimental import pallas as pl
from jax.experimental.pallas import tpu as pltpu
from jax.sharding import PartitionSpec as P

U_MAX = 8
GATHER_LIMIT = 4 * 1024 * 1024


sharpness = 10.0
epsilon = 1e-06


def normalize_rows(values):
    widened = values.astype(jnp.float32)
    return (
        widened
        * lax.rsqrt(jnp.mean(widened * widened, axis=-1, keepdims=True) + epsilon)
        * widened.shape[-1] ** (-0.5)
    ).astype(jnp.bfloat16)


def as_column(row):
    count = row.shape[1]
    across = lax.broadcasted_iota(jnp.int32, (count, count), 1)
    down = lax.broadcasted_iota(jnp.int32, (count, count), 0)
    return jnp.sum(jnp.where(across == down, row, jnp.zeros_like(row)), axis=1, keepdims=True)


def as_row(column):
    count = column.shape[0]
    across = lax.broadcasted_iota(jnp.int32, (count, count), 1)
    down = lax.broadcasted_iota(jnp.int32, (count, count), 0)
    return jnp.sum(jnp.where(across == down, column, jnp.zeros_like(column)), axis=0, keepdims=True)


LANES = 128


def arrange_kernel(ids_hbm, rows_hbm, out_ref, moves_ref, ids_out_ref, ids_ref, rows_ref, sems):
    ids_copy = pltpu.make_async_copy(ids_hbm, ids_ref, sems.at[0])
    rows_copy = pltpu.make_async_copy(rows_hbm, rows_ref, sems.at[1])
    ids_copy.start()
    rows_copy.start()
    count = rows_ref.shape[0]
    ids_copy.wait()
    ids_row = ids_ref[...].reshape(1, count)
    ids_column = as_column(ids_row)
    across = lax.broadcasted_iota(jnp.int32, (count, count), 1)
    down = lax.broadcasted_iota(jnp.int32, (count, count), 0)
    before = (ids_column < ids_row) | ((ids_column == ids_row) & (down < across))
    rank_row = jnp.sum(before.astype(jnp.int32), axis=0, keepdims=True)
    moves = (down == rank_row).astype(jnp.bfloat16)
    rows_copy.wait()
    unit = normalize_rows(rows_ref[...])
    out_ref[...] = jnp.dot(moves, unit, preferred_element_type=jnp.float32).astype(jnp.bfloat16)
    moves_ref[...] = moves
    ids_out_ref[...] = ids_row


def partial_sums(queries, keys, bounds, own):
    count = bounds.shape[0]
    blocks = queries.shape[0] // count
    similar = lax.dot_general(
        queries, keys, (((1,), (1,)), ((), ())), preferred_element_type=jnp.float32
    )
    bounds = jnp.concatenate([bounds] * blocks, axis=0)
    key = lax.broadcasted_iota(jnp.int32, similar.shape, 1)
    place = lax.rem(key, count)
    allowed = (place >= bounds[:, 0:1]) & (place < bounds[:, 1:2])
    if own:
        query = lax.broadcasted_iota(jnp.int32, similar.shape, 0)
        allowed = allowed & ((key != query) | (key >= count))
    weights = jnp.where(allowed, jnp.exp(sharpness * (similar - 1.0)), 0.0)
    totals = jnp.sum(weights, axis=1, keepdims=True)
    return totals, jnp.dot(weights.astype(jnp.bfloat16), keys, preferred_element_type=jnp.float32)


def first_kernel(moves_ref, ids_ref, own_ref, beside_ref, *refs):
    *key_refs, weighted_ref, totals_ref, bounds_ref = refs
    ids = ids_ref[...]
    label = jnp.sum(jnp.where(moves_ref[...] > 0, ids, 0), axis=1, keepdims=True)
    first = jnp.sum((ids < label).astype(jnp.int32), axis=1, keepdims=True)
    after = jnp.sum((ids <= label).astype(jnp.int32), axis=1, keepdims=True)
    lane = lax.broadcasted_iota(jnp.int32, bounds_ref.shape, 1)
    bounds = jnp.where(lane == 0, first, after)
    bounds_ref[...] = bounds
    queries = jnp.concatenate([own_ref[...], beside_ref[...]], axis=0)
    keys = jnp.concatenate([ref[...] for ref in key_refs], axis=0)
    totals, weighted = partial_sums(queries, keys, bounds, True)
    weighted_ref[...] = weighted
    totals_ref[...] = jnp.broadcast_to(totals, totals_ref.shape)


def beside_kernel(so_far_ref, totals_so_far_ref, bounds_ref, beside_ref, keys_ref, out_ref):
    count = beside_ref.shape[0]
    totals, weighted = partial_sums(beside_ref[...], keys_ref[...], bounds_ref[...], False)
    weighted = (weighted + so_far_ref[count:, :]).astype(jnp.bfloat16)
    columns = weighted.shape[1] // LANES
    for index in range(columns):
        out_ref[index * count : (index + 1) * count, :] = weighted[
            :, index * LANES : (index + 1) * LANES
        ]
    totals = as_row(totals + totals_so_far_ref[count:, 0:1])
    totals = jnp.concatenate([totals, jnp.zeros((1, LANES - count), jnp.float32)], axis=1)
    high = totals.astype(jnp.bfloat16).astype(jnp.float32)
    row = lax.broadcasted_iota(jnp.int32, (EXTRA, LANES), 0)
    out_ref[columns * count :, :] = jnp.where(row == 0, high, totals - high).astype(jnp.bfloat16)


def own_kernel(so_far_ref, totals_so_far_ref, bounds_ref, own_ref, keys_ref, weighted_ref, totals_ref):
    count = own_ref.shape[0]
    totals, weighted = partial_sums(own_ref[...], keys_ref[...], bounds_ref[...], False)
    weighted_ref[...] = weighted + so_far_ref[:count, :]
    totals_ref[...] = as_row(totals + totals_so_far_ref[:count, 0:1])


def finish_kernel(
    moves_ref,
    weighted_ref,
    totals_ref,
    back_ref,
    neighbour_hbm,
    score_hbm,
    neighbour_ref,
    score_ref,
    sems,
):
    count, features = neighbour_ref.shape
    columns = features // LANES
    back = [
        back_ref[index * count : (index + 1) * count, :].astype(jnp.float32)
        for index in range(columns)
    ]
    weighted = weighted_ref[...] + jnp.concatenate(back, axis=1)
    normed = (
        weighted * lax.rsqrt(jnp.mean(weighted * weighted, axis=-1, keepdims=True) + epsilon)
    ).astype(jnp.bfloat16)
    moves = moves_ref[...]
    copies = []
    for half in range(2):
        part = slice(half * features // 2, (half + 1) * features // 2)
        neighbour_ref[:, part] = lax.dot_general(
            moves, normed[:, part], (((0,), (0,)), ((), ())), preferred_element_type=jnp.float32
        ).astype(jnp.bfloat16)
        copies.append(
            pltpu.make_async_copy(
                neighbour_ref.at[:, part], neighbour_hbm.at[:, part], sems.at[half]
            )
        )
        copies[-1].start()
    pair = back_ref[columns * count :, :].astype(jnp.float32)
    totals = totals_ref[...] + (pair[0:1, :count] + pair[1:2, :count])
    scores = jnp.sum(moves.astype(jnp.float32) * as_column(jnp.log(totals)), axis=0, keepdims=True)
    score_ref[...] = scores.astype(jnp.bfloat16).reshape(count)
    copies.append(pltpu.make_async_copy(score_ref, score_hbm, sems.at[2]))
    copies[-1].start()
    for copy in copies:
        copy.wait()


EXTRA = 16
CORE, ACROSS, NEAR, FAR = 1, 2, 4, 8
GRID = 16


def gathered_body(embeddings, cluster_id):
    rows_dev, features = embeddings.shape
    vmem = pl.BlockSpec(memory_space=pltpu.VMEM)
    stored = pl.BlockSpec(memory_space=pltpu.HBM)

    def swap(value, bits):
        bits = bits | CORE
        return lax.ppermute(value, "blk", [(device, device ^ bits) for device in range(GRID)])

    def block(kind, *shape):
        return jax.ShapeDtypeStruct(shape, kind)

    def kernel(body, name, out_shape, *inputs, specs=vmem, out_specs=vmem, scratch=()):
        return pl.pallas_call(
            body,
            out_shape=out_shape,
            in_specs=[specs] * len(inputs),
            out_specs=(out_specs,) * len(out_shape),
            scratch_shapes=scratch,
            compiler_params=pltpu.CompilerParams(vmem_limit_bytes=32 * 1024 * 1024),
            name=name,
        )(*inputs)

    rows = block(jnp.bfloat16, rows_dev, features)
    own, moves, ids = kernel(
        arrange_kernel,
        "arrange",
        (rows, block(jnp.bfloat16, rows_dev, rows_dev), block(jnp.int32, 1, rows_dev)),
        pltpu.with_memory_space_constraint(cluster_id, pltpu.HBM),
        pltpu.with_memory_space_constraint(embeddings, pltpu.HBM),
        specs=stored,
        scratch=(
            pltpu.VMEM((rows_dev,), jnp.int32),
            pltpu.VMEM((rows_dev, features), jnp.bfloat16),
            pltpu.SemaphoreType.DMA((2,)),
        ),
    )

    far, farther, near, beside, mate = lax.optimization_barrier(
        tuple(swap(own, bits) for bits in (FAR, FAR | NEAR, NEAR, ACROSS, CORE))
    )
    mates = swap(jnp.concatenate([near, far, farther], axis=0), CORE)
    *so_far, bounds = kernel(
        first_kernel,
        "first",
        (
            block(jnp.float32, 2 * rows_dev, features),
            block(jnp.float32, 2 * rows_dev, LANES),
            block(jnp.int32, rows_dev, LANES),
        ),
        *(moves, ids, own, beside),
        *(own, mate, near, far, farther),
    )
    (partial,) = kernel(
        beside_kernel,
        "beside",
        (block(jnp.bfloat16, rows_dev * features // LANES + EXTRA, LANES),),
        *(*so_far, bounds, beside, mates),
    )
    back = swap(partial, ACROSS)
    weighted, totals = kernel(
        own_kernel,
        "own",
        (block(jnp.float32, rows_dev, features), block(jnp.float32, 1, rows_dev)),
        *(*so_far, bounds, own, mates),
    )
    return tuple(
        kernel(
            finish_kernel,
            "finish",
            (rows, block(jnp.bfloat16, rows_dev)),
            *(moves, weighted, totals, back),
            out_specs=stored,
            scratch=(
                pltpu.VMEM((rows_dev, features), jnp.bfloat16),
                pltpu.VMEM((rows_dev,), jnp.bfloat16),
                pltpu.SemaphoreType.DMA((3,)),
            ),
        )
    )


def from_behind(value, axis, steps):
    count = lax.axis_size(axis)
    initial, last = (max(0, -steps), min(count, count - steps))
    return lax.ppermute(value, axis, [(source, source + steps) for source in range(initial, last)])


def pair_terms(queries, visiting, allowed):
    similar = jnp.dot(queries, visiting.T, preferred_element_type=jnp.float32)
    return jnp.where(allowed, jnp.exp(sharpness * (similar - 1.0)), jnp.zeros_like(similar))


def finish(weighted, totals):
    normed = (
        weighted * lax.rsqrt(jnp.mean(weighted * weighted, axis=-1, keepdims=True) + epsilon)
    ).astype(jnp.bfloat16)
    return (normed, jnp.log(totals).astype(jnp.bfloat16))


def collected_body(embeddings, cluster_id):
    rows_dev, features = embeddings.shape
    devices = lax.axis_size("blk")
    per_peer = rows_dev // devices
    clusters = devices // 4
    unit_rows = normalize_rows(embeddings)
    labels = jnp.arange(clusters, dtype=jnp.int32)
    counts = jnp.sum((cluster_id[:, None] == labels[None, :]).astype(jnp.int32), axis=0)
    group_ends = jnp.cumsum(counts // per_peer)

    def owner_cluster(device):
        in_range = (device >= 0) & (device < devices)
        return jnp.where(in_range, jnp.sum((device >= group_ends).astype(jnp.int32)), -1)

    position = jnp.arange(rows_dev, dtype=jnp.int32)
    arrange_order = jnp.argsort(cluster_id * rows_dev + position)
    inverse = jnp.argsort(arrange_order)
    arranged = unit_rows[arrange_order].reshape(devices, per_peer, features)
    held_rows = lax.all_to_all(arranged, "blk", split_axis=0, concat_axis=0, tiled=True).reshape(
        rows_dev, features
    )
    self_index = lax.axis_index("blk")
    mine = owner_cluster(self_index)
    weights = pair_terms(held_rows, held_rows, position[:, None] != position[None, :])
    totals = jnp.sum(weights, axis=1)
    weighted = jnp.dot(weights.astype(jnp.bfloat16), held_rows, preferred_element_type=jnp.float32)
    from_lower = held_rows
    from_upper = held_rows
    for distance in range(1, U_MAX):
        from_lower = from_behind(from_lower, "blk", 1)
        from_upper = from_behind(from_upper, "blk", -1)
        for visiting, source in (
            (from_lower, self_index - distance),
            (from_upper, self_index + distance),
        ):
            weights = pair_terms(held_rows, visiting, owner_cluster(source) == mine)
            totals = totals + jnp.sum(weights, axis=1)
            weighted = weighted + jnp.dot(
                weights.astype(jnp.bfloat16), visiting, preferred_element_type=jnp.float32
            )
    normed, scores = finish(weighted, totals)
    returned_rows, returned_scores = (
        lax.all_to_all(
            normed.reshape(devices, per_peer, features),
            "blk",
            split_axis=0,
            concat_axis=0,
            tiled=True,
        ),
        lax.all_to_all(
            scores.reshape(devices, per_peer), "blk", split_axis=0, concat_axis=0, tiled=True
        ),
    )
    neighbour = returned_rows.reshape(rows_dev, features)[inverse]
    dup_score = returned_scores.reshape(rows_dev)[inverse]
    return (neighbour, dup_score)


def solution(mesh):
    placed = (P(("groups", "blk"), None), P(("groups", "blk")))
    devices = mesh.shape["blk"]

    def body(embeddings, cluster_id):
        gathered = embeddings.size * embeddings.dtype.itemsize * devices
        fits = gathered <= GATHER_LIMIT and devices == GRID and embeddings.shape[0] % 16 == 0
        plan = gathered_body if fits else collected_body
        return plan(embeddings, cluster_id)

    return jax.shard_map(
        body,
        mesh=mesh,
        in_specs=placed,
        out_specs=(P(("groups", "blk"), None), P(("groups", "blk"))),
        check_vma=False,
    )
```

```python
import jax
import jax.numpy as jnp
from jax import lax
from jax.experimental import pallas as pl
from jax.experimental.pallas import tpu as pltpu
from jax.sharding import PartitionSpec as P

U_MAX = 8
GATHER_LIMIT = 4 * 1024 * 1024


sharpness = 10.0
epsilon = 1e-06


def normalize_rows(values):
    widened = values.astype(jnp.float32)
    return (
        widened
        * lax.rsqrt(jnp.mean(widened * widened, axis=-1, keepdims=True) + epsilon)
        * widened.shape[-1] ** (-0.5)
    ).astype(jnp.bfloat16)


def as_column(row):
    count = row.shape[1]
    across = lax.broadcasted_iota(jnp.int32, (count, count), 1)
    down = lax.broadcasted_iota(jnp.int32, (count, count), 0)
    return jnp.sum(jnp.where(across == down, row, jnp.zeros_like(row)), axis=1, keepdims=True)


def as_row(column):
    count = column.shape[0]
    across = lax.broadcasted_iota(jnp.int32, (count, count), 1)
    down = lax.broadcasted_iota(jnp.int32, (count, count), 0)
    return jnp.sum(jnp.where(across == down, column, jnp.zeros_like(column)), axis=0, keepdims=True)


LANES = 128


def arrange_kernel(ids_hbm, rows_hbm, out_ref, moves_ref, ids_out_ref, ids_ref, rows_ref, sems):
    ids_copy = pltpu.make_async_copy(ids_hbm, ids_ref, sems.at[0])
    rows_copy = pltpu.make_async_copy(rows_hbm, rows_ref, sems.at[1])
    ids_copy.start()
    rows_copy.start()
    count = rows_ref.shape[0]
    ids_copy.wait()
    ids_row = ids_ref[...].reshape(1, count)
    ids_column = as_column(ids_row)
    across = lax.broadcasted_iota(jnp.int32, (count, count), 1)
    down = lax.broadcasted_iota(jnp.int32, (count, count), 0)
    before = (ids_column < ids_row) | ((ids_column == ids_row) & (down < across))
    rank_row = jnp.sum(before.astype(jnp.int32), axis=0, keepdims=True)
    moves = (down == rank_row).astype(jnp.bfloat16)
    rows_copy.wait()
    unit = normalize_rows(rows_ref[...])
    out_ref[...] = jnp.dot(moves, unit, preferred_element_type=jnp.float32).astype(jnp.bfloat16)
    moves_ref[...] = moves
    ids_out_ref[...] = ids_row


def partial_sums(queries, keys, bounds, own):
    count = bounds.shape[0]
    blocks = queries.shape[0] // count
    similar = lax.dot_general(
        queries, keys, (((1,), (1,)), ((), ())), preferred_element_type=jnp.float32
    )
    bounds = jnp.concatenate([bounds] * blocks, axis=0)
    key = lax.broadcasted_iota(jnp.int32, similar.shape, 1)
    place = lax.rem(key, count)
    allowed = (place >= bounds[:, 0:1]) & (place < bounds[:, 1:2])
    if own:
        query = lax.broadcasted_iota(jnp.int32, similar.shape, 0)
        allowed = allowed & ((key != query) | (key >= count))
    weights = jnp.where(allowed, jnp.exp(sharpness * (similar - 1.0)), 0.0)
    totals = jnp.sum(weights, axis=1, keepdims=True)
    return totals, jnp.dot(weights.astype(jnp.bfloat16), keys, preferred_element_type=jnp.float32)


def first_kernel(moves_ref, ids_ref, own_ref, beside_ref, *refs):
    *key_refs, weighted_ref, totals_ref, bounds_ref = refs
    ids = ids_ref[...]
    label = jnp.sum(jnp.where(moves_ref[...] > 0, ids, 0), axis=1, keepdims=True)
    first = jnp.sum((ids < label).astype(jnp.int32), axis=1, keepdims=True)
    after = jnp.sum((ids <= label).astype(jnp.int32), axis=1, keepdims=True)
    lane = lax.broadcasted_iota(jnp.int32, bounds_ref.shape, 1)
    bounds = jnp.where(lane == 0, first, after)
    bounds_ref[...] = bounds
    queries = jnp.concatenate([own_ref[...], beside_ref[...]], axis=0)
    keys = jnp.concatenate([ref[...] for ref in key_refs], axis=0)
    totals, weighted = partial_sums(queries, keys, bounds, True)
    weighted_ref[...] = weighted
    totals_ref[...] = jnp.broadcast_to(totals, totals_ref.shape)


def beside_kernel(so_far_ref, totals_so_far_ref, bounds_ref, beside_ref, keys_ref, out_ref):
    count = beside_ref.shape[0]
    totals, weighted = partial_sums(beside_ref[...], keys_ref[...], bounds_ref[...], False)
    weighted = (weighted + so_far_ref[count:, :]).astype(jnp.bfloat16)
    columns = weighted.shape[1] // LANES
    for index in range(columns):
        out_ref[index * count : (index + 1) * count, :] = weighted[
            :, index * LANES : (index + 1) * LANES
        ]
    totals = as_row(totals + totals_so_far_ref[count:, 0:1])
    totals = jnp.concatenate([totals, jnp.zeros((1, LANES - count), jnp.float32)], axis=1)
    high = totals.astype(jnp.bfloat16).astype(jnp.float32)
    row = lax.broadcasted_iota(jnp.int32, (EXTRA, LANES), 0)
    out_ref[columns * count :, :] = jnp.where(row == 0, high, totals - high).astype(jnp.bfloat16)


def own_kernel(so_far_ref, totals_so_far_ref, bounds_ref, own_ref, keys_ref, weighted_ref, totals_ref):
    count = own_ref.shape[0]
    totals, weighted = partial_sums(own_ref[...], keys_ref[...], bounds_ref[...], False)
    weighted_ref[...] = weighted + so_far_ref[:count, :]
    totals_ref[...] = as_row(totals + totals_so_far_ref[:count, 0:1])


def finish_kernel(
    moves_ref,
    weighted_ref,
    totals_ref,
    back_ref,
    neighbour_hbm,
    score_hbm,
    neighbour_ref,
    score_ref,
    sems,
):
    count, features = neighbour_ref.shape
    columns = features // LANES
    back = [
        back_ref[index * count : (index + 1) * count, :].astype(jnp.float32)
        for index in range(columns)
    ]
    weighted = weighted_ref[...] + jnp.concatenate(back, axis=1)
    normed = (
        weighted * lax.rsqrt(jnp.mean(weighted * weighted, axis=-1, keepdims=True) + epsilon)
    ).astype(jnp.bfloat16)
    moves = moves_ref[...]
    copies = []
    for half in range(2):
        part = slice(half * features // 2, (half + 1) * features // 2)
        neighbour_ref[:, part] = lax.dot_general(
            moves, normed[:, part], (((0,), (0,)), ((), ())), preferred_element_type=jnp.float32
        ).astype(jnp.bfloat16)
        copies.append(
            pltpu.make_async_copy(
                neighbour_ref.at[:, part], neighbour_hbm.at[:, part], sems.at[half]
            )
        )
        copies[-1].start()
    pair = back_ref[columns * count :, :].astype(jnp.float32)
    totals = totals_ref[...] + (pair[0:1, :count] + pair[1:2, :count])
    scores = jnp.sum(moves.astype(jnp.float32) * as_column(jnp.log(totals)), axis=0, keepdims=True)
    score_ref[...] = scores.astype(jnp.bfloat16).reshape(count)
    copies.append(pltpu.make_async_copy(score_ref, score_hbm, sems.at[2]))
    copies[-1].start()
    for copy in copies:
        copy.wait()


EXTRA = 16
CORE, ACROSS, NEAR, FAR = 1, 2, 4, 8
GRID = 16


def gathered_body(embeddings, cluster_id):
    rows_dev, features = embeddings.shape
    vmem = pl.BlockSpec(memory_space=pltpu.VMEM)
    stored = pl.BlockSpec(memory_space=pltpu.HBM)

    def swap(value, bits):
        return lax.ppermute(value, "blk", [(device, device ^ bits) for device in range(GRID)])

    def block(kind, *shape):
        return jax.ShapeDtypeStruct(shape, kind)

    def kernel(body, name, out_shape, *inputs, specs=vmem, out_specs=vmem, scratch=()):
        return pl.pallas_call(
            body,
            out_shape=out_shape,
            in_specs=[specs] * len(inputs),
            out_specs=(out_specs,) * len(out_shape),
            scratch_shapes=scratch,
            compiler_params=pltpu.CompilerParams(vmem_limit_bytes=32 * 1024 * 1024),
            name=name,
        )(*inputs)

    rows = block(jnp.bfloat16, rows_dev, features)
    own, moves, ids = kernel(
        arrange_kernel,
        "arrange",
        (rows, block(jnp.bfloat16, rows_dev, rows_dev), block(jnp.int32, 1, rows_dev)),
        pltpu.with_memory_space_constraint(cluster_id, pltpu.HBM),
        pltpu.with_memory_space_constraint(embeddings, pltpu.HBM),
        specs=stored,
        scratch=(
            pltpu.VMEM((rows_dev,), jnp.int32),
            pltpu.VMEM((rows_dev, features), jnp.bfloat16),
            pltpu.SemaphoreType.DMA((2,)),
        ),
    )

    far, near, farther, beside, mate = lax.optimization_barrier(
        tuple(swap(own, bits) for bits in (FAR, NEAR, FAR | NEAR, ACROSS, CORE))
    )
    mates = swap(jnp.concatenate([near, far, farther], axis=0), CORE)
    *so_far, bounds = kernel(
        first_kernel,
        "first",
        (
            block(jnp.float32, 2 * rows_dev, features),
            block(jnp.float32, 2 * rows_dev, LANES),
            block(jnp.int32, rows_dev, LANES),
        ),
        *(moves, ids, own, beside),
        *(own, mate, near, far, farther),
    )
    (partial,) = kernel(
        beside_kernel,
        "beside",
        (block(jnp.bfloat16, rows_dev * features // LANES + EXTRA, LANES),),
        *(*so_far, bounds, beside, mates),
    )
    back = swap(partial, ACROSS)
    weighted, totals = kernel(
        own_kernel,
        "own",
        (block(jnp.float32, rows_dev, features), block(jnp.float32, 1, rows_dev)),
        *(*so_far, bounds, own, mates),
    )
    return tuple(
        kernel(
            finish_kernel,
            "finish",
            (rows, block(jnp.bfloat16, rows_dev)),
            *(moves, weighted, totals, back),
            out_specs=stored,
            scratch=(
                pltpu.VMEM((rows_dev, features), jnp.bfloat16),
                pltpu.VMEM((rows_dev,), jnp.bfloat16),
                pltpu.SemaphoreType.DMA((3,)),
            ),
        )
    )


def from_behind(value, axis, steps):
    count = lax.axis_size(axis)
    initial, last = (max(0, -steps), min(count, count - steps))
    return lax.ppermute(value, axis, [(source, source + steps) for source in range(initial, last)])


def pair_terms(queries, visiting, allowed):
    similar = jnp.dot(queries, visiting.T, preferred_element_type=jnp.float32)
    return jnp.where(allowed, jnp.exp(sharpness * (similar - 1.0)), jnp.zeros_like(similar))


def finish(weighted, totals):
    normed = (
        weighted * lax.rsqrt(jnp.mean(weighted * weighted, axis=-1, keepdims=True) + epsilon)
    ).astype(jnp.bfloat16)
    return (normed, jnp.log(totals).astype(jnp.bfloat16))


def collected_body(embeddings, cluster_id):
    rows_dev, features = embeddings.shape
    devices = lax.axis_size("blk")
    per_peer = rows_dev // devices
    clusters = devices // 4
    unit_rows = normalize_rows(embeddings)
    labels = jnp.arange(clusters, dtype=jnp.int32)
    counts = jnp.sum((cluster_id[:, None] == labels[None, :]).astype(jnp.int32), axis=0)
    group_ends = jnp.cumsum(counts // per_peer)

    def owner_cluster(device):
        in_range = (device >= 0) & (device < devices)
        return jnp.where(in_range, jnp.sum((device >= group_ends).astype(jnp.int32)), -1)

    position = jnp.arange(rows_dev, dtype=jnp.int32)
    arrange_order = jnp.argsort(cluster_id * rows_dev + position)
    inverse = jnp.argsort(arrange_order)
    arranged = unit_rows[arrange_order].reshape(devices, per_peer, features)
    held_rows = lax.all_to_all(arranged, "blk", split_axis=0, concat_axis=0, tiled=True).reshape(
        rows_dev, features
    )
    self_index = lax.axis_index("blk")
    mine = owner_cluster(self_index)
    weights = pair_terms(held_rows, held_rows, position[:, None] != position[None, :])
    totals = jnp.sum(weights, axis=1)
    weighted = jnp.dot(weights.astype(jnp.bfloat16), held_rows, preferred_element_type=jnp.float32)
    from_lower = held_rows
    from_upper = held_rows
    for distance in range(1, U_MAX):
        from_lower = from_behind(from_lower, "blk", 1)
        from_upper = from_behind(from_upper, "blk", -1)
        for visiting, source in (
            (from_lower, self_index - distance),
            (from_upper, self_index + distance),
        ):
            weights = pair_terms(held_rows, visiting, owner_cluster(source) == mine)
            totals = totals + jnp.sum(weights, axis=1)
            weighted = weighted + jnp.dot(
                weights.astype(jnp.bfloat16), visiting, preferred_element_type=jnp.float32
            )
    normed, scores = finish(weighted, totals)
    returned_rows, returned_scores = (
        lax.all_to_all(
            normed.reshape(devices, per_peer, features),
            "blk",
            split_axis=0,
            concat_axis=0,
            tiled=True,
        ),
        lax.all_to_all(
            scores.reshape(devices, per_peer), "blk", split_axis=0, concat_axis=0, tiled=True
        ),
    )
    neighbour = returned_rows.reshape(rows_dev, features)[inverse]
    dup_score = returned_scores.reshape(rows_dev)[inverse]
    return (neighbour, dup_score)


def solution(mesh):
    placed = (P(("groups", "blk"), None), P(("groups", "blk")))
    devices = mesh.shape["blk"]

    def body(embeddings, cluster_id):
        gathered = embeddings.size * embeddings.dtype.itemsize * devices
        fits = gathered <= GATHER_LIMIT and devices == GRID and embeddings.shape[0] % 16 == 0
        plan = gathered_body if fits else collected_body
        return plan(embeddings, cluster_id)

    return jax.shard_map(
        body,
        mesh=mesh,
        in_specs=placed,
        out_specs=(P(("groups", "blk"), None), P(("groups", "blk"))),
        check_vma=False,
    )
```

```python
import jax
import jax.numpy as jnp
from jax import lax
from jax.experimental import pallas as pl
from jax.experimental.pallas import tpu as pltpu
from jax.sharding import PartitionSpec as P

U_MAX = 8
GATHER_LIMIT = 4 * 1024 * 1024


sharpness = 10.0
epsilon = 1e-06


def normalize_rows(values):
    widened = values.astype(jnp.float32)
    return (
        widened
        * lax.rsqrt(jnp.mean(widened * widened, axis=-1, keepdims=True) + epsilon)
        * widened.shape[-1] ** (-0.5)
    ).astype(jnp.bfloat16)


def as_column(row):
    count = row.shape[1]
    across = lax.broadcasted_iota(jnp.int32, (count, count), 1)
    down = lax.broadcasted_iota(jnp.int32, (count, count), 0)
    return jnp.sum(jnp.where(across == down, row, jnp.zeros_like(row)), axis=1, keepdims=True)


def as_row(column):
    count = column.shape[0]
    across = lax.broadcasted_iota(jnp.int32, (count, count), 1)
    down = lax.broadcasted_iota(jnp.int32, (count, count), 0)
    return jnp.sum(jnp.where(across == down, column, jnp.zeros_like(column)), axis=0, keepdims=True)


LANES = 128


def arrange_kernel(ids_hbm, rows_hbm, out_ref, moves_ref, ids_out_ref, ids_ref, rows_ref, sems):
    ids_copy = pltpu.make_async_copy(ids_hbm, ids_ref, sems.at[0])
    rows_copy = pltpu.make_async_copy(rows_hbm, rows_ref, sems.at[1])
    ids_copy.start()
    rows_copy.start()
    count = rows_ref.shape[0]
    ids_copy.wait()
    ids_row = ids_ref[...].reshape(1, count)
    ids_column = as_column(ids_row)
    across = lax.broadcasted_iota(jnp.int32, (count, count), 1)
    down = lax.broadcasted_iota(jnp.int32, (count, count), 0)
    before = (ids_column < ids_row) | ((ids_column == ids_row) & (down < across))
    rank_row = jnp.sum(before.astype(jnp.int32), axis=0, keepdims=True)
    moves = (down == rank_row).astype(jnp.bfloat16)
    rows_copy.wait()
    unit = normalize_rows(rows_ref[...])
    out_ref[...] = jnp.dot(moves, unit, preferred_element_type=jnp.float32).astype(jnp.bfloat16)
    moves_ref[...] = moves
    ids_out_ref[...] = ids_row


def partial_sums(queries, keys, bounds, own):
    count = bounds.shape[0]
    blocks = queries.shape[0] // count
    similar = lax.dot_general(
        queries, keys, (((1,), (1,)), ((), ())), preferred_element_type=jnp.float32
    )
    bounds = jnp.concatenate([bounds] * blocks, axis=0)
    key = lax.broadcasted_iota(jnp.int32, similar.shape, 1)
    place = lax.rem(key, count)
    allowed = (place >= bounds[:, 0:1]) & (place < bounds[:, 1:2])
    if own:
        query = lax.broadcasted_iota(jnp.int32, similar.shape, 0)
        allowed = allowed & ((key != query) | (key >= count))
    weights = jnp.where(allowed, jnp.exp(sharpness * (similar - 1.0)), 0.0)
    totals = jnp.sum(weights, axis=1, keepdims=True)
    return totals, jnp.dot(weights.astype(jnp.bfloat16), keys, preferred_element_type=jnp.float32)


def first_kernel(moves_ref, ids_ref, own_ref, beside_ref, *refs):
    *key_refs, weighted_ref, totals_ref, bounds_ref = refs
    ids = ids_ref[...]
    label = jnp.sum(jnp.where(moves_ref[...] > 0, ids, 0), axis=1, keepdims=True)
    first = jnp.sum((ids < label).astype(jnp.int32), axis=1, keepdims=True)
    after = jnp.sum((ids <= label).astype(jnp.int32), axis=1, keepdims=True)
    lane = lax.broadcasted_iota(jnp.int32, bounds_ref.shape, 1)
    bounds = jnp.where(lane == 0, first, after)
    bounds_ref[...] = bounds
    queries = jnp.concatenate([own_ref[...], beside_ref[...]], axis=0)
    keys = jnp.concatenate([ref[...] for ref in key_refs], axis=0)
    totals, weighted = partial_sums(queries, keys, bounds, True)
    weighted_ref[...] = weighted
    totals_ref[...] = jnp.broadcast_to(totals, totals_ref.shape)


def beside_kernel(so_far_ref, totals_so_far_ref, bounds_ref, beside_ref, keys_ref, out_ref):
    count = beside_ref.shape[0]
    totals, weighted = partial_sums(beside_ref[...], keys_ref[...], bounds_ref[...], False)
    weighted = (weighted + so_far_ref[count:, :]).astype(jnp.bfloat16)
    columns = weighted.shape[1] // LANES
    for index in range(columns):
        out_ref[index * count : (index + 1) * count, :] = weighted[
            :, index * LANES : (index + 1) * LANES
        ]
    totals = as_row(totals + totals_so_far_ref[count:, 0:1])
    totals = jnp.concatenate([totals, jnp.zeros((1, LANES - count), jnp.float32)], axis=1)
    high = totals.astype(jnp.bfloat16).astype(jnp.float32)
    row = lax.broadcasted_iota(jnp.int32, (EXTRA, LANES), 0)
    out_ref[columns * count :, :] = jnp.where(row == 0, high, totals - high).astype(jnp.bfloat16)


def own_kernel(so_far_ref, totals_so_far_ref, bounds_ref, own_ref, keys_ref, weighted_ref, totals_ref):
    count = own_ref.shape[0]
    totals, weighted = partial_sums(own_ref[...], keys_ref[...], bounds_ref[...], False)
    weighted_ref[...] = weighted + so_far_ref[:count, :]
    totals_ref[...] = as_row(totals + totals_so_far_ref[:count, 0:1])


def finish_kernel(
    moves_ref,
    weighted_ref,
    totals_ref,
    back_ref,
    neighbour_hbm,
    score_hbm,
    neighbour_ref,
    score_ref,
    sems,
):
    count, features = neighbour_ref.shape
    columns = features // LANES
    back = [
        back_ref[index * count : (index + 1) * count, :].astype(jnp.float32)
        for index in range(columns)
    ]
    weighted = weighted_ref[...] + jnp.concatenate(back, axis=1)
    normed = (
        weighted * lax.rsqrt(jnp.mean(weighted * weighted, axis=-1, keepdims=True) + epsilon)
    ).astype(jnp.bfloat16)
    moves = moves_ref[...]
    copies = []
    for half in range(2):
        part = slice(half * features // 2, (half + 1) * features // 2)
        neighbour_ref[:, part] = lax.dot_general(
            moves, normed[:, part], (((0,), (0,)), ((), ())), preferred_element_type=jnp.float32
        ).astype(jnp.bfloat16)
        copies.append(
            pltpu.make_async_copy(
                neighbour_ref.at[:, part], neighbour_hbm.at[:, part], sems.at[half]
            )
        )
        copies[-1].start()
    pair = back_ref[columns * count :, :].astype(jnp.float32)
    totals = totals_ref[...] + (pair[0:1, :count] + pair[1:2, :count])
    scores = jnp.sum(moves.astype(jnp.float32) * as_column(jnp.log(totals)), axis=0, keepdims=True)
    score_ref[...] = scores.astype(jnp.bfloat16).reshape(count)
    copies.append(pltpu.make_async_copy(score_ref, score_hbm, sems.at[2]))
    copies[-1].start()
    for copy in copies:
        copy.wait()


EXTRA = 16
CORE, ACROSS, NEAR, FAR = 1, 2, 4, 8
GRID = 16


def gathered_body(embeddings, cluster_id):
    rows_dev, features = embeddings.shape
    vmem = pl.BlockSpec(memory_space=pltpu.VMEM)
    stored = pl.BlockSpec(memory_space=pltpu.HBM)

    def swap(value, bits):
        return lax.ppermute(value, "blk", [(device, device ^ bits) for device in range(GRID)])

    def block(kind, *shape):
        return jax.ShapeDtypeStruct(shape, kind)

    def kernel(body, name, out_shape, *inputs, specs=vmem, out_specs=vmem, scratch=()):
        return pl.pallas_call(
            body,
            out_shape=out_shape,
            in_specs=[specs] * len(inputs),
            out_specs=(out_specs,) * len(out_shape),
            scratch_shapes=scratch,
            compiler_params=pltpu.CompilerParams(vmem_limit_bytes=32 * 1024 * 1024),
            name=name,
        )(*inputs)

    rows = block(jnp.bfloat16, rows_dev, features)
    own, moves, ids = kernel(
        arrange_kernel,
        "arrange",
        (rows, block(jnp.bfloat16, rows_dev, rows_dev), block(jnp.int32, 1, rows_dev)),
        pltpu.with_memory_space_constraint(cluster_id, pltpu.HBM),
        pltpu.with_memory_space_constraint(embeddings, pltpu.HBM),
        specs=stored,
        scratch=(
            pltpu.VMEM((rows_dev,), jnp.int32),
            pltpu.VMEM((rows_dev, features), jnp.bfloat16),
            pltpu.SemaphoreType.DMA((2,)),
        ),
    )

    far, farther, beside, near, mate = lax.optimization_barrier(
        tuple(swap(own, bits) for bits in (FAR, FAR | NEAR, ACROSS, NEAR, CORE))
    )
    mates = swap(jnp.concatenate([near, far, farther], axis=0), CORE)
    *so_far, bounds = kernel(
        first_kernel,
        "first",
        (
            block(jnp.float32, 2 * rows_dev, features),
            block(jnp.float32, 2 * rows_dev, LANES),
            block(jnp.int32, rows_dev, LANES),
        ),
        *(moves, ids, own, beside),
        *(own, mate, near, far, farther),
    )
    (partial,) = kernel(
        beside_kernel,
        "beside",
        (block(jnp.bfloat16, rows_dev * features // LANES + EXTRA, LANES),),
        *(*so_far, bounds, beside, mates),
    )
    back = swap(partial, ACROSS)
    weighted, totals = kernel(
        own_kernel,
        "own",
        (block(jnp.float32, rows_dev, features), block(jnp.float32, 1, rows_dev)),
        *(*so_far, bounds, own, mates),
    )
    return tuple(
        kernel(
            finish_kernel,
            "finish",
            (rows, block(jnp.bfloat16, rows_dev)),
            *(moves, weighted, totals, back),
            out_specs=stored,
            scratch=(
                pltpu.VMEM((rows_dev, features), jnp.bfloat16),
                pltpu.VMEM((rows_dev,), jnp.bfloat16),
                pltpu.SemaphoreType.DMA((3,)),
            ),
        )
    )


def from_behind(value, axis, steps):
    count = lax.axis_size(axis)
    initial, last = (max(0, -steps), min(count, count - steps))
    return lax.ppermute(value, axis, [(source, source + steps) for source in range(initial, last)])


def pair_terms(queries, visiting, allowed):
    similar = jnp.dot(queries, visiting.T, preferred_element_type=jnp.float32)
    return jnp.where(allowed, jnp.exp(sharpness * (similar - 1.0)), jnp.zeros_like(similar))


def finish(weighted, totals):
    normed = (
        weighted * lax.rsqrt(jnp.mean(weighted * weighted, axis=-1, keepdims=True) + epsilon)
    ).astype(jnp.bfloat16)
    return (normed, jnp.log(totals).astype(jnp.bfloat16))


def collected_body(embeddings, cluster_id):
    rows_dev, features = embeddings.shape
    devices = lax.axis_size("blk")
    per_peer = rows_dev // devices
    clusters = devices // 4
    unit_rows = normalize_rows(embeddings)
    labels = jnp.arange(clusters, dtype=jnp.int32)
    counts = jnp.sum((cluster_id[:, None] == labels[None, :]).astype(jnp.int32), axis=0)
    group_ends = jnp.cumsum(counts // per_peer)

    def owner_cluster(device):
        in_range = (device >= 0) & (device < devices)
        return jnp.where(in_range, jnp.sum((device >= group_ends).astype(jnp.int32)), -1)

    position = jnp.arange(rows_dev, dtype=jnp.int32)
    arrange_order = jnp.argsort(cluster_id * rows_dev + position)
    inverse = jnp.argsort(arrange_order)
    arranged = unit_rows[arrange_order].reshape(devices, per_peer, features)
    held_rows = lax.all_to_all(arranged, "blk", split_axis=0, concat_axis=0, tiled=True).reshape(
        rows_dev, features
    )
    self_index = lax.axis_index("blk")
    mine = owner_cluster(self_index)
    weights = pair_terms(held_rows, held_rows, position[:, None] != position[None, :])
    totals = jnp.sum(weights, axis=1)
    weighted = jnp.dot(weights.astype(jnp.bfloat16), held_rows, preferred_element_type=jnp.float32)
    from_lower = held_rows
    from_upper = held_rows
    for distance in range(1, U_MAX):
        from_lower = from_behind(from_lower, "blk", 1)
        from_upper = from_behind(from_upper, "blk", -1)
        for visiting, source in (
            (from_lower, self_index - distance),
            (from_upper, self_index + distance),
        ):
            weights = pair_terms(held_rows, visiting, owner_cluster(source) == mine)
            totals = totals + jnp.sum(weights, axis=1)
            weighted = weighted + jnp.dot(
                weights.astype(jnp.bfloat16), visiting, preferred_element_type=jnp.float32
            )
    normed, scores = finish(weighted, totals)
    returned_rows, returned_scores = (
        lax.all_to_all(
            normed.reshape(devices, per_peer, features),
            "blk",
            split_axis=0,
            concat_axis=0,
            tiled=True,
        ),
        lax.all_to_all(
            scores.reshape(devices, per_peer), "blk", split_axis=0, concat_axis=0, tiled=True
        ),
    )
    neighbour = returned_rows.reshape(rows_dev, features)[inverse]
    dup_score = returned_scores.reshape(rows_dev)[inverse]
    return (neighbour, dup_score)


def solution(mesh):
    placed = (P(("groups", "blk"), None), P(("groups", "blk")))
    devices = mesh.shape["blk"]

    def body(embeddings, cluster_id):
        gathered = embeddings.size * embeddings.dtype.itemsize * devices
        fits = gathered <= GATHER_LIMIT and devices == GRID and embeddings.shape[0] % 16 == 0
        plan = gathered_body if fits else collected_body
        return plan(embeddings, cluster_id)

    return jax.shard_map(
        body,
        mesh=mesh,
        in_specs=placed,
        out_specs=(P(("groups", "blk"), None), P(("groups", "blk"))),
        check_vma=False,
    )
```

```python
import jax
import jax.numpy as jnp
from jax import lax
from jax.experimental import pallas as pl
from jax.experimental.pallas import tpu as pltpu
from jax.sharding import PartitionSpec as P

U_MAX = 8
GATHER_LIMIT = 4 * 1024 * 1024


sharpness = 10.0
epsilon = 1e-06


def normalize_rows(values):
    widened = values.astype(jnp.float32)
    return (
        widened
        * lax.rsqrt(jnp.mean(widened * widened, axis=-1, keepdims=True) + epsilon)
        * widened.shape[-1] ** (-0.5)
    ).astype(jnp.bfloat16)


def as_column(row):
    count = row.shape[1]
    across = lax.broadcasted_iota(jnp.int32, (count, count), 1)
    down = lax.broadcasted_iota(jnp.int32, (count, count), 0)
    return jnp.sum(jnp.where(across == down, row, jnp.zeros_like(row)), axis=1, keepdims=True)


def as_row(column):
    count = column.shape[0]
    across = lax.broadcasted_iota(jnp.int32, (count, count), 1)
    down = lax.broadcasted_iota(jnp.int32, (count, count), 0)
    return jnp.sum(jnp.where(across == down, column, jnp.zeros_like(column)), axis=0, keepdims=True)


LANES = 128


def arrange_kernel(ids_hbm, rows_hbm, out_ref, moves_ref, ids_out_ref, ids_ref, rows_ref, sems):
    ids_copy = pltpu.make_async_copy(ids_hbm, ids_ref, sems.at[0])
    rows_copy = pltpu.make_async_copy(rows_hbm, rows_ref, sems.at[1])
    ids_copy.start()
    rows_copy.start()
    count = rows_ref.shape[0]
    ids_copy.wait()
    ids_row = ids_ref[...].reshape(1, count)
    ids_column = as_column(ids_row)
    across = lax.broadcasted_iota(jnp.int32, (count, count), 1)
    down = lax.broadcasted_iota(jnp.int32, (count, count), 0)
    before = (ids_column < ids_row) | ((ids_column == ids_row) & (down < across))
    rank_row = jnp.sum(before.astype(jnp.int32), axis=0, keepdims=True)
    moves = (down == rank_row).astype(jnp.bfloat16)
    rows_copy.wait()
    unit = normalize_rows(rows_ref[...])
    out_ref[...] = jnp.dot(moves, unit, preferred_element_type=jnp.float32).astype(jnp.bfloat16)
    moves_ref[...] = moves
    ids_out_ref[...] = ids_row


def partial_sums(queries, keys, bounds, own):
    count = bounds.shape[0]
    blocks = queries.shape[0] // count
    similar = lax.dot_general(
        queries, keys, (((1,), (1,)), ((), ())), preferred_element_type=jnp.float32
    )
    bounds = jnp.concatenate([bounds] * blocks, axis=0)
    key = lax.broadcasted_iota(jnp.int32, similar.shape, 1)
    place = lax.rem(key, count)
    allowed = (place >= bounds[:, 0:1]) & (place < bounds[:, 1:2])
    if own:
        query = lax.broadcasted_iota(jnp.int32, similar.shape, 0)
        allowed = allowed & ((key != query) | (key >= count))
    weights = jnp.where(allowed, jnp.exp(sharpness * (similar - 1.0)), 0.0)
    totals = jnp.sum(weights, axis=1, keepdims=True)
    return totals, jnp.dot(weights.astype(jnp.bfloat16), keys, preferred_element_type=jnp.float32)


def first_kernel(moves_ref, ids_ref, own_ref, beside_ref, *refs):
    *key_refs, weighted_ref, totals_ref, bounds_ref = refs
    ids = ids_ref[...]
    label = jnp.sum(jnp.where(moves_ref[...] > 0, ids, 0), axis=1, keepdims=True)
    first = jnp.sum((ids < label).astype(jnp.int32), axis=1, keepdims=True)
    after = jnp.sum((ids <= label).astype(jnp.int32), axis=1, keepdims=True)
    lane = lax.broadcasted_iota(jnp.int32, bounds_ref.shape, 1)
    bounds = jnp.where(lane == 0, first, after)
    bounds_ref[...] = bounds
    queries = jnp.concatenate([own_ref[...], beside_ref[...]], axis=0)
    keys = jnp.concatenate([ref[...] for ref in key_refs], axis=0)
    totals, weighted = partial_sums(queries, keys, bounds, True)
    weighted_ref[...] = weighted
    totals_ref[...] = jnp.broadcast_to(totals, totals_ref.shape)


def beside_kernel(so_far_ref, totals_so_far_ref, bounds_ref, beside_ref, keys_ref, out_ref):
    count = beside_ref.shape[0]
    totals, weighted = partial_sums(beside_ref[...], keys_ref[...], bounds_ref[...], False)
    weighted = (weighted + so_far_ref[count:, :]).astype(jnp.bfloat16)
    columns = weighted.shape[1] // LANES
    for index in range(columns):
        out_ref[index * count : (index + 1) * count, :] = weighted[
            :, index * LANES : (index + 1) * LANES
        ]
    totals = as_row(totals + totals_so_far_ref[count:, 0:1])
    totals = jnp.concatenate([totals, jnp.zeros((1, LANES - count), jnp.float32)], axis=1)
    high = totals.astype(jnp.bfloat16).astype(jnp.float32)
    row = lax.broadcasted_iota(jnp.int32, (EXTRA, LANES), 0)
    out_ref[columns * count :, :] = jnp.where(row == 0, high, totals - high).astype(jnp.bfloat16)


def own_kernel(so_far_ref, totals_so_far_ref, bounds_ref, own_ref, keys_ref, weighted_ref, totals_ref):
    count = own_ref.shape[0]
    totals, weighted = partial_sums(own_ref[...], keys_ref[...], bounds_ref[...], False)
    weighted_ref[...] = weighted + so_far_ref[:count, :]
    totals_ref[...] = as_row(totals + totals_so_far_ref[:count, 0:1])


def finish_kernel(
    moves_ref,
    weighted_ref,
    totals_ref,
    back_ref,
    neighbour_hbm,
    score_hbm,
    neighbour_ref,
    score_ref,
    sems,
):
    count, features = neighbour_ref.shape
    columns = features // LANES
    back = [
        back_ref[index * count : (index + 1) * count, :].astype(jnp.float32)
        for index in range(columns)
    ]
    weighted = weighted_ref[...] + jnp.concatenate(back, axis=1)
    normed = (
        weighted * lax.rsqrt(jnp.mean(weighted * weighted, axis=-1, keepdims=True) + epsilon)
    ).astype(jnp.bfloat16)
    moves = moves_ref[...]
    copies = []
    for half in range(2):
        part = slice(half * features // 2, (half + 1) * features // 2)
        neighbour_ref[:, part] = lax.dot_general(
            moves, normed[:, part], (((0,), (0,)), ((), ())), preferred_element_type=jnp.float32
        ).astype(jnp.bfloat16)
        copies.append(
            pltpu.make_async_copy(
                neighbour_ref.at[:, part], neighbour_hbm.at[:, part], sems.at[half]
            )
        )
        copies[-1].start()
    pair = back_ref[columns * count :, :].astype(jnp.float32)
    totals = totals_ref[...] + (pair[0:1, :count] + pair[1:2, :count])
    scores = jnp.sum(moves.astype(jnp.float32) * as_column(jnp.log(totals)), axis=0, keepdims=True)
    score_ref[...] = scores.astype(jnp.bfloat16).reshape(count)
    copies.append(pltpu.make_async_copy(score_ref, score_hbm, sems.at[2]))
    copies[-1].start()
    for copy in copies:
        copy.wait()


EXTRA = 16
CORE, ACROSS, NEAR, FAR = 1, 2, 4, 8
GRID = 16


def gathered_body(embeddings, cluster_id):
    rows_dev, features = embeddings.shape
    vmem = pl.BlockSpec(memory_space=pltpu.VMEM)
    stored = pl.BlockSpec(memory_space=pltpu.HBM)

    def swap(value, bits):
        return lax.ppermute(value, "blk", [(device, device ^ bits) for device in range(GRID)])

    def block(kind, *shape):
        return jax.ShapeDtypeStruct(shape, kind)

    def kernel(body, name, out_shape, *inputs, specs=vmem, out_specs=vmem, scratch=()):
        return pl.pallas_call(
            body,
            out_shape=out_shape,
            in_specs=[specs] * len(inputs),
            out_specs=(out_specs,) * len(out_shape),
            scratch_shapes=scratch,
            compiler_params=pltpu.CompilerParams(vmem_limit_bytes=32 * 1024 * 1024),
            name=name,
        )(*inputs)

    rows = block(jnp.bfloat16, rows_dev, features)
    own, moves, ids = kernel(
        arrange_kernel,
        "arrange",
        (rows, block(jnp.bfloat16, rows_dev, rows_dev), block(jnp.int32, 1, rows_dev)),
        pltpu.with_memory_space_constraint(cluster_id, pltpu.HBM),
        pltpu.with_memory_space_constraint(embeddings, pltpu.HBM),
        specs=stored,
        scratch=(
            pltpu.VMEM((rows_dev,), jnp.int32),
            pltpu.VMEM((rows_dev, features), jnp.bfloat16),
            pltpu.SemaphoreType.DMA((2,)),
        ),
    )

    far, farther, near, beside = lax.optimization_barrier(
        tuple(swap(own, bits) for bits in (FAR, FAR | NEAR, NEAR, ACROSS))
    )
    mates = swap(jnp.concatenate([own, near, far, farther], axis=0), CORE)
    *so_far, bounds = kernel(
        first_kernel,
        "first",
        (
            block(jnp.float32, 2 * rows_dev, features),
            block(jnp.float32, 2 * rows_dev, LANES),
            block(jnp.int32, rows_dev, LANES),
        ),
        *(moves, ids, own, beside),
        *(own, near, far, farther),
    )
    (partial,) = kernel(
        beside_kernel,
        "beside",
        (block(jnp.bfloat16, rows_dev * features // LANES + EXTRA, LANES),),
        *(*so_far, bounds, beside, mates),
    )
    back = swap(partial, ACROSS)
    weighted, totals = kernel(
        own_kernel,
        "own",
        (block(jnp.float32, rows_dev, features), block(jnp.float32, 1, rows_dev)),
        *(*so_far, bounds, own, mates),
    )
    return tuple(
        kernel(
            finish_kernel,
            "finish",
            (rows, block(jnp.bfloat16, rows_dev)),
            *(moves, weighted, totals, back),
            out_specs=stored,
            scratch=(
                pltpu.VMEM((rows_dev, features), jnp.bfloat16),
                pltpu.VMEM((rows_dev,), jnp.bfloat16),
                pltpu.SemaphoreType.DMA((3,)),
            ),
        )
    )


def from_behind(value, axis, steps):
    count = lax.axis_size(axis)
    initial, last = (max(0, -steps), min(count, count - steps))
    return lax.ppermute(value, axis, [(source, source + steps) for source in range(initial, last)])


def pair_terms(queries, visiting, allowed):
    similar = jnp.dot(queries, visiting.T, preferred_element_type=jnp.float32)
    return jnp.where(allowed, jnp.exp(sharpness * (similar - 1.0)), jnp.zeros_like(similar))


def finish(weighted, totals):
    normed = (
        weighted * lax.rsqrt(jnp.mean(weighted * weighted, axis=-1, keepdims=True) + epsilon)
    ).astype(jnp.bfloat16)
    return (normed, jnp.log(totals).astype(jnp.bfloat16))


def collected_body(embeddings, cluster_id):
    rows_dev, features = embeddings.shape
    devices = lax.axis_size("blk")
    per_peer = rows_dev // devices
    clusters = devices // 4
    unit_rows = normalize_rows(embeddings)
    labels = jnp.arange(clusters, dtype=jnp.int32)
    counts = jnp.sum((cluster_id[:, None] == labels[None, :]).astype(jnp.int32), axis=0)
    group_ends = jnp.cumsum(counts // per_peer)

    def owner_cluster(device):
        in_range = (device >= 0) & (device < devices)
        return jnp.where(in_range, jnp.sum((device >= group_ends).astype(jnp.int32)), -1)

    position = jnp.arange(rows_dev, dtype=jnp.int32)
    arrange_order = jnp.argsort(cluster_id * rows_dev + position)
    inverse = jnp.argsort(arrange_order)
    arranged = unit_rows[arrange_order].reshape(devices, per_peer, features)
    held_rows = lax.all_to_all(arranged, "blk", split_axis=0, concat_axis=0, tiled=True).reshape(
        rows_dev, features
    )
    self_index = lax.axis_index("blk")
    mine = owner_cluster(self_index)
    weights = pair_terms(held_rows, held_rows, position[:, None] != position[None, :])
    totals = jnp.sum(weights, axis=1)
    weighted = jnp.dot(weights.astype(jnp.bfloat16), held_rows, preferred_element_type=jnp.float32)
    from_lower = held_rows
    from_upper = held_rows
    for distance in range(1, U_MAX):
        from_lower = from_behind(from_lower, "blk", 1)
        from_upper = from_behind(from_upper, "blk", -1)
        for visiting, source in (
            (from_lower, self_index - distance),
            (from_upper, self_index + distance),
        ):
            weights = pair_terms(held_rows, visiting, owner_cluster(source) == mine)
            totals = totals + jnp.sum(weights, axis=1)
            weighted = weighted + jnp.dot(
                weights.astype(jnp.bfloat16), visiting, preferred_element_type=jnp.float32
            )
    normed, scores = finish(weighted, totals)
    returned_rows, returned_scores = (
        lax.all_to_all(
            normed.reshape(devices, per_peer, features),
            "blk",
            split_axis=0,
            concat_axis=0,
            tiled=True,
        ),
        lax.all_to_all(
            scores.reshape(devices, per_peer), "blk", split_axis=0, concat_axis=0, tiled=True
        ),
    )
    neighbour = returned_rows.reshape(rows_dev, features)[inverse]
    dup_score = returned_scores.reshape(rows_dev)[inverse]
    return (neighbour, dup_score)


def solution(mesh):
    placed = (P(("groups", "blk"), None), P(("groups", "blk")))
    devices = mesh.shape["blk"]

    def body(embeddings, cluster_id):
        gathered = embeddings.size * embeddings.dtype.itemsize * devices
        fits = gathered <= GATHER_LIMIT and devices == GRID and embeddings.shape[0] % 16 == 0
        plan = gathered_body if fits else collected_body
        return plan(embeddings, cluster_id)

    return jax.shard_map(
        body,
        mesh=mesh,
        in_specs=placed,
        out_specs=(P(("groups", "blk"), None), P(("groups", "blk"))),
        check_vma=False,
    )
```

```python
import jax
import jax.numpy as jnp
from jax import lax
from jax.experimental import pallas as pl
from jax.experimental.pallas import tpu as pltpu
from jax.sharding import PartitionSpec as P

U_MAX = 8
GATHER_LIMIT = 4 * 1024 * 1024


sharpness = 10.0
epsilon = 1e-06


def normalize_rows(values):
    widened = values.astype(jnp.float32)
    return (
        widened
        * lax.rsqrt(jnp.mean(widened * widened, axis=-1, keepdims=True) + epsilon)
        * widened.shape[-1] ** (-0.5)
    ).astype(jnp.bfloat16)


def as_column(row):
    count = row.shape[1]
    across = lax.broadcasted_iota(jnp.int32, (count, count), 1)
    down = lax.broadcasted_iota(jnp.int32, (count, count), 0)
    return jnp.sum(jnp.where(across == down, row, jnp.zeros_like(row)), axis=1, keepdims=True)


def as_row(column):
    count = column.shape[0]
    across = lax.broadcasted_iota(jnp.int32, (count, count), 1)
    down = lax.broadcasted_iota(jnp.int32, (count, count), 0)
    return jnp.sum(jnp.where(across == down, column, jnp.zeros_like(column)), axis=0, keepdims=True)


LANES = 128


def arrange_kernel(ids_hbm, rows_hbm, out_ref, moves_ref, ids_out_ref, ids_ref, rows_ref, sems):
    ids_copy = pltpu.make_async_copy(ids_hbm, ids_ref, sems.at[0])
    rows_copy = pltpu.make_async_copy(rows_hbm, rows_ref, sems.at[1])
    ids_copy.start()
    rows_copy.start()
    count = rows_ref.shape[0]
    ids_copy.wait()
    ids_row = ids_ref[...].reshape(1, count)
    ids_column = as_column(ids_row)
    across = lax.broadcasted_iota(jnp.int32, (count, count), 1)
    down = lax.broadcasted_iota(jnp.int32, (count, count), 0)
    before = (ids_column < ids_row) | ((ids_column == ids_row) & (down < across))
    rank_row = jnp.sum(before.astype(jnp.int32), axis=0, keepdims=True)
    moves = (down == rank_row).astype(jnp.bfloat16)
    rows_copy.wait()
    unit = normalize_rows(rows_ref[...])
    out_ref[...] = jnp.dot(moves, unit, preferred_element_type=jnp.float32).astype(jnp.bfloat16)
    moves_ref[...] = moves
    ids_out_ref[...] = ids_row


def pack(out_ref, weighted, totals):
    count = weighted.shape[0]
    weighted = weighted.astype(jnp.bfloat16)
    columns = weighted.shape[1] // LANES
    for index in range(columns):
        out_ref[index * count : (index + 1) * count, :] = weighted[
            :, index * LANES : (index + 1) * LANES
        ]
    totals = as_row(totals)
    totals = jnp.concatenate([totals, jnp.zeros((1, LANES - count), jnp.float32)], axis=1)
    high = totals.astype(jnp.bfloat16).astype(jnp.float32)
    row = lax.broadcasted_iota(jnp.int32, (EXTRA, LANES), 0)
    out_ref[columns * count :, :] = jnp.where(row == 0, high, totals - high).astype(jnp.bfloat16)


def unpack(packed_ref, count):
    columns = packed_ref.shape[0] // count
    block = [
        packed_ref[index * count : (index + 1) * count, :].astype(jnp.float32)
        for index in range(columns)
    ]
    pair = packed_ref[columns * count :, :].astype(jnp.float32)
    return jnp.concatenate(block, axis=1), pair[0:1, :count] + pair[1:2, :count]


def partial_sums(queries, keys, bounds, own):
    count = bounds.shape[0]
    blocks = queries.shape[0] // count
    similar = lax.dot_general(
        queries, keys, (((1,), (1,)), ((), ())), preferred_element_type=jnp.float32
    )
    bounds = jnp.concatenate([bounds] * blocks, axis=0)
    key = lax.broadcasted_iota(jnp.int32, similar.shape, 1)
    place = lax.rem(key, count)
    allowed = (place >= bounds[:, 0:1]) & (place < bounds[:, 1:2])
    if own:
        query = lax.broadcasted_iota(jnp.int32, similar.shape, 0)
        allowed = allowed & ((key != query) | (key >= count))
    weights = jnp.where(allowed, jnp.exp(sharpness * (similar - 1.0)), 0.0)
    totals = jnp.sum(weights, axis=1, keepdims=True)
    return totals, jnp.dot(weights.astype(jnp.bfloat16), keys, preferred_element_type=jnp.float32)


def first_kernel(moves_ref, ids_ref, own_ref, beside_ref, key_ref, weighted_ref, totals_ref, bounds_ref):
    ids = ids_ref[...]
    label = jnp.sum(jnp.where(moves_ref[...] > 0, ids, 0), axis=1, keepdims=True)
    first = jnp.sum((ids < label).astype(jnp.int32), axis=1, keepdims=True)
    after = jnp.sum((ids <= label).astype(jnp.int32), axis=1, keepdims=True)
    lane = lax.broadcasted_iota(jnp.int32, bounds_ref.shape, 1)
    bounds = jnp.where(lane == 0, first, after)
    bounds_ref[...] = bounds
    own = own_ref[...]
    queries = jnp.concatenate([own, beside_ref[...]], axis=0)
    keys = jnp.concatenate([own, key_ref[...]], axis=0)
    totals, weighted = partial_sums(queries, keys, bounds, True)
    weighted_ref[...] = weighted
    totals_ref[...] = jnp.broadcast_to(totals, totals_ref.shape)


def visitor_kernel(bounds_ref, visitor_ref, own_ref, beside_ref, mates_ref, out_ref):
    keys = jnp.concatenate([own_ref[...], beside_ref[...], mates_ref[...]], axis=0)
    totals, weighted = partial_sums(visitor_ref[...], keys, bounds_ref[...], False)
    pack(out_ref, weighted, totals)


def other_keys(mates_ref, visitor_ref, later_ref):
    visitor = visitor_ref[...]
    return jnp.concatenate([mates_ref[: visitor.shape[0], :], visitor, later_ref[...]], axis=0)


def beside_kernel(so_far_ref, totals_so_far_ref, bounds_ref, beside_ref, *refs):
    *key_refs, out_ref = refs
    count = beside_ref.shape[0]
    totals, weighted = partial_sums(beside_ref[...], other_keys(*key_refs), bounds_ref[...], False)
    pack(out_ref, weighted + so_far_ref[count:, :], totals + totals_so_far_ref[count:, 0:1])


def own_kernel(so_far_ref, totals_so_far_ref, bounds_ref, own_ref, *refs):
    *key_refs, weighted_ref, totals_ref = refs
    count = own_ref.shape[0]
    totals, weighted = partial_sums(own_ref[...], other_keys(*key_refs), bounds_ref[...], False)
    weighted_ref[...] = weighted + so_far_ref[:count, :]
    totals_ref[...] = as_row(totals + totals_so_far_ref[:count, 0:1])


def finish_kernel(moves_ref, weighted_ref, totals_ref, *refs):
    *back_refs, neighbour_hbm, score_hbm, neighbour_ref, score_ref, sems = refs
    count = neighbour_ref.shape[0]
    weighted, totals = weighted_ref[...], totals_ref[...]
    for back_ref in back_refs:
        back, back_totals = unpack(back_ref, count)
        weighted = weighted + back
        totals = totals + back_totals
    normed = (
        weighted * lax.rsqrt(jnp.mean(weighted * weighted, axis=-1, keepdims=True) + epsilon)
    ).astype(jnp.bfloat16)
    moves = moves_ref[...]
    neighbour_ref[...] = lax.dot_general(
        moves, normed, (((0,), (0,)), ((), ())), preferred_element_type=jnp.float32
    ).astype(jnp.bfloat16)
    neighbour_copy = pltpu.make_async_copy(neighbour_ref, neighbour_hbm, sems.at[0])
    neighbour_copy.start()
    scores = jnp.sum(moves.astype(jnp.float32) * as_column(jnp.log(totals)), axis=0, keepdims=True)
    score_ref[...] = scores.astype(jnp.bfloat16).reshape(count)
    score_copy = pltpu.make_async_copy(score_ref, score_hbm, sems.at[1])
    score_copy.start()
    neighbour_copy.wait()
    score_copy.wait()


EXTRA = 16
CORE, ACROSS, MIRROR = 1, 2, 12
PLANE, GRID = 4, 16
NEXT = (1, 3, 0, 2)


def gathered_body(embeddings, cluster_id):
    rows_dev, features = embeddings.shape
    vmem = pl.BlockSpec(memory_space=pltpu.VMEM)
    stored = pl.BlockSpec(memory_space=pltpu.HBM)

    def swap(value, bits):
        return lax.ppermute(value, "blk", [(device, device ^ bits) for device in range(GRID)])

    def visit(value, home):
        pairs = [
            (device, NEXT[device // PLANE] * PLANE + device % PLANE) for device in range(GRID)
        ]
        return lax.ppermute(value, "blk", [pair[::-1] for pair in pairs] if home else pairs)

    def block(kind, *shape):
        return jax.ShapeDtypeStruct(shape, kind)

    def kernel(body, name, out_shape, *inputs, specs=vmem, out_specs=vmem, scratch=()):
        return pl.pallas_call(
            body,
            out_shape=out_shape,
            in_specs=[specs] * len(inputs),
            out_specs=(out_specs,) * len(out_shape),
            scratch_shapes=scratch,
            compiler_params=pltpu.CompilerParams(vmem_limit_bytes=32 * 1024 * 1024),
            name=name,
        )(*inputs)

    rows = block(jnp.bfloat16, rows_dev, features)
    own, moves, ids = kernel(
        arrange_kernel,
        "arrange",
        (rows, block(jnp.bfloat16, rows_dev, rows_dev), block(jnp.int32, 1, rows_dev)),
        pltpu.with_memory_space_constraint(cluster_id, pltpu.HBM),
        pltpu.with_memory_space_constraint(embeddings, pltpu.HBM),
        specs=stored,
        scratch=(
            pltpu.VMEM((rows_dev,), jnp.int32),
            pltpu.VMEM((rows_dev, features), jnp.bfloat16),
            pltpu.SemaphoreType.DMA((2,)),
        ),
    )

    packed = block(jnp.bfloat16, rows_dev * features // LANES + EXTRA, LANES)
    beside, mirror = lax.optimization_barrier((swap(own, ACROSS), swap(own, MIRROR)))
    visitor = visit(own, home=False)
    mates = swap(jnp.concatenate([own, beside], axis=0), CORE)
    later = swap(jnp.concatenate([mirror, visitor], axis=0), CORE)
    *so_far, bounds = kernel(
        first_kernel,
        "first",
        (
            block(jnp.float32, 2 * rows_dev, features),
            block(jnp.float32, 2 * rows_dev, LANES),
            block(jnp.int32, rows_dev, LANES),
        ),
        *(moves, ids, own, beside, mirror),
    )
    (partial,) = kernel(
        visitor_kernel, "visitor", (packed,), bounds, visitor, own, beside, mates
    )
    back_home = visit(partial, home=True)
    keys = (mates, visitor, later)
    (partial,) = kernel(beside_kernel, "beside", (packed,), *so_far, bounds, beside, *keys)
    back = swap(partial, ACROSS)
    weighted, totals = kernel(
        own_kernel,
        "own",
        (block(jnp.float32, rows_dev, features), block(jnp.float32, 1, rows_dev)),
        *(*so_far, bounds, own, *keys),
    )
    weighted, back_home = lax.optimization_barrier((weighted, back_home))
    return tuple(
        kernel(
            finish_kernel,
            "finish",
            (rows, block(jnp.bfloat16, rows_dev)),
            *(moves, weighted, totals, back, back_home),
            out_specs=stored,
            scratch=(
                pltpu.VMEM((rows_dev, features), jnp.bfloat16),
                pltpu.VMEM((rows_dev,), jnp.bfloat16),
                pltpu.SemaphoreType.DMA((2,)),
            ),
        )
    )


def from_behind(value, axis, steps):
    count = lax.axis_size(axis)
    initial, last = (max(0, -steps), min(count, count - steps))
    return lax.ppermute(value, axis, [(source, source + steps) for source in range(initial, last)])


def pair_terms(queries, visiting, allowed):
    similar = jnp.dot(queries, visiting.T, preferred_element_type=jnp.float32)
    return jnp.where(allowed, jnp.exp(sharpness * (similar - 1.0)), jnp.zeros_like(similar))


def finish(weighted, totals):
    normed = (
        weighted * lax.rsqrt(jnp.mean(weighted * weighted, axis=-1, keepdims=True) + epsilon)
    ).astype(jnp.bfloat16)
    return (normed, jnp.log(totals).astype(jnp.bfloat16))


def collected_body(embeddings, cluster_id):
    rows_dev, features = embeddings.shape
    devices = lax.axis_size("blk")
    per_peer = rows_dev // devices
    clusters = devices // 4
    unit_rows = normalize_rows(embeddings)
    labels = jnp.arange(clusters, dtype=jnp.int32)
    counts = jnp.sum((cluster_id[:, None] == labels[None, :]).astype(jnp.int32), axis=0)
    group_ends = jnp.cumsum(counts // per_peer)

    def owner_cluster(device):
        in_range = (device >= 0) & (device < devices)
        return jnp.where(in_range, jnp.sum((device >= group_ends).astype(jnp.int32)), -1)

    position = jnp.arange(rows_dev, dtype=jnp.int32)
    arrange_order = jnp.argsort(cluster_id * rows_dev + position)
    inverse = jnp.argsort(arrange_order)
    arranged = unit_rows[arrange_order].reshape(devices, per_peer, features)
    held_rows = lax.all_to_all(arranged, "blk", split_axis=0, concat_axis=0, tiled=True).reshape(
        rows_dev, features
    )
    self_index = lax.axis_index("blk")
    mine = owner_cluster(self_index)
    weights = pair_terms(held_rows, held_rows, position[:, None] != position[None, :])
    totals = jnp.sum(weights, axis=1)
    weighted = jnp.dot(weights.astype(jnp.bfloat16), held_rows, preferred_element_type=jnp.float32)
    from_lower = held_rows
    from_upper = held_rows
    for distance in range(1, U_MAX):
        from_lower = from_behind(from_lower, "blk", 1)
        from_upper = from_behind(from_upper, "blk", -1)
        for visiting, source in (
            (from_lower, self_index - distance),
            (from_upper, self_index + distance),
        ):
            weights = pair_terms(held_rows, visiting, owner_cluster(source) == mine)
            totals = totals + jnp.sum(weights, axis=1)
            weighted = weighted + jnp.dot(
                weights.astype(jnp.bfloat16), visiting, preferred_element_type=jnp.float32
            )
    normed, scores = finish(weighted, totals)
    returned_rows, returned_scores = (
        lax.all_to_all(
            normed.reshape(devices, per_peer, features),
            "blk",
            split_axis=0,
            concat_axis=0,
            tiled=True,
        ),
        lax.all_to_all(
            scores.reshape(devices, per_peer), "blk", split_axis=0, concat_axis=0, tiled=True
        ),
    )
    neighbour = returned_rows.reshape(rows_dev, features)[inverse]
    dup_score = returned_scores.reshape(rows_dev)[inverse]
    return (neighbour, dup_score)


def solution(mesh):
    placed = (P(("groups", "blk"), None), P(("groups", "blk")))
    devices = mesh.shape["blk"]

    def body(embeddings, cluster_id):
        gathered = embeddings.size * embeddings.dtype.itemsize * devices
        fits = gathered <= GATHER_LIMIT and devices == GRID and embeddings.shape[0] % 16 == 0
        plan = gathered_body if fits else collected_body
        return plan(embeddings, cluster_id)

    return jax.shard_map(
        body,
        mesh=mesh,
        in_specs=placed,
        out_specs=(P(("groups", "blk"), None), P(("groups", "blk"))),
        check_vma=False,
    )
```

```python
import jax
import jax.numpy as jnp
from jax import lax
from jax.experimental import pallas as pl
from jax.experimental.pallas import tpu as pltpu
from jax.sharding import PartitionSpec as P

U_MAX = 8
GATHER_LIMIT = 4 * 1024 * 1024


sharpness = 10.0
epsilon = 1e-06


def normalize_rows(values):
    widened = values.astype(jnp.float32)
    return (
        widened
        * lax.rsqrt(jnp.mean(widened * widened, axis=-1, keepdims=True) + epsilon)
        * widened.shape[-1] ** (-0.5)
    ).astype(jnp.bfloat16)


def as_column(row):
    count = row.shape[1]
    across = lax.broadcasted_iota(jnp.int32, (count, count), 1)
    down = lax.broadcasted_iota(jnp.int32, (count, count), 0)
    return jnp.sum(jnp.where(across == down, row, jnp.zeros_like(row)), axis=1, keepdims=True)


def as_row(column):
    count = column.shape[0]
    across = lax.broadcasted_iota(jnp.int32, (count, count), 1)
    down = lax.broadcasted_iota(jnp.int32, (count, count), 0)
    return jnp.sum(jnp.where(across == down, column, jnp.zeros_like(column)), axis=0, keepdims=True)


LANES = 128


def arrange_kernel(ids_hbm, rows_hbm, out_ref, moves_ref, ids_out_ref, ids_ref, rows_ref, sems):
    ids_copy = pltpu.make_async_copy(ids_hbm, ids_ref, sems.at[0])
    rows_copy = pltpu.make_async_copy(rows_hbm, rows_ref, sems.at[1])
    ids_copy.start()
    rows_copy.start()
    count = rows_ref.shape[0]
    ids_copy.wait()
    ids_row = ids_ref[...].reshape(1, count)
    ids_column = as_column(ids_row)
    across = lax.broadcasted_iota(jnp.int32, (count, count), 1)
    down = lax.broadcasted_iota(jnp.int32, (count, count), 0)
    before = (ids_column < ids_row) | ((ids_column == ids_row) & (down < across))
    rank_row = jnp.sum(before.astype(jnp.int32), axis=0, keepdims=True)
    moves = (down == rank_row).astype(jnp.bfloat16)
    rows_copy.wait()
    unit = normalize_rows(rows_ref[...])
    out_ref[...] = jnp.dot(moves, unit, preferred_element_type=jnp.float32).astype(jnp.bfloat16)
    moves_ref[...] = moves
    ids_out_ref[...] = ids_row


def partial_sums(queries, keys, bounds, own):
    count = bounds.shape[0]
    blocks = queries.shape[0] // count
    similar = lax.dot_general(
        queries, keys, (((1,), (1,)), ((), ())), preferred_element_type=jnp.float32
    )
    bounds = jnp.concatenate([bounds] * blocks, axis=0)
    key = lax.broadcasted_iota(jnp.int32, similar.shape, 1)
    place = lax.rem(key, count)
    allowed = (place >= bounds[:, 0:1]) & (place < bounds[:, 1:2])
    if own:
        query = lax.broadcasted_iota(jnp.int32, similar.shape, 0)
        allowed = allowed & ((key != query) | (key >= count))
    weights = jnp.where(allowed, jnp.exp(sharpness * (similar - 1.0)), 0.0)
    totals = jnp.sum(weights, axis=1, keepdims=True)
    return totals, jnp.dot(weights.astype(jnp.bfloat16), keys, preferred_element_type=jnp.float32)


def first_kernel(moves_ref, ids_ref, own_ref, beside_ref, *refs):
    *key_refs, weighted_ref, totals_ref, bounds_ref = refs
    ids = ids_ref[...]
    label = jnp.sum(jnp.where(moves_ref[...] > 0, ids, 0), axis=1, keepdims=True)
    first = jnp.sum((ids < label).astype(jnp.int32), axis=1, keepdims=True)
    after = jnp.sum((ids <= label).astype(jnp.int32), axis=1, keepdims=True)
    lane = lax.broadcasted_iota(jnp.int32, bounds_ref.shape, 1)
    bounds = jnp.where(lane == 0, first, after)
    bounds_ref[...] = bounds
    queries = jnp.concatenate([own_ref[...], beside_ref[...]], axis=0)
    keys = jnp.concatenate([ref[...] for ref in key_refs], axis=0)
    totals, weighted = partial_sums(queries, keys, bounds, True)
    weighted_ref[...] = weighted
    totals_ref[...] = jnp.broadcast_to(totals, totals_ref.shape)


def beside_kernel(so_far_ref, totals_so_far_ref, bounds_ref, beside_ref, keys_ref, out_ref):
    count = beside_ref.shape[0]
    totals, weighted = partial_sums(beside_ref[...], keys_ref[...], bounds_ref[...], False)
    weighted = (weighted + so_far_ref[count:, :]).astype(jnp.bfloat16)
    columns = weighted.shape[1] // LANES
    for index in range(columns):
        out_ref[index * count : (index + 1) * count, :] = weighted[
            :, index * LANES : (index + 1) * LANES
        ]
    totals = as_row(totals + totals_so_far_ref[count:, 0:1])
    totals = jnp.concatenate([totals, jnp.zeros((1, LANES - count), jnp.float32)], axis=1)
    high = totals.astype(jnp.bfloat16).astype(jnp.float32)
    row = lax.broadcasted_iota(jnp.int32, (EXTRA, LANES), 0)
    out_ref[columns * count :, :] = jnp.where(row == 0, high, totals - high).astype(jnp.bfloat16)


def own_kernel(so_far_ref, totals_so_far_ref, bounds_ref, own_ref, keys_ref, weighted_ref, totals_ref):
    count = own_ref.shape[0]
    totals, weighted = partial_sums(own_ref[...], keys_ref[...], bounds_ref[...], False)
    weighted_ref[...] = weighted + so_far_ref[:count, :]
    totals_ref[...] = as_row(totals + totals_so_far_ref[:count, 0:1])


def finish_kernel(
    moves_ref,
    weighted_ref,
    totals_ref,
    back_ref,
    neighbour_hbm,
    score_hbm,
    neighbour_ref,
    score_ref,
    sems,
):
    count, features = neighbour_ref.shape
    columns = features // LANES
    back = [
        back_ref[index * count : (index + 1) * count, :].astype(jnp.float32)
        for index in range(columns)
    ]
    weighted = weighted_ref[...] + jnp.concatenate(back, axis=1)
    normed = (
        weighted * lax.rsqrt(jnp.mean(weighted * weighted, axis=-1, keepdims=True) + epsilon)
    ).astype(jnp.bfloat16)
    moves = moves_ref[...]
    copies = []
    for half in range(2):
        part = slice(half * features // 2, (half + 1) * features // 2)
        neighbour_ref[:, part] = lax.dot_general(
            moves, normed[:, part], (((0,), (0,)), ((), ())), preferred_element_type=jnp.float32
        ).astype(jnp.bfloat16)
        copies.append(
            pltpu.make_async_copy(
                neighbour_ref.at[:, part], neighbour_hbm.at[:, part], sems.at[half]
            )
        )
        copies[-1].start()
    pair = back_ref[columns * count :, :].astype(jnp.float32)
    totals = totals_ref[...] + (pair[0:1, :count] + pair[1:2, :count])
    scores = jnp.sum(moves.astype(jnp.float32) * as_column(jnp.log(totals)), axis=0, keepdims=True)
    score_ref[...] = scores.astype(jnp.bfloat16).reshape(count)
    copies.append(pltpu.make_async_copy(score_ref, score_hbm, sems.at[2]))
    copies[-1].start()
    for copy in copies:
        copy.wait()


EXTRA = 16
CORE, ACROSS, NEAR, FAR = 1, 2, 4, 8
GRID = 16


def gathered_body(embeddings, cluster_id):
    rows_dev, features = embeddings.shape
    vmem = pl.BlockSpec(memory_space=pltpu.VMEM)
    stored = pl.BlockSpec(memory_space=pltpu.HBM)

    def swap(value, bits):
        return lax.ppermute(value, "blk", [(device, device ^ bits) for device in range(GRID)])

    def block(kind, *shape):
        return jax.ShapeDtypeStruct(shape, kind)

    def kernel(body, name, out_shape, *inputs, specs=vmem, out_specs=vmem, scratch=()):
        return pl.pallas_call(
            body,
            out_shape=out_shape,
            in_specs=[specs] * len(inputs),
            out_specs=(out_specs,) * len(out_shape),
            scratch_shapes=scratch,
            compiler_params=pltpu.CompilerParams(vmem_limit_bytes=32 * 1024 * 1024),
            name=name,
        )(*inputs)

    rows = block(jnp.bfloat16, rows_dev, features)
    own, moves, ids = kernel(
        arrange_kernel,
        "arrange",
        (rows, block(jnp.bfloat16, rows_dev, rows_dev), block(jnp.int32, 1, rows_dev)),
        pltpu.with_memory_space_constraint(cluster_id, pltpu.HBM),
        pltpu.with_memory_space_constraint(embeddings, pltpu.HBM),
        specs=stored,
        scratch=(
            pltpu.VMEM((rows_dev,), jnp.int32),
            pltpu.VMEM((rows_dev, features), jnp.bfloat16),
            pltpu.SemaphoreType.DMA((2,)),
        ),
    )

    far, diagonal, across, beside, mate = lax.optimization_barrier(
        tuple(swap(own, bits) for bits in (FAR, FAR | ACROSS, ACROSS, NEAR, CORE))
    )
    mates = swap(jnp.concatenate([across, far, diagonal], axis=0), CORE)
    *so_far, bounds = kernel(
        first_kernel,
        "first",
        (
            block(jnp.float32, 2 * rows_dev, features),
            block(jnp.float32, 2 * rows_dev, LANES),
            block(jnp.int32, rows_dev, LANES),
        ),
        *(moves, ids, own, beside),
        *(own, mate, across, far, diagonal),
    )
    (partial,) = kernel(
        beside_kernel,
        "beside",
        (block(jnp.bfloat16, rows_dev * features // LANES + EXTRA, LANES),),
        *(*so_far, bounds, beside, mates),
    )
    back = swap(partial, NEAR)
    weighted, totals = kernel(
        own_kernel,
        "own",
        (block(jnp.float32, rows_dev, features), block(jnp.float32, 1, rows_dev)),
        *(*so_far, bounds, own, mates),
    )
    return tuple(
        kernel(
            finish_kernel,
            "finish",
            (rows, block(jnp.bfloat16, rows_dev)),
            *(moves, weighted, totals, back),
            out_specs=stored,
            scratch=(
                pltpu.VMEM((rows_dev, features), jnp.bfloat16),
                pltpu.VMEM((rows_dev,), jnp.bfloat16),
                pltpu.SemaphoreType.DMA((3,)),
            ),
        )
    )


def from_behind(value, axis, steps):
    count = lax.axis_size(axis)
    initial, last = (max(0, -steps), min(count, count - steps))
    return lax.ppermute(value, axis, [(source, source + steps) for source in range(initial, last)])


def pair_terms(queries, visiting, allowed):
    similar = jnp.dot(queries, visiting.T, preferred_element_type=jnp.float32)
    return jnp.where(allowed, jnp.exp(sharpness * (similar - 1.0)), jnp.zeros_like(similar))


def finish(weighted, totals):
    normed = (
        weighted * lax.rsqrt(jnp.mean(weighted * weighted, axis=-1, keepdims=True) + epsilon)
    ).astype(jnp.bfloat16)
    return (normed, jnp.log(totals).astype(jnp.bfloat16))


def collected_body(embeddings, cluster_id):
    rows_dev, features = embeddings.shape
    devices = lax.axis_size("blk")
    per_peer = rows_dev // devices
    clusters = devices // 4
    unit_rows = normalize_rows(embeddings)
    labels = jnp.arange(clusters, dtype=jnp.int32)
    counts = jnp.sum((cluster_id[:, None] == labels[None, :]).astype(jnp.int32), axis=0)
    group_ends = jnp.cumsum(counts // per_peer)

    def owner_cluster(device):
        in_range = (device >= 0) & (device < devices)
        return jnp.where(in_range, jnp.sum((device >= group_ends).astype(jnp.int32)), -1)

    position = jnp.arange(rows_dev, dtype=jnp.int32)
    arrange_order = jnp.argsort(cluster_id * rows_dev + position)
    inverse = jnp.argsort(arrange_order)
    arranged = unit_rows[arrange_order].reshape(devices, per_peer, features)
    held_rows = lax.all_to_all(arranged, "blk", split_axis=0, concat_axis=0, tiled=True).reshape(
        rows_dev, features
    )
    self_index = lax.axis_index("blk")
    mine = owner_cluster(self_index)
    weights = pair_terms(held_rows, held_rows, position[:, None] != position[None, :])
    totals = jnp.sum(weights, axis=1)
    weighted = jnp.dot(weights.astype(jnp.bfloat16), held_rows, preferred_element_type=jnp.float32)
    from_lower = held_rows
    from_upper = held_rows
    for distance in range(1, U_MAX):
        from_lower = from_behind(from_lower, "blk", 1)
        from_upper = from_behind(from_upper, "blk", -1)
        for visiting, source in (
            (from_lower, self_index - distance),
            (from_upper, self_index + distance),
        ):
            weights = pair_terms(held_rows, visiting, owner_cluster(source) == mine)
            totals = totals + jnp.sum(weights, axis=1)
            weighted = weighted + jnp.dot(
                weights.astype(jnp.bfloat16), visiting, preferred_element_type=jnp.float32
            )
    normed, scores = finish(weighted, totals)
    returned_rows, returned_scores = (
        lax.all_to_all(
            normed.reshape(devices, per_peer, features),
            "blk",
            split_axis=0,
            concat_axis=0,
            tiled=True,
        ),
        lax.all_to_all(
            scores.reshape(devices, per_peer), "blk", split_axis=0, concat_axis=0, tiled=True
        ),
    )
    neighbour = returned_rows.reshape(rows_dev, features)[inverse]
    dup_score = returned_scores.reshape(rows_dev)[inverse]
    return (neighbour, dup_score)


def solution(mesh):
    placed = (P(("groups", "blk"), None), P(("groups", "blk")))
    devices = mesh.shape["blk"]

    def body(embeddings, cluster_id):
        gathered = embeddings.size * embeddings.dtype.itemsize * devices
        fits = gathered <= GATHER_LIMIT and devices == GRID and embeddings.shape[0] % 16 == 0
        plan = gathered_body if fits else collected_body
        return plan(embeddings, cluster_id)

    return jax.shard_map(
        body,
        mesh=mesh,
        in_specs=placed,
        out_specs=(P(("groups", "blk"), None), P(("groups", "blk"))),
        check_vma=False,
    )
```

```python
import jax
import jax.numpy as jnp
from jax import lax
from jax.experimental import pallas as pl
from jax.experimental.pallas import tpu as pltpu
from jax.sharding import PartitionSpec as P

U_MAX = 8
GATHER_LIMIT = 4 * 1024 * 1024


sharpness = 10.0
epsilon = 1e-06


def normalize_rows(values):
    widened = values.astype(jnp.float32)
    return (
        widened
        * lax.rsqrt(jnp.mean(widened * widened, axis=-1, keepdims=True) + epsilon)
        * widened.shape[-1] ** (-0.5)
    ).astype(jnp.bfloat16)


def as_column(row):
    count = row.shape[1]
    across = lax.broadcasted_iota(jnp.int32, (count, count), 1)
    down = lax.broadcasted_iota(jnp.int32, (count, count), 0)
    return jnp.sum(jnp.where(across == down, row, jnp.zeros_like(row)), axis=1, keepdims=True)


def as_row(column):
    count = column.shape[0]
    across = lax.broadcasted_iota(jnp.int32, (count, count), 1)
    down = lax.broadcasted_iota(jnp.int32, (count, count), 0)
    return jnp.sum(jnp.where(across == down, column, jnp.zeros_like(column)), axis=0, keepdims=True)


LANES = 128


def arrange_kernel(ids_hbm, rows_hbm, out_ref, moves_ref, ids_out_ref, ids_ref, rows_ref, sems):
    ids_copy = pltpu.make_async_copy(ids_hbm, ids_ref, sems.at[0])
    rows_copy = pltpu.make_async_copy(rows_hbm, rows_ref, sems.at[1])
    ids_copy.start()
    rows_copy.start()
    count = rows_ref.shape[0]
    ids_copy.wait()
    ids_row = ids_ref[...].reshape(1, count)
    ids_column = as_column(ids_row)
    across = lax.broadcasted_iota(jnp.int32, (count, count), 1)
    down = lax.broadcasted_iota(jnp.int32, (count, count), 0)
    before = (ids_column < ids_row) | ((ids_column == ids_row) & (down < across))
    rank_row = jnp.sum(before.astype(jnp.int32), axis=0, keepdims=True)
    moves = (down == rank_row).astype(jnp.bfloat16)
    rows_copy.wait()
    unit = normalize_rows(rows_ref[...])
    out_ref[...] = jnp.dot(moves, unit, preferred_element_type=jnp.float32).astype(jnp.bfloat16)
    moves_ref[...] = moves
    ids_out_ref[...] = ids_row


def partial_sums(queries, keys, bounds, own):
    count = bounds.shape[0]
    blocks = queries.shape[0] // count
    similar = lax.dot_general(
        queries, keys, (((1,), (1,)), ((), ())), preferred_element_type=jnp.float32
    )
    bounds = jnp.concatenate([bounds] * blocks, axis=0)
    key = lax.broadcasted_iota(jnp.int32, similar.shape, 1)
    place = lax.rem(key, count)
    allowed = (place >= bounds[:, 0:1]) & (place < bounds[:, 1:2])
    if own:
        query = lax.broadcasted_iota(jnp.int32, similar.shape, 0)
        allowed = allowed & ((key != query) | (key >= count))
    weights = jnp.where(allowed, jnp.exp(sharpness * (similar - 1.0)), 0.0)
    totals = jnp.sum(weights, axis=1, keepdims=True)
    return totals, jnp.dot(weights.astype(jnp.bfloat16), keys, preferred_element_type=jnp.float32)


def first_kernel(moves_ref, ids_ref, own_ref, beside_ref, *refs):
    *key_refs, weighted_ref, totals_ref, bounds_ref = refs
    ids = ids_ref[...]
    label = jnp.sum(jnp.where(moves_ref[...] > 0, ids, 0), axis=1, keepdims=True)
    first = jnp.sum((ids < label).astype(jnp.int32), axis=1, keepdims=True)
    after = jnp.sum((ids <= label).astype(jnp.int32), axis=1, keepdims=True)
    lane = lax.broadcasted_iota(jnp.int32, bounds_ref.shape, 1)
    bounds = jnp.where(lane == 0, first, after)
    bounds_ref[...] = bounds
    queries = jnp.concatenate([own_ref[...], beside_ref[...]], axis=0)
    keys = jnp.concatenate([ref[...] for ref in key_refs], axis=0)
    totals, weighted = partial_sums(queries, keys, bounds, True)
    weighted_ref[...] = weighted
    totals_ref[...] = jnp.broadcast_to(totals, totals_ref.shape)


def beside_kernel(so_far_ref, totals_so_far_ref, bounds_ref, beside_ref, keys_ref, out_ref):
    count = beside_ref.shape[0]
    totals, weighted = partial_sums(beside_ref[...], keys_ref[...], bounds_ref[...], False)
    weighted = (weighted + so_far_ref[count:, :]).astype(jnp.bfloat16)
    columns = weighted.shape[1] // LANES
    for index in range(columns):
        out_ref[index * count : (index + 1) * count, :] = weighted[
            :, index * LANES : (index + 1) * LANES
        ]
    totals = as_row(totals + totals_so_far_ref[count:, 0:1])
    totals = jnp.concatenate([totals, jnp.zeros((1, LANES - count), jnp.float32)], axis=1)
    high = totals.astype(jnp.bfloat16).astype(jnp.float32)
    row = lax.broadcasted_iota(jnp.int32, (EXTRA, LANES), 0)
    out_ref[columns * count :, :] = jnp.where(row == 0, high, totals - high).astype(jnp.bfloat16)


def own_kernel(so_far_ref, totals_so_far_ref, bounds_ref, own_ref, keys_ref, weighted_ref, totals_ref):
    count = own_ref.shape[0]
    totals, weighted = partial_sums(own_ref[...], keys_ref[...], bounds_ref[...], False)
    weighted_ref[...] = weighted + so_far_ref[:count, :]
    totals_ref[...] = as_row(totals + totals_so_far_ref[:count, 0:1])


def finish_kernel(
    moves_ref,
    weighted_ref,
    totals_ref,
    back_ref,
    neighbour_hbm,
    score_hbm,
    neighbour_ref,
    score_ref,
    sems,
):
    count, features = neighbour_ref.shape
    columns = features // LANES
    back = [
        back_ref[index * count : (index + 1) * count, :].astype(jnp.float32)
        for index in range(columns)
    ]
    weighted = weighted_ref[...] + jnp.concatenate(back, axis=1)
    normed = (
        weighted * lax.rsqrt(jnp.mean(weighted * weighted, axis=-1, keepdims=True) + epsilon)
    ).astype(jnp.bfloat16)
    moves = moves_ref[...]
    copies = []
    for half in range(2):
        part = slice(half * features // 2, (half + 1) * features // 2)
        neighbour_ref[:, part] = lax.dot_general(
            moves, normed[:, part], (((0,), (0,)), ((), ())), preferred_element_type=jnp.float32
        ).astype(jnp.bfloat16)
        copies.append(
            pltpu.make_async_copy(
                neighbour_ref.at[:, part], neighbour_hbm.at[:, part], sems.at[half]
            )
        )
        copies[-1].start()
    pair = back_ref[columns * count :, :].astype(jnp.float32)
    totals = totals_ref[...] + (pair[0:1, :count] + pair[1:2, :count])
    scores = jnp.sum(moves.astype(jnp.float32) * as_column(jnp.log(totals)), axis=0, keepdims=True)
    score_ref[...] = scores.astype(jnp.bfloat16).reshape(count)
    copies.append(pltpu.make_async_copy(score_ref, score_hbm, sems.at[2]))
    copies[-1].start()
    for copy in copies:
        copy.wait()


EXTRA = 16
CORE, ACROSS, NEAR, FAR = 1, 2, 4, 8
GRID = 16
Z_TURNS = ((FAR, FAR | NEAR, NEAR), (FAR, NEAR, FAR | NEAR))


def gathered_body(embeddings, cluster_id):
    rows_dev, features = embeddings.shape
    vmem = pl.BlockSpec(memory_space=pltpu.VMEM)
    stored = pl.BlockSpec(memory_space=pltpu.HBM)

    def swap(value, bits):
        pairs = [(device, device ^ bits[device & CORE]) for device in range(GRID)]
        return lax.ppermute(value, "blk", pairs)

    def block(kind, *shape):
        return jax.ShapeDtypeStruct(shape, kind)

    def kernel(body, name, out_shape, *inputs, specs=vmem, out_specs=vmem, scratch=()):
        return pl.pallas_call(
            body,
            out_shape=out_shape,
            in_specs=[specs] * len(inputs),
            out_specs=(out_specs,) * len(out_shape),
            scratch_shapes=scratch,
            compiler_params=pltpu.CompilerParams(vmem_limit_bytes=32 * 1024 * 1024),
            name=name,
        )(*inputs)

    rows = block(jnp.bfloat16, rows_dev, features)
    own, moves, ids = kernel(
        arrange_kernel,
        "arrange",
        (rows, block(jnp.bfloat16, rows_dev, rows_dev), block(jnp.int32, 1, rows_dev)),
        pltpu.with_memory_space_constraint(cluster_id, pltpu.HBM),
        pltpu.with_memory_space_constraint(embeddings, pltpu.HBM),
        specs=stored,
        scratch=(
            pltpu.VMEM((rows_dev,), jnp.int32),
            pltpu.VMEM((rows_dev, features), jnp.bfloat16),
            pltpu.SemaphoreType.DMA((2,)),
        ),
    )

    *visiting, beside, mate = lax.optimization_barrier(
        (*(swap(own, turn) for turn in zip(*Z_TURNS)), swap(own, (ACROSS,) * 2), swap(own, (CORE,) * 2))
    )
    mates = swap(jnp.concatenate(visiting, axis=0), (CORE,) * 2)
    *so_far, bounds = kernel(
        first_kernel,
        "first",
        (
            block(jnp.float32, 2 * rows_dev, features),
            block(jnp.float32, 2 * rows_dev, LANES),
            block(jnp.int32, rows_dev, LANES),
        ),
        *(moves, ids, own, beside),
        *(own, mate, *visiting),
    )
    (partial,) = kernel(
        beside_kernel,
        "beside",
        (block(jnp.bfloat16, rows_dev * features // LANES + EXTRA, LANES),),
        *(*so_far, bounds, beside, mates),
    )
    back = swap(partial, (ACROSS,) * 2)
    weighted, totals = kernel(
        own_kernel,
        "own",
        (block(jnp.float32, rows_dev, features), block(jnp.float32, 1, rows_dev)),
        *(*so_far, bounds, own, mates),
    )
    return tuple(
        kernel(
            finish_kernel,
            "finish",
            (rows, block(jnp.bfloat16, rows_dev)),
            *(moves, weighted, totals, back),
            out_specs=stored,
            scratch=(
                pltpu.VMEM((rows_dev, features), jnp.bfloat16),
                pltpu.VMEM((rows_dev,), jnp.bfloat16),
                pltpu.SemaphoreType.DMA((3,)),
            ),
        )
    )


def from_behind(value, axis, steps):
    count = lax.axis_size(axis)
    initial, last = (max(0, -steps), min(count, count - steps))
    return lax.ppermute(value, axis, [(source, source + steps) for source in range(initial, last)])


def pair_terms(queries, visiting, allowed):
    similar = jnp.dot(queries, visiting.T, preferred_element_type=jnp.float32)
    return jnp.where(allowed, jnp.exp(sharpness * (similar - 1.0)), jnp.zeros_like(similar))


def finish(weighted, totals):
    normed = (
        weighted * lax.rsqrt(jnp.mean(weighted * weighted, axis=-1, keepdims=True) + epsilon)
    ).astype(jnp.bfloat16)
    return (normed, jnp.log(totals).astype(jnp.bfloat16))


def collected_body(embeddings, cluster_id):
    rows_dev, features = embeddings.shape
    devices = lax.axis_size("blk")
    per_peer = rows_dev // devices
    clusters = devices // 4
    unit_rows = normalize_rows(embeddings)
    labels = jnp.arange(clusters, dtype=jnp.int32)
    counts = jnp.sum((cluster_id[:, None] == labels[None, :]).astype(jnp.int32), axis=0)
    group_ends = jnp.cumsum(counts // per_peer)

    def owner_cluster(device):
        in_range = (device >= 0) & (device < devices)
        return jnp.where(in_range, jnp.sum((device >= group_ends).astype(jnp.int32)), -1)

    position = jnp.arange(rows_dev, dtype=jnp.int32)
    arrange_order = jnp.argsort(cluster_id * rows_dev + position)
    inverse = jnp.argsort(arrange_order)
    arranged = unit_rows[arrange_order].reshape(devices, per_peer, features)
    held_rows = lax.all_to_all(arranged, "blk", split_axis=0, concat_axis=0, tiled=True).reshape(
        rows_dev, features
    )
    self_index = lax.axis_index("blk")
    mine = owner_cluster(self_index)
    weights = pair_terms(held_rows, held_rows, position[:, None] != position[None, :])
    totals = jnp.sum(weights, axis=1)
    weighted = jnp.dot(weights.astype(jnp.bfloat16), held_rows, preferred_element_type=jnp.float32)
    from_lower = held_rows
    from_upper = held_rows
    for distance in range(1, U_MAX):
        from_lower = from_behind(from_lower, "blk", 1)
        from_upper = from_behind(from_upper, "blk", -1)
        for visiting, source in (
            (from_lower, self_index - distance),
            (from_upper, self_index + distance),
        ):
            weights = pair_terms(held_rows, visiting, owner_cluster(source) == mine)
            totals = totals + jnp.sum(weights, axis=1)
            weighted = weighted + jnp.dot(
                weights.astype(jnp.bfloat16), visiting, preferred_element_type=jnp.float32
            )
    normed, scores = finish(weighted, totals)
    returned_rows, returned_scores = (
        lax.all_to_all(
            normed.reshape(devices, per_peer, features),
            "blk",
            split_axis=0,
            concat_axis=0,
            tiled=True,
        ),
        lax.all_to_all(
            scores.reshape(devices, per_peer), "blk", split_axis=0, concat_axis=0, tiled=True
        ),
    )
    neighbour = returned_rows.reshape(rows_dev, features)[inverse]
    dup_score = returned_scores.reshape(rows_dev)[inverse]
    return (neighbour, dup_score)


def solution(mesh):
    placed = (P(("groups", "blk"), None), P(("groups", "blk")))
    devices = mesh.shape["blk"]

    def body(embeddings, cluster_id):
        gathered = embeddings.size * embeddings.dtype.itemsize * devices
        fits = gathered <= GATHER_LIMIT and devices == GRID and embeddings.shape[0] % 16 == 0
        plan = gathered_body if fits else collected_body
        return plan(embeddings, cluster_id)

    return jax.shard_map(
        body,
        mesh=mesh,
        in_specs=placed,
        out_specs=(P(("groups", "blk"), None), P(("groups", "blk"))),
        check_vma=False,
    )
```

```python
import jax
import jax.numpy as jnp
from jax import lax
from jax.experimental import pallas as pl
from jax.experimental.pallas import tpu as pltpu
from jax.sharding import PartitionSpec as P

U_MAX = 8
GATHER_LIMIT = 4 * 1024 * 1024


sharpness = 10.0
epsilon = 1e-06


def normalize_rows(values):
    widened = values.astype(jnp.float32)
    return (
        widened
        * lax.rsqrt(jnp.mean(widened * widened, axis=-1, keepdims=True) + epsilon)
        * widened.shape[-1] ** (-0.5)
    ).astype(jnp.bfloat16)


def as_column(row):
    count = row.shape[1]
    across = lax.broadcasted_iota(jnp.int32, (count, count), 1)
    down = lax.broadcasted_iota(jnp.int32, (count, count), 0)
    return jnp.sum(jnp.where(across == down, row, jnp.zeros_like(row)), axis=1, keepdims=True)


def as_row(column):
    count = column.shape[0]
    across = lax.broadcasted_iota(jnp.int32, (count, count), 1)
    down = lax.broadcasted_iota(jnp.int32, (count, count), 0)
    return jnp.sum(jnp.where(across == down, column, jnp.zeros_like(column)), axis=0, keepdims=True)


LANES = 128


def arrange_kernel(ids_hbm, rows_hbm, out_ref, moves_ref, ids_out_ref, ids_ref, rows_ref, sems):
    ids_copy = pltpu.make_async_copy(ids_hbm, ids_ref, sems.at[0])
    rows_copy = pltpu.make_async_copy(rows_hbm, rows_ref, sems.at[1])
    ids_copy.start()
    rows_copy.start()
    count = rows_ref.shape[0]
    ids_copy.wait()
    ids_row = ids_ref[...].reshape(1, count)
    ids_column = as_column(ids_row)
    across = lax.broadcasted_iota(jnp.int32, (count, count), 1)
    down = lax.broadcasted_iota(jnp.int32, (count, count), 0)
    before = (ids_column < ids_row) | ((ids_column == ids_row) & (down < across))
    rank_row = jnp.sum(before.astype(jnp.int32), axis=0, keepdims=True)
    moves = (down == rank_row).astype(jnp.bfloat16)
    rows_copy.wait()
    unit = normalize_rows(rows_ref[...])
    out_ref[...] = jnp.dot(moves, unit, preferred_element_type=jnp.float32).astype(jnp.bfloat16)
    moves_ref[...] = moves
    ids_out_ref[...] = ids_row


def partial_sums(queries, keys, bounds, own):
    count = bounds.shape[0]
    blocks = queries.shape[0] // count
    similar = lax.dot_general(
        queries, keys, (((1,), (1,)), ((), ())), preferred_element_type=jnp.float32
    )
    bounds = jnp.concatenate([bounds] * blocks, axis=0)
    key = lax.broadcasted_iota(jnp.int32, similar.shape, 1)
    place = lax.rem(key, count)
    allowed = (place >= bounds[:, 0:1]) & (place < bounds[:, 1:2])
    if own:
        query = lax.broadcasted_iota(jnp.int32, similar.shape, 0)
        allowed = allowed & ((key != query) | (key >= count))
    weights = jnp.where(allowed, jnp.exp(sharpness * (similar - 1.0)), 0.0)
    totals = jnp.sum(weights, axis=1, keepdims=True)
    return totals, jnp.dot(weights.astype(jnp.bfloat16), keys, preferred_element_type=jnp.float32)


def first_kernel(moves_ref, ids_ref, own_ref, beside_ref, *refs):
    *key_refs, weighted_ref, totals_ref, bounds_ref = refs
    ids = ids_ref[...]
    label = jnp.sum(jnp.where(moves_ref[...] > 0, ids, 0), axis=1, keepdims=True)
    first = jnp.sum((ids < label).astype(jnp.int32), axis=1, keepdims=True)
    after = jnp.sum((ids <= label).astype(jnp.int32), axis=1, keepdims=True)
    lane = lax.broadcasted_iota(jnp.int32, bounds_ref.shape, 1)
    bounds = jnp.where(lane == 0, first, after)
    bounds_ref[...] = bounds
    queries = jnp.concatenate([own_ref[...], beside_ref[...]], axis=0)
    keys = jnp.concatenate([ref[...] for ref in key_refs], axis=0)
    totals, weighted = partial_sums(queries, keys, bounds, True)
    weighted_ref[...] = weighted
    totals_ref[...] = jnp.broadcast_to(totals, totals_ref.shape)


def beside_kernel(so_far_ref, totals_so_far_ref, bounds_ref, beside_ref, keys_ref, out_ref):
    count = beside_ref.shape[0]
    totals, weighted = partial_sums(beside_ref[...], keys_ref[...], bounds_ref[...], False)
    weighted = (weighted + so_far_ref[count:, :]).astype(jnp.bfloat16)
    columns = weighted.shape[1] // LANES
    for index in range(columns):
        out_ref[index * count : (index + 1) * count, :] = weighted[
            :, index * LANES : (index + 1) * LANES
        ]
    totals = as_row(totals + totals_so_far_ref[count:, 0:1])
    totals = jnp.concatenate([totals, jnp.zeros((1, LANES - count), jnp.float32)], axis=1)
    high = totals.astype(jnp.bfloat16).astype(jnp.float32)
    row = lax.broadcasted_iota(jnp.int32, (EXTRA, LANES), 0)
    out_ref[columns * count :, :] = jnp.where(row == 0, high, totals - high).astype(jnp.bfloat16)


def own_kernel(so_far_ref, totals_so_far_ref, bounds_ref, own_ref, keys_ref, weighted_ref, totals_ref):
    count = own_ref.shape[0]
    totals, weighted = partial_sums(own_ref[...], keys_ref[...], bounds_ref[...], False)
    weighted_ref[...] = weighted + so_far_ref[:count, :]
    totals_ref[...] = as_row(totals + totals_so_far_ref[:count, 0:1])


def finish_kernel(
    moves_ref,
    weighted_ref,
    totals_ref,
    back_ref,
    neighbour_hbm,
    score_hbm,
    neighbour_ref,
    score_ref,
    sems,
):
    count, features = neighbour_ref.shape
    columns = features // LANES
    back = [
        back_ref[index * count : (index + 1) * count, :].astype(jnp.float32)
        for index in range(columns)
    ]
    weighted = weighted_ref[...] + jnp.concatenate(back, axis=1)
    normed = (
        weighted * lax.rsqrt(jnp.mean(weighted * weighted, axis=-1, keepdims=True) + epsilon)
    ).astype(jnp.bfloat16)
    moves = moves_ref[...]
    copies = []
    for half in range(2):
        part = slice(half * features // 2, (half + 1) * features // 2)
        neighbour_ref[:, part] = lax.dot_general(
            moves, normed[:, part], (((0,), (0,)), ((), ())), preferred_element_type=jnp.float32
        ).astype(jnp.bfloat16)
        copies.append(
            pltpu.make_async_copy(
                neighbour_ref.at[:, part], neighbour_hbm.at[:, part], sems.at[half]
            )
        )
        copies[-1].start()
    pair = back_ref[columns * count :, :].astype(jnp.float32)
    totals = totals_ref[...] + (pair[0:1, :count] + pair[1:2, :count])
    scores = jnp.sum(moves.astype(jnp.float32) * as_column(jnp.log(totals)), axis=0, keepdims=True)
    score_ref[...] = scores.astype(jnp.bfloat16).reshape(count)
    copies.append(pltpu.make_async_copy(score_ref, score_hbm, sems.at[2]))
    copies[-1].start()
    for copy in copies:
        copy.wait()


EXTRA = 16
CORE, ACROSS, NEAR, FAR = 1, 2, 4, 8
GRID = 16
TURNS = (
    (FAR, FAR | NEAR, NEAR, ACROSS, CORE),
    (FAR, FAR | NEAR, ACROSS, NEAR, CORE),
)


def gathered_body(embeddings, cluster_id):
    rows_dev, features = embeddings.shape
    vmem = pl.BlockSpec(memory_space=pltpu.VMEM)
    stored = pl.BlockSpec(memory_space=pltpu.HBM)

    def swap(value, bits):
        pairs = [(device, device ^ bits[device & CORE]) for device in range(GRID)]
        return lax.ppermute(value, "blk", pairs)

    def block(kind, *shape):
        return jax.ShapeDtypeStruct(shape, kind)

    def kernel(body, name, out_shape, *inputs, specs=vmem, out_specs=vmem, scratch=()):
        return pl.pallas_call(
            body,
            out_shape=out_shape,
            in_specs=[specs] * len(inputs),
            out_specs=(out_specs,) * len(out_shape),
            scratch_shapes=scratch,
            compiler_params=pltpu.CompilerParams(vmem_limit_bytes=32 * 1024 * 1024),
            name=name,
        )(*inputs)

    rows = block(jnp.bfloat16, rows_dev, features)
    own, moves, ids = kernel(
        arrange_kernel,
        "arrange",
        (rows, block(jnp.bfloat16, rows_dev, rows_dev), block(jnp.int32, 1, rows_dev)),
        pltpu.with_memory_space_constraint(cluster_id, pltpu.HBM),
        pltpu.with_memory_space_constraint(embeddings, pltpu.HBM),
        specs=stored,
        scratch=(
            pltpu.VMEM((rows_dev,), jnp.int32),
            pltpu.VMEM((rows_dev, features), jnp.bfloat16),
            pltpu.SemaphoreType.DMA((2,)),
        ),
    )

    far, farther, third, fourth, mate = lax.optimization_barrier(
        tuple(swap(own, turn) for turn in zip(*TURNS))
    )
    first_core = (lax.axis_index("blk") & CORE) == 0
    near, beside = jnp.where(first_core, third, fourth), jnp.where(first_core, fourth, third)
    visiting = (near, far, farther)
    mates = swap(jnp.concatenate(visiting, axis=0), (CORE,) * 2)
    *so_far, bounds = kernel(
        first_kernel,
        "first",
        (
            block(jnp.float32, 2 * rows_dev, features),
            block(jnp.float32, 2 * rows_dev, LANES),
            block(jnp.int32, rows_dev, LANES),
        ),
        *(moves, ids, own, beside),
        *(own, mate, *visiting),
    )
    (partial,) = kernel(
        beside_kernel,
        "beside",
        (block(jnp.bfloat16, rows_dev * features // LANES + EXTRA, LANES),),
        *(*so_far, bounds, beside, mates),
    )
    back = swap(partial, (ACROSS,) * 2)
    weighted, totals = kernel(
        own_kernel,
        "own",
        (block(jnp.float32, rows_dev, features), block(jnp.float32, 1, rows_dev)),
        *(*so_far, bounds, own, mates),
    )
    return tuple(
        kernel(
            finish_kernel,
            "finish",
            (rows, block(jnp.bfloat16, rows_dev)),
            *(moves, weighted, totals, back),
            out_specs=stored,
            scratch=(
                pltpu.VMEM((rows_dev, features), jnp.bfloat16),
                pltpu.VMEM((rows_dev,), jnp.bfloat16),
                pltpu.SemaphoreType.DMA((3,)),
            ),
        )
    )


def from_behind(value, axis, steps):
    count = lax.axis_size(axis)
    initial, last = (max(0, -steps), min(count, count - steps))
    return lax.ppermute(value, axis, [(source, source + steps) for source in range(initial, last)])


def pair_terms(queries, visiting, allowed):
    similar = jnp.dot(queries, visiting.T, preferred_element_type=jnp.float32)
    return jnp.where(allowed, jnp.exp(sharpness * (similar - 1.0)), jnp.zeros_like(similar))


def finish(weighted, totals):
    normed = (
        weighted * lax.rsqrt(jnp.mean(weighted * weighted, axis=-1, keepdims=True) + epsilon)
    ).astype(jnp.bfloat16)
    return (normed, jnp.log(totals).astype(jnp.bfloat16))


def collected_body(embeddings, cluster_id):
    rows_dev, features = embeddings.shape
    devices = lax.axis_size("blk")
    per_peer = rows_dev // devices
    clusters = devices // 4
    unit_rows = normalize_rows(embeddings)
    labels = jnp.arange(clusters, dtype=jnp.int32)
    counts = jnp.sum((cluster_id[:, None] == labels[None, :]).astype(jnp.int32), axis=0)
    group_ends = jnp.cumsum(counts // per_peer)

    def owner_cluster(device):
        in_range = (device >= 0) & (device < devices)
        return jnp.where(in_range, jnp.sum((device >= group_ends).astype(jnp.int32)), -1)

    position = jnp.arange(rows_dev, dtype=jnp.int32)
    arrange_order = jnp.argsort(cluster_id * rows_dev + position)
    inverse = jnp.argsort(arrange_order)
    arranged = unit_rows[arrange_order].reshape(devices, per_peer, features)
    held_rows = lax.all_to_all(arranged, "blk", split_axis=0, concat_axis=0, tiled=True).reshape(
        rows_dev, features
    )
    self_index = lax.axis_index("blk")
    mine = owner_cluster(self_index)
    weights = pair_terms(held_rows, held_rows, position[:, None] != position[None, :])
    totals = jnp.sum(weights, axis=1)
    weighted = jnp.dot(weights.astype(jnp.bfloat16), held_rows, preferred_element_type=jnp.float32)
    from_lower = held_rows
    from_upper = held_rows
    for distance in range(1, U_MAX):
        from_lower = from_behind(from_lower, "blk", 1)
        from_upper = from_behind(from_upper, "blk", -1)
        for visiting, source in (
            (from_lower, self_index - distance),
            (from_upper, self_index + distance),
        ):
            weights = pair_terms(held_rows, visiting, owner_cluster(source) == mine)
            totals = totals + jnp.sum(weights, axis=1)
            weighted = weighted + jnp.dot(
                weights.astype(jnp.bfloat16), visiting, preferred_element_type=jnp.float32
            )
    normed, scores = finish(weighted, totals)
    returned_rows, returned_scores = (
        lax.all_to_all(
            normed.reshape(devices, per_peer, features),
            "blk",
            split_axis=0,
            concat_axis=0,
            tiled=True,
        ),
        lax.all_to_all(
            scores.reshape(devices, per_peer), "blk", split_axis=0, concat_axis=0, tiled=True
        ),
    )
    neighbour = returned_rows.reshape(rows_dev, features)[inverse]
    dup_score = returned_scores.reshape(rows_dev)[inverse]
    return (neighbour, dup_score)


def solution(mesh):
    placed = (P(("groups", "blk"), None), P(("groups", "blk")))
    devices = mesh.shape["blk"]

    def body(embeddings, cluster_id):
        gathered = embeddings.size * embeddings.dtype.itemsize * devices
        fits = gathered <= GATHER_LIMIT and devices == GRID and embeddings.shape[0] % 16 == 0
        plan = gathered_body if fits else collected_body
        return plan(embeddings, cluster_id)

    return jax.shard_map(
        body,
        mesh=mesh,
        in_specs=placed,
        out_specs=(P(("groups", "blk"), None), P(("groups", "blk"))),
        check_vma=False,
    )
```

```python
import jax
import jax.numpy as jnp
from jax import lax
from jax.experimental import pallas as pl
from jax.experimental.pallas import tpu as pltpu
from jax.sharding import PartitionSpec as P

U_MAX = 8
GATHER_LIMIT = 4 * 1024 * 1024


sharpness = 10.0
epsilon = 1e-06


def normalize_rows(values):
    widened = values.astype(jnp.float32)
    return (
        widened
        * lax.rsqrt(jnp.mean(widened * widened, axis=-1, keepdims=True) + epsilon)
        * widened.shape[-1] ** (-0.5)
    ).astype(jnp.bfloat16)


def as_column(row):
    count = row.shape[1]
    across = lax.broadcasted_iota(jnp.int32, (count, count), 1)
    down = lax.broadcasted_iota(jnp.int32, (count, count), 0)
    return jnp.sum(jnp.where(across == down, row, jnp.zeros_like(row)), axis=1, keepdims=True)


def as_row(column):
    count = column.shape[0]
    across = lax.broadcasted_iota(jnp.int32, (count, count), 1)
    down = lax.broadcasted_iota(jnp.int32, (count, count), 0)
    return jnp.sum(jnp.where(across == down, column, jnp.zeros_like(column)), axis=0, keepdims=True)


LANES = 128


def arrange_kernel(ids_hbm, rows_hbm, out_ref, moves_ref, ids_out_ref, ids_ref, rows_ref, sems):
    ids_copy = pltpu.make_async_copy(ids_hbm, ids_ref, sems.at[0])
    rows_copy = pltpu.make_async_copy(rows_hbm, rows_ref, sems.at[1])
    ids_copy.start()
    rows_copy.start()
    count = rows_ref.shape[0]
    ids_copy.wait()
    ids_row = ids_ref[...].reshape(1, count)
    ids_column = as_column(ids_row)
    across = lax.broadcasted_iota(jnp.int32, (count, count), 1)
    down = lax.broadcasted_iota(jnp.int32, (count, count), 0)
    before = (ids_column < ids_row) | ((ids_column == ids_row) & (down < across))
    rank_row = jnp.sum(before.astype(jnp.int32), axis=0, keepdims=True)
    moves = (down == rank_row).astype(jnp.bfloat16)
    rows_copy.wait()
    unit = normalize_rows(rows_ref[...])
    out_ref[...] = jnp.dot(moves, unit, preferred_element_type=jnp.float32).astype(jnp.bfloat16)
    moves_ref[...] = moves
    ids_out_ref[...] = ids_row


def partial_sums(queries, keys, bounds, own):
    count = bounds.shape[0]
    blocks = queries.shape[0] // count
    similar = lax.dot_general(
        queries, keys, (((1,), (1,)), ((), ())), preferred_element_type=jnp.float32
    )
    bounds = jnp.concatenate([bounds] * blocks, axis=0)
    key = lax.broadcasted_iota(jnp.int32, similar.shape, 1)
    place = lax.rem(key, count)
    allowed = (place >= bounds[:, 0:1]) & (place < bounds[:, 1:2])
    if own:
        query = lax.broadcasted_iota(jnp.int32, similar.shape, 0)
        allowed = allowed & ((key != query) | (key >= count))
    weights = jnp.where(allowed, jnp.exp(sharpness * (similar - 1.0)), 0.0)
    totals = jnp.sum(weights, axis=1, keepdims=True)
    return totals, jnp.dot(weights.astype(jnp.bfloat16), keys, preferred_element_type=jnp.float32)


def first_kernel(moves_ref, ids_ref, own_ref, beside_ref, *refs):
    *key_refs, weighted_ref, totals_ref, bounds_ref = refs
    ids = ids_ref[...]
    label = jnp.sum(jnp.where(moves_ref[...] > 0, ids, 0), axis=1, keepdims=True)
    first = jnp.sum((ids < label).astype(jnp.int32), axis=1, keepdims=True)
    after = jnp.sum((ids <= label).astype(jnp.int32), axis=1, keepdims=True)
    lane = lax.broadcasted_iota(jnp.int32, bounds_ref.shape, 1)
    bounds = jnp.where(lane == 0, first, after)
    bounds_ref[...] = bounds
    queries = jnp.concatenate([own_ref[...], beside_ref[...]], axis=0)
    keys = jnp.concatenate([ref[...] for ref in key_refs], axis=0)
    totals, weighted = partial_sums(queries, keys, bounds, True)
    weighted_ref[...] = weighted
    totals_ref[...] = jnp.broadcast_to(totals, totals_ref.shape)


def beside_kernel(so_far_ref, totals_so_far_ref, bounds_ref, beside_ref, keys_ref, out_ref):
    count = beside_ref.shape[0]
    totals, weighted = partial_sums(beside_ref[...], keys_ref[...], bounds_ref[...], False)
    weighted = (weighted + so_far_ref[count:, :]).astype(jnp.bfloat16)
    columns = weighted.shape[1] // LANES
    for index in range(columns):
        out_ref[index * count : (index + 1) * count, :] = weighted[
            :, index * LANES : (index + 1) * LANES
        ]
    totals = as_row(totals + totals_so_far_ref[count:, 0:1])
    totals = jnp.concatenate([totals, jnp.zeros((1, LANES - count), jnp.float32)], axis=1)
    high = totals.astype(jnp.bfloat16).astype(jnp.float32)
    row = lax.broadcasted_iota(jnp.int32, (EXTRA, LANES), 0)
    out_ref[columns * count :, :] = jnp.where(row == 0, high, totals - high).astype(jnp.bfloat16)


def own_kernel(so_far_ref, totals_so_far_ref, bounds_ref, own_ref, keys_ref, weighted_ref, totals_ref):
    count = own_ref.shape[0]
    totals, weighted = partial_sums(own_ref[...], keys_ref[...], bounds_ref[...], False)
    weighted_ref[...] = weighted + so_far_ref[:count, :]
    totals_ref[...] = as_row(totals + totals_so_far_ref[:count, 0:1])


def finish_kernel(
    moves_ref,
    weighted_ref,
    totals_ref,
    back_ref,
    neighbour_hbm,
    score_hbm,
    neighbour_ref,
    score_ref,
    sems,
):
    count, features = neighbour_ref.shape
    columns = features // LANES
    back = [
        back_ref[index * count : (index + 1) * count, :].astype(jnp.float32)
        for index in range(columns)
    ]
    weighted = weighted_ref[...] + jnp.concatenate(back, axis=1)
    normed = (
        weighted * lax.rsqrt(jnp.mean(weighted * weighted, axis=-1, keepdims=True) + epsilon)
    ).astype(jnp.bfloat16)
    moves = moves_ref[...]
    neighbour_ref[...] = lax.dot_general(
        moves, normed, (((0,), (0,)), ((), ())), preferred_element_type=jnp.float32
    ).astype(jnp.bfloat16)
    copies = [pltpu.make_async_copy(neighbour_ref, neighbour_hbm, sems.at[0])]
    copies[0].start()
    pair = back_ref[columns * count :, :].astype(jnp.float32)
    totals = totals_ref[...] + (pair[0:1, :count] + pair[1:2, :count])
    scores = jnp.sum(moves.astype(jnp.float32) * as_column(jnp.log(totals)), axis=0, keepdims=True)
    score_ref[...] = scores.astype(jnp.bfloat16).reshape(count)
    copies.append(pltpu.make_async_copy(score_ref, score_hbm, sems.at[1]))
    copies[-1].start()
    for copy in copies:
        copy.wait()


EXTRA = 16
CORE, ACROSS, NEAR, FAR = 1, 2, 4, 8
GRID = 16


def gathered_body(embeddings, cluster_id):
    rows_dev, features = embeddings.shape
    vmem = pl.BlockSpec(memory_space=pltpu.VMEM)
    stored = pl.BlockSpec(memory_space=pltpu.HBM)

    def swap(value, bits):
        return lax.ppermute(value, "blk", [(device, device ^ bits) for device in range(GRID)])

    def block(kind, *shape):
        return jax.ShapeDtypeStruct(shape, kind)

    def kernel(body, name, out_shape, *inputs, specs=vmem, out_specs=vmem, scratch=()):
        return pl.pallas_call(
            body,
            out_shape=out_shape,
            in_specs=[specs] * len(inputs),
            out_specs=(out_specs,) * len(out_shape),
            scratch_shapes=scratch,
            compiler_params=pltpu.CompilerParams(vmem_limit_bytes=32 * 1024 * 1024),
            name=name,
        )(*inputs)

    rows = block(jnp.bfloat16, rows_dev, features)
    own, moves, ids = kernel(
        arrange_kernel,
        "arrange",
        (rows, block(jnp.bfloat16, rows_dev, rows_dev), block(jnp.int32, 1, rows_dev)),
        pltpu.with_memory_space_constraint(cluster_id, pltpu.HBM),
        pltpu.with_memory_space_constraint(embeddings, pltpu.HBM),
        specs=stored,
        scratch=(
            pltpu.VMEM((rows_dev,), jnp.int32),
            pltpu.VMEM((rows_dev, features), jnp.bfloat16),
            pltpu.SemaphoreType.DMA((2,)),
        ),
    )

    far, farther, near, beside, mate = lax.optimization_barrier(
        tuple(swap(own, bits) for bits in (FAR, FAR | NEAR, NEAR, ACROSS, CORE))
    )
    mates = swap(jnp.concatenate([near, far, farther], axis=0), CORE)
    *so_far, bounds = kernel(
        first_kernel,
        "first",
        (
            block(jnp.float32, 2 * rows_dev, features),
            block(jnp.float32, 2 * rows_dev, LANES),
            block(jnp.int32, rows_dev, LANES),
        ),
        *(moves, ids, own, beside),
        *(own, mate, near, far, farther),
    )
    (partial,) = kernel(
        beside_kernel,
        "beside",
        (block(jnp.bfloat16, rows_dev * features // LANES + EXTRA, LANES),),
        *(*so_far, bounds, beside, mates),
    )
    back = swap(partial, ACROSS)
    weighted, totals = kernel(
        own_kernel,
        "own",
        (block(jnp.float32, rows_dev, features), block(jnp.float32, 1, rows_dev)),
        *(*so_far, bounds, own, mates),
    )
    return tuple(
        kernel(
            finish_kernel,
            "finish",
            (rows, block(jnp.bfloat16, rows_dev)),
            *(moves, weighted, totals, back),
            out_specs=stored,
            scratch=(
                pltpu.VMEM((rows_dev, features), jnp.bfloat16),
                pltpu.VMEM((rows_dev,), jnp.bfloat16),
                pltpu.SemaphoreType.DMA((2,)),
            ),
        )
    )


def from_behind(value, axis, steps):
    count = lax.axis_size(axis)
    initial, last = (max(0, -steps), min(count, count - steps))
    return lax.ppermute(value, axis, [(source, source + steps) for source in range(initial, last)])


def pair_terms(queries, visiting, allowed):
    similar = jnp.dot(queries, visiting.T, preferred_element_type=jnp.float32)
    return jnp.where(allowed, jnp.exp(sharpness * (similar - 1.0)), jnp.zeros_like(similar))


def finish(weighted, totals):
    normed = (
        weighted * lax.rsqrt(jnp.mean(weighted * weighted, axis=-1, keepdims=True) + epsilon)
    ).astype(jnp.bfloat16)
    return (normed, jnp.log(totals).astype(jnp.bfloat16))


def collected_body(embeddings, cluster_id):
    rows_dev, features = embeddings.shape
    devices = lax.axis_size("blk")
    per_peer = rows_dev // devices
    clusters = devices // 4
    unit_rows = normalize_rows(embeddings)
    labels = jnp.arange(clusters, dtype=jnp.int32)
    counts = jnp.sum((cluster_id[:, None] == labels[None, :]).astype(jnp.int32), axis=0)
    group_ends = jnp.cumsum(counts // per_peer)

    def owner_cluster(device):
        in_range = (device >= 0) & (device < devices)
        return jnp.where(in_range, jnp.sum((device >= group_ends).astype(jnp.int32)), -1)

    position = jnp.arange(rows_dev, dtype=jnp.int32)
    arrange_order = jnp.argsort(cluster_id * rows_dev + position)
    inverse = jnp.argsort(arrange_order)
    arranged = unit_rows[arrange_order].reshape(devices, per_peer, features)
    held_rows = lax.all_to_all(arranged, "blk", split_axis=0, concat_axis=0, tiled=True).reshape(
        rows_dev, features
    )
    self_index = lax.axis_index("blk")
    mine = owner_cluster(self_index)
    weights = pair_terms(held_rows, held_rows, position[:, None] != position[None, :])
    totals = jnp.sum(weights, axis=1)
    weighted = jnp.dot(weights.astype(jnp.bfloat16), held_rows, preferred_element_type=jnp.float32)
    from_lower = held_rows
    from_upper = held_rows
    for distance in range(1, U_MAX):
        from_lower = from_behind(from_lower, "blk", 1)
        from_upper = from_behind(from_upper, "blk", -1)
        for visiting, source in (
            (from_lower, self_index - distance),
            (from_upper, self_index + distance),
        ):
            weights = pair_terms(held_rows, visiting, owner_cluster(source) == mine)
            totals = totals + jnp.sum(weights, axis=1)
            weighted = weighted + jnp.dot(
                weights.astype(jnp.bfloat16), visiting, preferred_element_type=jnp.float32
            )
    normed, scores = finish(weighted, totals)
    returned_rows, returned_scores = (
        lax.all_to_all(
            normed.reshape(devices, per_peer, features),
            "blk",
            split_axis=0,
            concat_axis=0,
            tiled=True,
        ),
        lax.all_to_all(
            scores.reshape(devices, per_peer), "blk", split_axis=0, concat_axis=0, tiled=True
        ),
    )
    neighbour = returned_rows.reshape(rows_dev, features)[inverse]
    dup_score = returned_scores.reshape(rows_dev)[inverse]
    return (neighbour, dup_score)


def solution(mesh):
    placed = (P(("groups", "blk"), None), P(("groups", "blk")))
    devices = mesh.shape["blk"]

    def body(embeddings, cluster_id):
        gathered = embeddings.size * embeddings.dtype.itemsize * devices
        fits = gathered <= GATHER_LIMIT and devices == GRID
        plan = gathered_body if fits else collected_body
        return plan(embeddings, cluster_id)

    return jax.shard_map(
        body,
        mesh=mesh,
        in_specs=placed,
        out_specs=(P(("groups", "blk"), None), P(("groups", "blk"))),
        check_vma=False,
    )
```
